256 devices in a mesh: bead: 4 (over x), px: 8 (over y, core), py: 8 (over z).
Axes of the slice: x: 4, y: 4, z: 8, core: 2. Of those that a mesh axis runs over, the one named last changes fastest.
Arguments:
- block_owner: int32 [4096, 1], P(('px', 'py')), may hold values from 0 to 63; in each aligned block of 64 rows (0 to 63, 64 to 127, ...) at most 2 rows name the same one
- block_tile: int32 [4096], P(('px', 'py')), may hold values from 0 to 511
- atom_cell: int32 [4096, 128], P(('px', 'py')), may hold values from 0 to 511
- atom_frac: float32 [4, 4096, 3, 128], P('bead', ('px', 'py')), may hold values from 0 to 1
- charge: float32 [4096, 128], P(('px', 'py')), may hold values from -4 to 4
- zone: int32 [4096, 128], P(('px', 'py')), may hold values 0 or 1
Outputs:
- force: float32 [4, 4096, 3, 128], P('bead', ('px', 'py'))
The draws below stay inside these ranges and needn't reach their ends.
Inputs may be any that keep to these rules, and one draw needn't show every extreme that they name: `block_owner`: among the 64 blocks held by one device, no owner is named by more than 2 blocks.
All inputs are finite; a program needn't handle non-finite values. No bound on the sum of `zone` on one device may be relied on, other than what follows from the above.
Results may differ from the reference program's by a relative error of at most 0.0003.
Values sent between devices are 32-bit elements; how exact they have to be, the bound alone decides.
A program may use at most 128 MiB of HBM per device.

```python
import math
import jax
import jax.numpy as jnp
import numpy as np
from jax import lax

NG = 256
ROWS = 128
BLK_DEV = 64
NBEAD = 4
ALLBLK = 4096
CAP = 2
CX = 32
CY = 32
TPO = 512
N_PX = 8
N_PY = 8


def set_ends(entries, key, least, high):
    dims = entries.shape
    spot = [jax.random.randint(jax.random.fold_in(key, axis), (), 0, dims[axis]) for axis in range(len(dims))]
    entries = entries.at[tuple(spot)].set(least)
    longest = dims.index(max(dims))
    spot[longest] = (spot[longest] + 1) % dims[longest]
    return entries.at[tuple(spot)].set(high)


def shard_levels(stream_key, shape, cuts, low, high):
    def one(position, parts):
        draws = jax.random.uniform(jax.random.fold_in(jax.random.fold_in(stream_key, 6), position), (parts,), jnp.float32, low / len(cuts), high / len(cuts))
        return jnp.repeat(jnp.exp(draws), shape[position] // parts).reshape((-1,) + (1,) * (len(shape) - position - 1))

    factor_of = one(*cuts[0])
    for cut in cuts[1:]:
        factor_of = factor_of * one(*cut)
    return factor_of


def routed_block(own_key, own, number, rows, number_of, top, limit, slope):
    sequence = jax.random.permutation(own_key, number_of)
    heavy_load, common = load_shares(number_of, rows * top, limit, slope, True), load_shares(number_of, rows * top, limit, slope, False)
    places = jnp.arange(number_of)

    def named(lengths, rotation):
        used = int((lengths > 0).sum())
        fixed = max(1, used // 4)
        passed = fixed + (places - fixed + rotation * (used - fixed)) % max(1, number_of - fixed)
        return jnp.zeros((number_of,), jnp.int32).at[sequence[jnp.where(places < fixed, places, passed)]].set(jnp.asarray(lengths, jnp.int32))

    lengths = jnp.where(number % 4 == 0, named(heavy_load, number // 4), named(common, number - number // 4 - 1))
    mixed = jax.random.permutation(jax.random.fold_in(own, 3), number_of)
    giver, sink = mixed[0:number_of // 2 * 2:2], mixed[1:number_of // 2 * 2:2]
    margin = jnp.minimum(lengths[giver] - 1, limit - lengths[sink]) // 2
    margin = jnp.where((giver == sequence[0]) | (sink == sequence[0]) | (lengths[sink] == 0), 0, jnp.maximum(margin, 0))
    passed = jax.random.randint(jax.random.fold_in(own, 4), (number_of // 2,), 0, 1 << 20) % (margin + 1)
    lengths = lengths.at[giver].add(-passed).at[sink].add(passed)
    members = jnp.searchsorted(jnp.cumsum(lengths), jnp.arange(rows * top), side="right").astype(jnp.int32)
    listing = members.reshape(top, rows).T
    listing = listing[jax.random.permutation(jax.random.fold_in(own, 1), rows)]
    rotation = jax.random.randint(jax.random.fold_in(own, 2), (rows, 1), 0, top)
    return jnp.take_along_axis(listing, (jnp.arange(top)[None, :] + rotation) % top, axis=1)


def load_shares(number_of, total, bound, skew, full):
    loads = [(1 << 20) // math.isqrt(standing ** skew) + 1 for standing in range(1, number_of + 1)]
    largest = bound if full else min(bound, max(-(-total // number_of), total * loads[0] // sum(loads)))
    least = 1 if total - largest >= number_of - 1 else 0
    given, spare = [largest] + [least] * (number_of - 1), total - largest - least * (number_of - 1)
    while spare > 0:
        candidates = [i for i in range(1, number_of) if given[i] < largest] or [i for i in range(1, number_of) if given[i] < bound]
        mass, left = sum([loads[i] for i in candidates]), spare
        for i in candidates:
            addition = min(bound - given[i], max(1, left * loads[i] // mass), spare)
            given[i] = given[i] + addition
            spare = spare - addition
    return np.array(given)


def normal_values(key, extent, scale, most, split=(), held_as=jnp.bfloat16):
    drawn = scale * jax.random.normal(key, extent, jnp.float32)
    if split:
        drawn = drawn * shard_levels(key, extent, split, -0.22, 0.18)
    return jnp.clip(drawn, -most, most).astype(held_as)


def setup_inputs(seed: int = 0) -> dict:
    key_list = jax.random.split(jax.random.key(seed), 7)
    block_owner_keys = jax.random.split(jax.random.fold_in(key_list[0], 1), ALLBLK // BLK_DEV)
    block_owner_turns = jax.random.permutation(jax.random.fold_in(key_list[0], 3), ALLBLK // BLK_DEV)
    block_owner = jax.vmap(lambda own, number: routed_block(jax.random.fold_in(key_list[0], 2), own, number, BLK_DEV, N_PX * N_PY, 1, CAP, 2))(block_owner_keys, block_owner_turns).reshape((ALLBLK, 1))
    block_tile = set_ends(jax.random.randint(key_list[1], (ALLBLK,), 0, TPO), jax.random.fold_in(key_list[1], 1), 0, TPO - 1).astype(jnp.int32)
    atom_cell = set_ends(jax.random.randint(key_list[2], (ALLBLK, ROWS), 0, 512), jax.random.fold_in(key_list[2], 1), 0, 511).astype(jnp.int32)
    atom_frac = jnp.clip(1.0 * jax.random.uniform(key_list[3], (NBEAD, ALLBLK, 3, ROWS), jnp.float32) ** shard_levels(key_list[3], (NBEAD, ALLBLK, 3, ROWS), ((0, 4), (1, 64)), -0.2, 0.2), 0.0, 1.0)
    charge = normal_values(key_list[4], (ALLBLK, ROWS), 1.0, 4.0, ((0, 64),), jnp.float32)
    zone = set_ends((jax.random.randint(key_list[5], (ALLBLK, ROWS), 0, 2) < 1).astype(jnp.int32), jax.random.fold_in(key_list[5], 1), 0, 1)
    return {"block_owner": block_owner, "block_tile": block_tile, "atom_cell": atom_cell, "atom_frac": atom_frac, "charge": charge, "zone": zone}


ewald_beta = 0.75
spring_scale = 0.25


def spline(offset):
    rest = 1.0 - offset
    weights = [rest * rest * rest / 6.0,
               (3.0 * offset * offset * offset - 6.0 * offset * offset + 4.0) / 6.0,
               (-3.0 * offset * offset * offset + 3.0 * offset * offset + 3.0 * offset + 1.0) / 6.0,
               offset * offset * offset / 6.0]
    slopes = [-0.5 * rest * rest,
              1.5 * offset * offset - 2.0 * offset,
              -1.5 * offset * offset + offset + 0.5,
              0.5 * offset * offset]
    return weights, slopes


def influence_part(index_values):
    wave = ((index_values + NG // 2) % NG) - NG // 2
    theta = wave.astype(jnp.float32) * (2.0 * math.pi / NG)
    factor = 6.0 / (4.0 + 2.0 * jnp.cos(theta))
    return theta * theta, factor * factor


def influence(index_x, index_y, index_z):
    square_x, factor_x = influence_part(index_x)
    square_y, factor_y = influence_part(index_y)
    square_z, factor_z = influence_part(index_z)
    wave_sq = square_x + square_y + square_z
    safe_sq = jnp.where(wave_sq > 0, wave_sq, 1.0)
    value = 4.0 * math.pi / safe_sq * jnp.exp(-wave_sq / (4.0 * ewald_beta * ewald_beta)) * factor_x * factor_y * factor_z
    kept = jnp.logical_and(wave_sq > 0, (index_z % NG) != NG // 2)
    return jnp.where(kept, value, 0.0).astype(jnp.float32)


def grid_cells(owners, tile_ids, cell_ids, width_x, width_y, count_y):
    tiles_y = width_y // 8
    tiles_z = NG // 8
    tile_x = tile_ids // (tiles_y * tiles_z)
    tile_y = (tile_ids // tiles_z) % tiles_y
    tile_z = tile_ids % tiles_z
    base_x = ((owners // count_y) * width_x + tile_x * 8)[..., None] + cell_ids // 64
    base_y = ((owners % count_y) * width_y + tile_y * 8)[..., None] + (cell_ids // 8) % 8
    base_z = (tile_z * 8)[..., None] + cell_ids % 8
    return jnp.stack([base_x, base_y, base_z], -2).astype(jnp.int32)


def reference(block_owner, block_tile, atom_cell, atom_frac, charge, zone):
    owners = block_owner[:, 0]
    cells = grid_cells(owners, block_tile, atom_cell, CX, CY, N_PY)
    charged = charge * zone.astype(jnp.float32)
    index_all = jnp.arange(NG, dtype=jnp.int32)
    green = influence(index_all[:, None, None], index_all[None, :, None], index_all[None, None, :])

    def one_bead(bead_frac):
        weights_x, slopes_x = spline(bead_frac[:, 0])
        weights_y, slopes_y = spline(bead_frac[:, 1])
        weights_z, slopes_z = spline(bead_frac[:, 2])
        density = jnp.zeros((NG, NG, NG), jnp.float32)
        for first in range(4):
            for second in range(4):
                for third in range(4):
                    density = density.at[(cells[:, 0] + first) % NG,
                                         (cells[:, 1] + second) % NG,
                                         (cells[:, 2] + third) % NG].add(
                        charged * weights_x[first] * weights_y[second] * weights_z[third])
        potential = jnp.real(jnp.fft.ifftn(jnp.fft.fftn(density) * green)).astype(jnp.float32)
        grad_x = jnp.zeros_like(charged)
        grad_y = jnp.zeros_like(charged)
        grad_z = jnp.zeros_like(charged)
        for first in range(4):
            for second in range(4):
                for third in range(4):
                    values = potential[(cells[:, 0] + first) % NG,
                                       (cells[:, 1] + second) % NG,
                                       (cells[:, 2] + third) % NG]
                    grad_x = grad_x + slopes_x[first] * weights_y[second] * weights_z[third] * values
                    grad_y = grad_y + weights_x[first] * slopes_y[second] * weights_z[third] * values
                    grad_z = grad_z + weights_x[first] * weights_y[second] * slopes_z[third] * values
        return -charged[:, None, :] * jnp.stack([grad_x, grad_y, grad_z], 1)

    mesh_force = lax.map(one_bead, atom_frac)
    located = cells.astype(jnp.float32)[None] + atom_frac
    before = jnp.roll(located, 1, 0)
    after = jnp.roll(located, -1, 0)
    spring = -spring_scale * (2.0 * located - before - after)
    return mesh_force + spring
```

```python
import functools
import math

import jax
import jax.numpy as jnp
import ml_dtypes
import numpy as np
from jax import lax
from jax.experimental import pallas as pl
from jax.experimental.pallas import tpu as pltpu
from jax.sharding import PartitionSpec as P

NG = 256
OWN = 64
f32 = jnp.float32
bf16 = jnp.bfloat16
MESH = pl.DeviceIdType.MESH
VMEM = pltpu.VMEM
SMEM = pltpu.SMEM
ewald_beta = 0.75
spring_scale = 0.25


def halves(table):
    table = table.astype(np.float32)
    high = table.astype(ml_dtypes.bfloat16)
    low = (table - high.astype(np.float32)).astype(ml_dtypes.bfloat16)
    return high, low


def waves(rows, columns):
    angle = (np.outer(rows, columns) % NG) * (2.0 * math.pi / NG)
    return np.cos(angle), np.sin(angle)


@functools.lru_cache(None)
def tables():
    whole = np.arange(NG)
    owner = np.arange(OWN)
    kz = np.stack([2 * owner, 2 * owner + 1])
    cos_z, sin_z = waves(kz.reshape(-1), whole)
    forward_z = np.concatenate([cos_z, -sin_z])
    scale = np.where(kz.reshape(-1) == 0, 1.0, 2.0) / float(NG**3)
    back_z = (forward_z * np.concatenate([scale, scale])[:, None]).T
    main = whole
    rim = np.arange(256)
    rim = 32 * (rim // 32 + 1) + rim % 4
    cos_y, sin_y = waves(np.concatenate([main, rim]), whole)
    forward_y = np.concatenate([cos_y, sin_y], 1)
    back_y = np.concatenate([cos_y.T, sin_y.T], 1)
    step, block, group = np.meshgrid(np.arange(4), np.arange(8), np.arange(8), indexing="ij")
    place = (32 * block + 4 * group + step).reshape(-1)
    cos_x, sin_x = waves(whole, place)
    forward_x = np.concatenate([cos_x, sin_x])
    back_x = np.concatenate([cos_x.T, sin_x.T])
    wave = (whole + NG // 2) % NG - NG // 2
    theta = wave * (2.0 * math.pi / NG)
    factor = (6.0 / (4.0 + 2.0 * np.cos(theta))) ** 2
    factor = factor * np.exp(-theta * theta / (4.0 * ewald_beta * ewald_beta))
    column = np.zeros((256, 128), np.float32)
    column[:, 0], column[:, 1] = theta * theta, factor
    row = np.zeros((8, 256), np.float32)
    row[0], row[1] = theta * theta, factor
    in_z = np.stack([(theta * theta)[kz.T], factor[kz.T]], 1).astype(np.float32)
    return dict(
        forward_z=halves(forward_z),
        back_z=halves(back_z),
        forward_y=halves(forward_y),
        back_y=halves(back_y),
        forward_x=halves(forward_x),
        back_x=halves(back_x),
        column=column,
        row=row,
        in_z=in_z,
    )


def split(value):
    high = value.astype(bf16)
    return high, (value - high.astype(f32)).astype(bf16)


def dots(a_high, a_low, b_high, b_low):
    dot = functools.partial(jnp.dot, preferred_element_type=f32)
    return dot(a_high, b_high) + (dot(a_high, b_low) + dot(a_low, b_high))


def lane_of(rank):
    return lax.broadcasted_iota(jnp.int32, (1,) * (rank - 1) + (128,), rank - 1)


def turn(value, steps):
    steps = steps % 128
    if steps == 0:
        return value
    flat = value.reshape(-1, 128)
    return pltpu.roll(flat, steps, 1).reshape(value.shape)


def blocks_exchanged(parts):
    lane = lane_of(parts[0].ndim)
    low = lane < 64
    even = (lane // 32) % 2 == 0
    first = [
        jnp.where(low, parts[0], turn(parts[2], 64)),
        jnp.where(low, parts[1], turn(parts[3], 64)),
        jnp.where(low, turn(parts[0], 64), parts[2]),
        jnp.where(low, turn(parts[1], 64), parts[3]),
    ]
    return [
        jnp.where(even, first[0], turn(first[1], 32)),
        jnp.where(even, turn(first[0], 96), first[1]),
        jnp.where(even, first[2], turn(first[3], 32)),
        jnp.where(even, turn(first[2], 96), first[3]),
    ]


def bspline(offsets, slopes):
    v = jnp.abs(offsets)
    a = jnp.maximum(2.0 - v, 0.0)
    b = jnp.maximum(1.0 - v, 0.0)
    aa = a * a
    bb = b * b
    weight = aa * a * (1.0 / 6.0) - bb * b * (4.0 / 6.0)
    if not slopes:
        return weight
    half = 0.5 * aa - 2.0 * bb
    return weight, jnp.where(offsets < 0.0, -half, half)


def vmem(count):
    return [pl.BlockSpec(memory_space=VMEM)] * count


def targets(owner_row):
    blocks = owner_row.shape[1]
    up = lax.broadcasted_iota(jnp.int32, (blocks, blocks), 0)
    across = lax.broadcasted_iota(jnp.int32, (blocks, blocks), 1)
    owner_column = jnp.sum(jnp.where(up == across, owner_row, 0).astype(f32), 1, keepdims=True)
    owner_float = owner_row.astype(f32)
    before = jnp.where((owner_column == owner_float) & (up < across), 1.0, 0.0)
    rank = jnp.sum(before, 0, keepdims=True)
    target = 2.0 * owner_float + rank
    slot = lax.broadcasted_iota(jnp.int32, (2 * OWN, blocks), 0).astype(f32)
    return slot == target


def three(value):
    high = value.astype(bf16)
    rest = value - high.astype(f32)
    middle = rest.astype(bf16)
    return high, middle, (rest - middle.astype(f32)).astype(bf16)


def pack_kernel(owner_ref, tile_ref, cell_ref, frac_ref, charge_ref, zone_ref, out_ref):
    chosen = jnp.where(targets(owner_ref[...]), 1.0, 0.0).astype(bf16)
    blocks = cell_ref.shape[0]
    up = lax.broadcasted_iota(jnp.int32, (blocks, blocks), 0)
    across = lax.broadcasted_iota(jnp.int32, (blocks, blocks), 1)
    tile = jnp.sum(jnp.where(up == across, tile_ref[...], 0).astype(f32), 1, keepdims=True)
    tile = tile.astype(jnp.int32)
    cell = cell_ref[...]
    corners = [tile >> 7, (tile >> 5) & 3, tile & 31]
    cells = [cell >> 6, (cell >> 3) & 7, cell & 7]
    fields = [charge_ref[...] * zone_ref[...].astype(f32)]
    for axis in range(3):
        base = (corners[axis] * 8).astype(f32)
        inside = cells[axis].astype(f32) + frac_ref[axis]
        fields.append(base + jnp.minimum(inside, 8.0 - 2.0**-16))
    for place, field in enumerate(fields):
        parts = three(field)
        moved = sum(
            jnp.dot(chosen, part, preferred_element_type=f32) for part in reversed(parts)
        )
        out_ref[pl.ds(place, 2 * OWN, stride=4), :] = moved


def pack(owner_row, tile_row, cell, frac, charge, zone):
    return pl.pallas_call(
        pack_kernel,
        out_shape=jax.ShapeDtypeStruct((8 * OWN, 128), f32),
        in_specs=vmem(6),
        out_specs=pl.BlockSpec(memory_space=VMEM),
        name="pack",
    )(owner_row, tile_row, cell, frac, charge, zone)


def slot_list(slots_ref, list_ref, codes, codes_scalar, sem):
    charge = slots_ref[pl.ds(0, 2 * OWN, stride=4), :]
    along_x = slots_ref[pl.ds(1, 2 * OWN, stride=4), :]
    along_z = slots_ref[pl.ds(3, 2 * OWN, stride=4), :]
    tile_x = (jnp.max(along_x, 1, keepdims=True) * 0.125).astype(jnp.int32)
    tile_z = (jnp.max(along_z, 1, keepdims=True) * 0.125).astype(jnp.int32)
    filled = jnp.max(jnp.abs(charge), 1, keepdims=True) > 0.0
    code = jnp.where(filled, tile_x * 32 + tile_z, -1)
    up = lax.broadcasted_iota(jnp.int32, (128, 128), 0)
    across = lax.broadcasted_iota(jnp.int32, (128, 128), 1)
    row = jnp.sum(jnp.where(up == across, code.astype(f32), 0.0), 0, keepdims=True)
    codes[...] = jnp.broadcast_to(row.astype(jnp.int32), (8, 128))
    copy = pltpu.make_async_copy(codes, codes_scalar, sem)
    copy.start()
    copy.wait()

    def step(slot, carry):
        count, empty = carry
        value = codes_scalar[0, slot]
        held = value >= 0
        list_ref[count] = slot * 128 + jnp.maximum(value, 0)
        return count + held.astype(jnp.int32), jnp.where(held, empty, slot)

    count, empty = lax.fori_loop(0, 2 * OWN, step, (jnp.int32(0), jnp.int32(0)))
    list_ref[count] = empty * 128
    list_ref[255] = (count + 1) // 2


def spread_kernel(slots_ref, ez_high, ez_low, out_ref, list_ref, density, packed_high, packed_low, codes, codes_scalar, sem):
    slot_list(slots_ref, list_ref, codes, codes_scalar, sem)
    density[...] = jnp.zeros_like(density)
    rows16 = lax.broadcasted_iota(jnp.int32, (16, 128), 0).astype(f32) - 1.0
    rows48 = lax.broadcasted_iota(jnp.int32, (48, 128), 0).astype(f32) - 1.0
    nothing = jnp.zeros((16, 128), f32)

    def one(item):
        slot = item >> 7
        tile_x = (item >> 5) & 3
        tile_z = item & 31
        charge = slots_ref[pl.ds(4 * slot, 1), :]
        at_x = slots_ref[pl.ds(4 * slot + 1, 1), :] - (8 * tile_x).astype(f32)
        at_y = slots_ref[pl.ds(4 * slot + 2, 1), :]
        at_z = slots_ref[pl.ds(4 * slot + 3, 1), :] - (8 * tile_z).astype(f32)
        weight_x = bspline(rows16 - at_x, False) * charge
        weight_z = bspline(rows16 - at_z, False)
        weight_y = bspline(rows48 - at_y, False)
        plane = jnp.concatenate([weight_x[i : i + 1] * weight_z for i in range(11)], 0)
        plane = jnp.concatenate(split(plane), 1)
        y_high = weight_y.astype(bf16).astype(f32)
        y_low = weight_y - y_high
        left = jnp.concatenate([y_high, nothing, y_low, nothing], 0)
        right = jnp.concatenate([y_high, nothing, jnp.zeros((64, 128), f32)], 0)
        both = jnp.concatenate([left, right], 1).astype(bf16)
        out = lax.dot_general(plane, both, (((1,), (1,)), ((), ())), preferred_element_type=f32)
        return tile_x, tile_z, out

    def put(tile_x, tile_z, out):
        base = pl.multiple_of(8 * tile_z, 8)
        for i in range(11):
            density[8 * tile_x + i, pl.ds(base, 16), :] += out[16 * i : 16 * i + 16]

    def step(index, carry):
        first = one(list_ref[2 * index])
        second = one(list_ref[2 * index + 1])
        put(*first)
        put(*second)
        return carry

    lax.fori_loop(0, list_ref[255], step, 0)

    lane = lane_of(2)
    low = lane < 64
    even = (lane // 32) % 2 == 0

    def fold(plane, carry):
        density[plane, 0:8, :] += density[plane, 256:264, :]
        return carry

    lax.fori_loop(0, 36, fold, 0)

    def regroup(chunk, carry):
        here = pl.ds(pl.multiple_of(chunk * 32, 32), 32)
        rim = jnp.zeros((32, 128), f32)

        def keep(group, value):
            high, rest = split(value)
            packed_high[group, here, :] = high
            packed_low[group, here, :] = rest

        for group in range(9):
            four = [density[4 * group + i, here, :] for i in range(4)]
            pair_even = jnp.where(low, four[0], four[2]) + turn(jnp.where(low, four[2], four[0]), 64)
            pair_odd = jnp.where(low, four[1], four[3]) + turn(jnp.where(low, four[3], four[1]), 64)
            pair_odd = turn(pair_odd, 32)
            main = jnp.where(even, pair_even, pair_odd)
            side = jnp.where(even, pair_odd, pair_even)
            if group < 8:
                keep(group, main)
                rim = rim + turn(side, 4 * group)
            else:
                last = lane >= 96
                corner = jnp.where((lane >= 96) & (lane < 100), turn(side, 64), 0.0)
                corner = jnp.where((lane >= 100) & (lane < 104), turn(side, 36), corner)
                corner = jnp.where((lane >= 104) & (lane < 108), turn(side, 8), corner)
                keep(8, jnp.where(last, corner, main))
        keep(9, rim)
        return carry

    lax.fori_loop(0, 8, regroup, 0)

    for pair in range(5):
        high = jnp.concatenate([packed_high[2 * pair], packed_high[2 * pair + 1]], 1)
        rest = jnp.concatenate([packed_low[2 * pair], packed_low[2 * pair + 1]], 1)
        result = dots(ez_high[...], ez_low[...], high, rest)
        for part in range(2):
            group = 2 * pair + part
            for c in range(4):
                start = 8 * c + group if group < 8 else 32 + c + 4 * (group - 8)
                out_ref[pl.ds(start, OWN, stride=40), :] = result[
                    64 * c : 64 * c + 64, 128 * part : 128 * part + 128
                ]


def spread(slots):
    table = tables()
    high, low = table["forward_z"]
    return pl.pallas_call(
        spread_kernel,
        out_shape=[
            jax.ShapeDtypeStruct((OWN * 40, 128), f32),
            jax.ShapeDtypeStruct((256,), jnp.int32),
        ],
        in_specs=vmem(3),
        out_specs=[pl.BlockSpec(memory_space=VMEM), pl.BlockSpec(memory_space=SMEM)],
        scratch_shapes=[
            VMEM((36, 264, 128), f32),
            VMEM((10, 256, 128), bf16),
            VMEM((10, 256, 128), bf16),
            VMEM((8, 128), jnp.int32),
            SMEM((8, 128), jnp.int32),
            pltpu.SemaphoreType.DMA,
        ],
        compiler_params=pltpu.CompilerParams(vmem_limit_bytes=48 << 20),
        name="spread",
    )(slots, jnp.asarray(high), jnp.asarray(low))


def shifted(value, steps):
    if steps == 1:
        return jnp.concatenate([value[7:8], value[0:7]], 0)
    return jnp.concatenate([value[1:8], value[0:1]], 0)


def middle_kernel(
    in_z, in_ref, fy_high, fy_low, fx_high, fx_low, bx_high, bx_low, by_high, by_low,
    column_ref, row_ref, out_ref, plane_high, plane_low, back,
):
    lane = lane_of(3)
    sub = lax.broadcasted_iota(jnp.int32, (1, 8, 128), 1)
    lane_group = (lane // 4) % 8

    for q in range(2):
        extra = blocks_exchanged([in_ref[:, 4 * q + j, 32:40, :] for j in range(4)])
        for c in range(4):
            main = blocks_exchanged(
                [in_ref[:, 4 * q + j, 8 * c : 8 * c + 8, :] for j in range(4)]
            )
            for i in range(4):
                value = main[i]
                rim = jnp.where(lane_group == sub, extra[(i + 1) % 4][:, 4 + c : 5 + c, :], 0.0)
                if i < 3:
                    value = value + jnp.where(sub == 0, shifted(extra[i][:, c : c + 1, :], 1), 0.0)
                    corner = shifted(extra[3][:, c : c + 1, :], 1)
                    rim = rim + jnp.where((sub == 0) & (lane_group == i), corner, 0.0)
                for part, array in enumerate((value, rim)):
                    high, rest = split(array.reshape(64, 128))
                    at = (c, slice(64 * i, 64 * i + 64), slice(256 * part + 128 * q, 256 * part + 128 * q + 128))
                    plane_high[at] = high
                    plane_low[at] = rest

    column = column_ref[...]
    row = row_ref[...]

    def one(n, carry):
        real = dots(plane_high[n], plane_low[n], fy_high[...], fy_low[...])
        imag = dots(plane_high[2 + n], plane_low[2 + n], fy_high[...], fy_low[...])
        spec = jnp.concatenate(
            [real[:, :256] + imag[:, 256:], imag[:, :256] - real[:, 256:]], 1
        )
        high, rest = split(spec)
        both = dots(fx_high[...], fx_low[...], high, rest)
        square = column[:, 0:1] + row[0:1, :] + in_z[0, n]
        green = column[:, 1:2] * row[1:2, :] * (in_z[1, n] * (4.0 * math.pi))
        green = jnp.where(square > 0.0, green / jnp.where(square > 0.0, square, 1.0), 0.0)
        spec = jnp.concatenate(
            [
                (both[:256, :256] + both[256:, 256:]) * green,
                (both[:256, 256:] - both[256:, :256]) * green,
            ],
            1,
        )
        high, rest = split(spec)
        both = dots(bx_high[...], bx_low[...], high, rest)
        spec = jnp.concatenate(
            [both[:256, :256] - both[256:, 256:], both[:256, 256:] + both[256:, :256]], 0
        )
        high, rest = split(spec)
        both = dots(high, rest, by_high[...], by_low[...])
        back[n] = both[:256, :512] - both[256:, 512:]
        back[2 + n] = both[256:, :512] + both[:256, 512:]
        return carry

    lax.fori_loop(0, 2, one, 0)

    for q in range(2):
        extra = [jnp.zeros((8, 8, 128), f32) for _ in range(4)]
        for c in range(4):
            main, corner = [], jnp.zeros((8, 1, 128), f32)
            for i in range(4):
                value = back[c, 64 * i : 64 * i + 64, 128 * q : 128 * q + 128].reshape(8, 8, 128)
                rim = back[c, 64 * i : 64 * i + 64, 256 + 128 * q : 384 + 128 * q].reshape(8, 8, 128)
                main.append(value)
                if i < 3:
                    extra[i] = jnp.where(sub == c, shifted(value[:, 0:1, :], -1), extra[i])
                    corner = jnp.where(lane_group == i, shifted(rim[:, 0:1, :], -1), corner)
                side = jnp.sum(jnp.where(lane_group == sub, rim, 0.0), 1, keepdims=True)
                extra[(i + 1) % 4] = jnp.where(sub == 4 + c, side, extra[(i + 1) % 4])
            extra[3] = jnp.where(sub == c, corner, extra[3])
            main = blocks_exchanged(main)
            for j in range(4):
                out_ref[:, 4 * q + j, 8 * c : 8 * c + 8, :] = main[j]
        extra = blocks_exchanged(extra)
        for j in range(4):
            out_ref[:, 4 * q + j, 32:40, :] = extra[j]


def middle(spectrum, in_z):
    table = tables()
    consts = [jnp.asarray(half) for name in ("forward_y", "forward_x", "back_x", "back_y") for half in table[name]]
    return pl.pallas_call(
        middle_kernel,
        out_shape=jax.ShapeDtypeStruct((8, 8, 40, 128), f32),
        in_specs=[pl.BlockSpec(memory_space=SMEM)] + vmem(11),
        out_specs=pl.BlockSpec(memory_space=VMEM),
        scratch_shapes=[
            VMEM((4, 256, 512), bf16),
            VMEM((4, 256, 512), bf16),
            VMEM((4, 256, 512), f32),
        ],
        compiler_params=pltpu.CompilerParams(vmem_limit_bytes=56 << 20),
        name="middle",
    )(in_z, spectrum.reshape(8, 8, 40, 128), *consts, jnp.asarray(table["column"]), jnp.asarray(table["row"]))


def force_kernel(list_ref, slots_ref, in_ref, bz_high, bz_low, out_ref, lines, field):
    out_ref[...] = jnp.zeros_like(out_ref)
    for pair in range(5):
        columns = []
        for group in (2 * pair, 2 * pair + 1):
            starts = [8 * c + group if group < 8 else 32 + c + 4 * (group - 8) for c in range(4)]
            columns.append(
                jnp.concatenate([in_ref[pl.ds(start, OWN, stride=40), :] for start in starts], 0)
            )
        high, rest = split(jnp.concatenate(columns, 1))
        result = dots(bz_high[...], bz_low[...], high, rest)
        lines[2 * pair] = result[:, :128]
        lines[2 * pair + 1] = result[:, 128:]

    lane = lane_of(2)
    low = lane < 64
    even = (lane // 32) % 2 == 0

    def regroup(chunk, carry):
        here = pl.ds(pl.multiple_of(chunk * 32, 32), 32)
        rim = lines[9, here, :]
        for group in range(9):
            main = lines[group, here, :]
            if group < 8:
                side = turn(rim, -4 * group)
            else:
                side = jnp.where(lane < 64, turn(main, -64), jnp.where(lane < 96, turn(main, -36), turn(main, -8)))
            pair_even = jnp.where(even, main, side)
            pair_odd = turn(jnp.where(even, side, main), -32)
            for part, value in enumerate((pair_even, pair_odd)):
                high = value.astype(bf16).astype(f32)
                rest = (value - high).astype(bf16).astype(f32)
                field[4 * group + part, here, :] = jnp.where(low, high, turn(rest, 64))
                field[4 * group + 2 + part, here, :] = jnp.where(low, turn(high, 64), rest)
        return carry

    lax.fori_loop(0, 8, regroup, 0)

    def wrap(plane, carry):
        field[plane, 256:264, :] = field[plane, 0:8, :]
        return carry

    lax.fori_loop(0, 36, wrap, 0)

    rows16 = lax.broadcasted_iota(jnp.int32, (16, 128), 0).astype(f32) - 1.0
    rows48 = lax.broadcasted_iota(jnp.int32, (48, 128), 0).astype(f32) - 1.0
    nothing = jnp.zeros((16, 256), f32)

    def one(item):
        slot = item >> 7
        tile_x = (item >> 5) & 3
        tile_z = item & 31
        charge = slots_ref[pl.ds(4 * slot, 1), :]
        at_x = slots_ref[pl.ds(4 * slot + 1, 1), :] - (8 * tile_x).astype(f32)
        at_y = slots_ref[pl.ds(4 * slot + 2, 1), :]
        at_z = slots_ref[pl.ds(4 * slot + 3, 1), :] - (8 * tile_z).astype(f32)
        weight_x, slope_x = bspline(rows16 - at_x, True)
        weight_z, slope_z = bspline(rows16 - at_z, True)
        along_y = jnp.concatenate(bspline(rows48 - at_y, True), 1)
        y_high = along_y.astype(bf16).astype(f32)
        y_low = along_y - y_high
        both = jnp.concatenate(
            [y_high, nothing, y_high, nothing, y_low, nothing, y_low, nothing], 0
        ).astype(bf16)
        base = pl.multiple_of(8 * tile_z, 8)
        window = jnp.concatenate(
            [field[8 * tile_x + i, pl.ds(base, 16), :] for i in range(11)], 0
        ).astype(bf16)
        out = jnp.dot(jnp.concatenate([window, window], 1), both, preferred_element_type=f32)
        plain = jnp.zeros((16, 128), f32)
        along_x = jnp.zeros((16, 128), f32)
        sloped = jnp.zeros((16, 128), f32)
        for i in range(11):
            value = out[16 * i : 16 * i + 16, :128]
            slope = out[16 * i : 16 * i + 16, 128:]
            plain = plain + weight_x[i : i + 1] * value
            along_x = along_x + slope_x[i : i + 1] * value
            sloped = sloped + weight_x[i : i + 1] * slope
        minus = -charge
        forces = [
            minus * jnp.sum(along_x * weight_z, 0, keepdims=True),
            minus * jnp.sum(sloped * weight_z, 0, keepdims=True),
            minus * jnp.sum(plain * slope_z, 0, keepdims=True),
        ]
        return slot, forces

    def put(slot, forces):
        for axis in range(3):
            out_ref[pl.ds(4 * slot + axis, 1), :] = forces[axis]

    def step(index, carry):
        first = one(list_ref[2 * index])
        second = one(list_ref[2 * index + 1])
        put(*first)
        put(*second)
        return carry

    lax.fori_loop(0, list_ref[255], step, 0)


def forces(listing, slots, potential):
    high, low = tables()["back_z"]
    return pl.pallas_call(
        force_kernel,
        out_shape=jax.ShapeDtypeStruct((8 * OWN, 128), f32),
        in_specs=[pl.BlockSpec(memory_space=SMEM)] + vmem(4),
        out_specs=pl.BlockSpec(memory_space=VMEM),
        scratch_shapes=[VMEM((10, 256, 128), f32), VMEM((36, 264, 128), f32)],
        compiler_params=pltpu.CompilerParams(vmem_limit_bytes=48 << 20),
        name="forces",
    )(listing, slots, potential, jnp.asarray(high), jnp.asarray(low))


def finish_kernel(owner_ref, back_ref, frac_ref, before_ref, after_ref, out_ref):
    chosen = jnp.where(targets(owner_ref[...]), 1.0, 0.0).astype(bf16)
    for axis in range(3):
        moved = sum(
            lax.dot_general(chosen, part, (((0,), (0,)), ((), ())), preferred_element_type=f32)
            for part in reversed(three(back_ref[pl.ds(axis, 2 * OWN, stride=4), :]))
        )
        spring = 2.0 * frac_ref[axis] - before_ref[axis] - after_ref[axis]
        out_ref[axis] = moved - spring_scale * spring


def finish(owner_row, back, frac, before, after):
    return pl.pallas_call(
        finish_kernel,
        out_shape=jax.ShapeDtypeStruct((3, OWN, 128), f32),
        in_specs=vmem(5),
        out_specs=pl.BlockSpec(memory_space=VMEM),
        name="finish",
    )(owner_row, back, frac, before, after)


def place(number, bead):
    return (number // 16, (number // 2) % 8, 2 * bead + number % 2)


def here():
    return lax.axis_index("bead"), lax.axis_index("px"), lax.axis_index("py")


def number_of(at):
    return at[0] * 16 + at[1] * 2 + at[2] % 2


def hop(step):
    return lax.rem(step * 37, OWN)


def block_kernel(src, dst, send_sem, recv_sem, own_sem):
    at = here()
    mine, bead = number_of(at), at[2] // 2
    barrier = pltpu.get_barrier_semaphore()

    def greet(step, carry):
        other = lax.rem(mine + hop(step), OWN)
        pl.semaphore_signal(barrier, inc=1, device_id=place(other, bead), device_id_type=MESH)
        return carry

    lax.fori_loop(1, OWN, greet, 0)
    pl.semaphore_wait(barrier, OWN - 1)
    own = pltpu.make_async_copy(src.at[mine], dst.at[mine], own_sem)
    own.start()

    def send(step, carry):
        other = lax.rem(mine + hop(step), OWN)
        pltpu.make_async_remote_copy(
            src_ref=src.at[other], dst_ref=dst.at[mine], send_sem=send_sem, recv_sem=recv_sem,
            device_id=place(other, bead), device_id_type=MESH,
        ).start()
        return carry

    lax.fori_loop(1, OWN, send, 0)
    own.wait()
    rest = pl.ds(0, OWN - 1)
    pltpu.make_async_copy(src.at[rest], dst.at[rest], send_sem).wait()
    pltpu.make_async_copy(src.at[rest], dst.at[rest], recv_sem).wait()


def route_kernel(outward, src, dst, send_sem, recv_sem, own_sem):
    at = here()
    number, chunk = number_of(at), at[1] * 8 + at[2]
    atoms_bead, grid_bead = at[0], at[2] // 2
    both = atoms_bead == grid_bead
    def grid_device(index):
        return place(index, atoms_bead)

    def atoms_device(index):
        return (grid_bead, index // 8, index % 8)

    if outward:
        to, to_self, mark, origin, from_self = grid_device, number, chunk, atoms_device, chunk
    else:
        to, to_self, mark, origin, from_self = atoms_device, chunk, number, grid_device, number
    barrier = pltpu.get_barrier_semaphore()

    def greet(step, carry):
        other = lax.rem(from_self + hop(step), OWN)
        pl.semaphore_signal(barrier, inc=1, device_id=origin(other), device_id_type=MESH)
        return carry

    def send(step, carry):
        other = lax.rem(to_self + hop(step), OWN)
        pltpu.make_async_remote_copy(
            src_ref=src.at[other], dst_ref=dst.at[mark], send_sem=send_sem, recv_sem=recv_sem,
            device_id=to(other), device_id_type=MESH,
        ).start()
        return carry

    def run(first):
        lax.fori_loop(first, OWN, greet, 0)
        pl.semaphore_wait(barrier, OWN - first)
        if first:
            own = pltpu.make_async_copy(src.at[to_self], dst.at[mark], own_sem)
            own.start()
        lax.fori_loop(first, OWN, send, 0)
        if first:
            own.wait()
        rest = pl.ds(0, OWN - first)
        pltpu.make_async_copy(src.at[rest], dst.at[rest], send_sem).wait()
        pltpu.make_async_copy(src.at[rest], dst.at[rest], recv_sem).wait()

    @pl.when(both)
    def _():
        run(1)

    @pl.when(jnp.logical_not(both))
    def _():
        run(0)


def transfer(kernel, value, rows, identity, name):
    return pl.pallas_call(
        kernel,
        out_shape=jax.ShapeDtypeStruct((OWN, rows, 128), f32),
        in_specs=[pl.BlockSpec(memory_space=pl.ANY)],
        out_specs=pl.BlockSpec(memory_space=pl.ANY),
        scratch_shapes=[pltpu.SemaphoreType.DMA] * 3,
        compiler_params=pltpu.CompilerParams(collective_id=identity, has_side_effects=True),
        name=name,
    )(value.reshape(OWN, rows, 128))


def local(block_owner, block_tile, atom_cell, atom_frac, charge, zone):
    owner_row = block_owner.reshape(1, OWN)
    frac = jnp.transpose(atom_frac[0], (1, 0, 2))
    beads = lax.axis_size("bead")
    before = lax.ppermute(frac, "bead", [(i, (i + 1) % beads) for i in range(beads)])
    after = lax.ppermute(frac, "bead", [((i + 1) % beads, i) for i in range(beads)])
    sent = pack(owner_row, block_tile.reshape(1, OWN), atom_cell, frac, charge, zone)
    slots = transfer(functools.partial(route_kernel, True), sent, 8, 0, "to_grid").reshape(8 * OWN, 128)
    lines, listing = spread(slots)
    spectrum = transfer(block_kernel, lines, 40, 1, "to_waves")
    number = lax.axis_index("bead") * 16 + lax.axis_index("px") * 2 + lax.axis_index("py") % 2
    in_z = lax.dynamic_index_in_dim(jnp.asarray(tables()["in_z"]), number, 0, keepdims=False)
    potential = middle(spectrum, in_z)
    potential = transfer(block_kernel, potential, 40, 1, "to_lines").reshape(OWN * 40, 128)
    force = forces(listing, slots, potential)
    back = transfer(functools.partial(route_kernel, False), force, 8, 2, "to_atoms").reshape(8 * OWN, 128)
    total = finish(owner_row, back, frac, before, after)
    return jnp.transpose(total, (1, 0, 2))[None]


def solution(mesh):
    return jax.shard_map(
        local,
        mesh=mesh,
        in_specs=(
            P(("px", "py"), None),
            P(("px", "py")),
            P(("px", "py"), None),
            P("bead", ("px", "py"), None, None),
            P(("px", "py"), None),
            P(("px", "py"), None),
        ),
        out_specs=P("bead", ("px", "py"), None, None),
        check_vma=False,
    )
```

```python
import functools
import math

import jax
import jax.numpy as jnp
import ml_dtypes
import numpy as np
from jax import lax
from jax.experimental import pallas as pl
from jax.experimental.pallas import tpu as pltpu
from jax.sharding import PartitionSpec as P

NG = 256
OWN = 64
f32 = jnp.float32
bf16 = jnp.bfloat16
MESH = pl.DeviceIdType.MESH
VMEM = pltpu.VMEM
SMEM = pltpu.SMEM
ewald_beta = 0.75
spring_scale = 0.25


def halves(table):
    table = table.astype(np.float32)
    high = table.astype(ml_dtypes.bfloat16)
    low = (table - high.astype(np.float32)).astype(ml_dtypes.bfloat16)
    return high, low


def waves(rows, columns):
    angle = (np.outer(rows, columns) % NG) * (2.0 * math.pi / NG)
    return np.cos(angle), np.sin(angle)


@functools.lru_cache(None)
def tables():
    whole = np.arange(NG)
    owner = np.arange(OWN)
    kz = np.stack([2 * owner, 2 * owner + 1])
    cos_z, sin_z = waves(kz.reshape(-1), whole)
    forward_z = np.concatenate([cos_z[:OWN], -sin_z[:OWN], cos_z[OWN:], -sin_z[OWN:]])
    scale = np.where(kz == 0, 1.0, 2.0) / float(NG**3)
    scale = np.repeat(scale, 2, 0).reshape(-1)
    back_z = (forward_z * scale[:, None]).T
    main = whole
    rim = np.arange(256)
    rim = 32 * (rim // 32 + 1) + rim % 4
    cos_y, sin_y = waves(np.concatenate([main, rim]), whole)
    forward_y = np.concatenate([cos_y, sin_y], 1)
    back_y = np.concatenate([cos_y.T, sin_y.T], 1)
    step, block, group = np.meshgrid(np.arange(4), np.arange(8), np.arange(8), indexing="ij")
    place = (32 * block + 4 * group + step).reshape(-1)
    cos_x, sin_x = waves(whole, place)
    forward_x = np.concatenate([cos_x, sin_x])
    back_x = np.concatenate([cos_x.T, sin_x.T])
    wave = (whole + NG // 2) % NG - NG // 2
    theta = wave * (2.0 * math.pi / NG)
    factor = (6.0 / (4.0 + 2.0 * np.cos(theta))) ** 2
    factor = factor * np.exp(-theta * theta / (4.0 * ewald_beta * ewald_beta))
    column = np.zeros((256, 128), np.float32)
    column[:, 0], column[:, 1] = theta * theta, factor
    row = np.zeros((8, 256), np.float32)
    row[0], row[1] = theta * theta, factor
    in_z = np.stack([(theta * theta)[kz.T], factor[kz.T]], 1).astype(np.float32).reshape(-1)
    return dict(
        forward_z=halves(forward_z),
        back_z=halves(back_z),
        forward_y=halves(forward_y),
        back_y=halves(back_y),
        forward_x=halves(forward_x),
        back_x=halves(back_x),
        column=column,
        row=row,
        in_z=in_z,
    )


def split(value):
    high = value.astype(bf16)
    return high, (value - high.astype(f32)).astype(bf16)


def dots(a_high, a_low, b_high, b_low):
    dot = functools.partial(jnp.dot, preferred_element_type=f32)
    return dot(a_high, b_high) + (dot(a_high, b_low) + dot(a_low, b_high))


def lane_of(rank):
    return lax.broadcasted_iota(jnp.int32, (1,) * (rank - 1) + (128,), rank - 1)


def turn(value, steps):
    steps = steps % 128
    if steps == 0:
        return value
    flat = value.reshape(-1, 128)
    return pltpu.roll(flat, steps, 1).reshape(value.shape)


def blocks_exchanged(parts):
    lane = lane_of(parts[0].ndim)
    low = lane < 64
    even = (lane // 32) % 2 == 0
    first = [
        jnp.where(low, parts[0], turn(parts[2], 64)),
        jnp.where(low, parts[1], turn(parts[3], 64)),
        jnp.where(low, turn(parts[0], 64), parts[2]),
        jnp.where(low, turn(parts[1], 64), parts[3]),
    ]
    return [
        jnp.where(even, first[0], turn(first[1], 32)),
        jnp.where(even, turn(first[0], 96), first[1]),
        jnp.where(even, first[2], turn(first[3], 32)),
        jnp.where(even, turn(first[2], 96), first[3]),
    ]


def bspline(offsets, slopes):
    v = jnp.abs(offsets)
    a = jnp.maximum(2.0 - v, 0.0)
    b = jnp.maximum(1.0 - v, 0.0)
    aa = a * a
    bb = b * b
    weight = aa * a * (1.0 / 6.0) - bb * b * (4.0 / 6.0)
    if not slopes:
        return weight
    half = 0.5 * aa - 2.0 * bb
    return weight, jnp.where(offsets < 0.0, -half, half)


def vmem(count):
    return [pl.BlockSpec(memory_space=VMEM)] * count


def targets(owner_row, apart):
    blocks = owner_row.shape[1]
    up = lax.broadcasted_iota(jnp.int32, (blocks, blocks), 0)
    across = lax.broadcasted_iota(jnp.int32, (blocks, blocks), 1)
    owner_column = jnp.sum(jnp.where(up == across, owner_row, 0).astype(f32), 1, keepdims=True)
    owner_float = owner_row.astype(f32)
    before = jnp.where((owner_column == owner_float) & (up < across), 1.0, 0.0)
    rank = jnp.sum(before, 0, keepdims=True)
    target = owner_float + OWN * rank if apart else 2.0 * owner_float + rank
    slot = lax.broadcasted_iota(jnp.int32, (2 * OWN, blocks), 0).astype(f32)
    return slot == target


def three(value):
    high = value.astype(bf16)
    rest = value - high.astype(f32)
    middle = rest.astype(bf16)
    return high, middle, (rest - middle.astype(f32)).astype(bf16)


def remote(src, dst, send_sem, recv_sem, device):
    return pltpu.make_async_remote_copy(
        src_ref=src, dst_ref=dst, send_sem=send_sem, recv_sem=recv_sem,
        device_id=device, device_id_type=MESH,
    )


def settle(ref, sem):
    pltpu.make_async_copy(ref, ref, sem).wait()


def atoms_kernel(
    owner_ref, tile_ref, cell_ref, frac_ref, charge_ref, zone_ref, slots_ref, before_ref, after_ref,
    payload, stage, stage_send, stage_recv, send_sem, recv_sem, own_sem, bead_send, bead_recv,
):
    bead, px, py = here()
    chunk = px * 8 + py
    barrier = pltpu.get_barrier_semaphore()

    def greet(step, carry):
        other = lax.rem(chunk + step, OWN)
        pl.semaphore_signal(barrier, inc=1, device_id=(bead, other // 8, other % 8), device_id_type=MESH)
        return carry

    lax.fori_loop(1, OWN, greet, 0)
    for step in range(1, 4):
        pl.semaphore_signal(barrier, inc=1, device_id=(lax.rem(bead + step, 4), px, py), device_id_type=MESH)

    chosen = jnp.where(targets(owner_ref[...], False), 1.0, 0.0).astype(bf16)
    blocks = cell_ref.shape[0]
    up = lax.broadcasted_iota(jnp.int32, (blocks, blocks), 0)
    across = lax.broadcasted_iota(jnp.int32, (blocks, blocks), 1)
    tile = jnp.sum(jnp.where(up == across, tile_ref[...], 0).astype(f32), 1, keepdims=True)
    tile = tile.astype(jnp.int32)
    cell = cell_ref[...]
    corners = [tile >> 7, (tile >> 5) & 3, tile & 31]
    cells = [cell >> 6, (cell >> 3) & 7, cell & 7]
    fields = [charge_ref[...] * zone_ref[...].astype(f32)]
    for axis in range(3):
        base = (corners[axis] * 8).astype(f32)
        inside = cells[axis].astype(f32) + frac_ref[axis]
        fields.append(base + jnp.minimum(inside, 8.0 - 2.0**-16))
    for place_in, field in enumerate(fields):
        parts = three(field)
        moved = sum(
            jnp.dot(chosen, part, preferred_element_type=f32) for part in reversed(parts)
        )
        payload[pl.ds(place_in, 2 * OWN, stride=4), :] = moved

    pl.semaphore_wait(barrier, OWN - 1 + 3)
    staged = [
        remote(
            payload.at[pl.ds(pl.multiple_of(lax.rem(bead + step, 4) * 128, 128), 128)], stage.at[bead],
            stage_send.at[step - 1], stage_recv.at[step - 1], (lax.rem(bead + step, 4), px, py),
        )
        for step in (1, 3, 2)
    ]
    for copy in staged:
        copy.start()
    springs = [
        remote(frac_ref, target, bead_send.at[i], bead_recv.at[i], (lax.rem(bead + step, 4), px, py))
        for i, (target, step) in enumerate(((before_ref, 1), (after_ref, 3)))
    ]

    mark = pl.ds(pl.multiple_of(chunk * 8, 8), 8)

    def deliver(source, from_bead):
        def send(step, carry):
            j = lax.rem(step + 2 * px + 1, 16)
            device = (bead, j // 2, 2 * from_bead + j % 2)
            mine = jnp.logical_and(j == 2 * px + py % 2, py // 2 == from_bead)
            piece = source(j)

            @pl.when(jnp.logical_not(mine))
            def _():
                remote(piece, slots_ref.at[mark], send_sem, recv_sem, device).start()

            @pl.when(mine)
            def _():
                pltpu.make_async_copy(piece, slots_ref.at[mark], own_sem).start()

            return carry

        lax.fori_loop(0, 16, send, 0)

    deliver(lambda j: payload.at[pl.ds(pl.multiple_of(bead * 128 + j * 8, 8), 8)], bead)
    for copy in springs:
        copy.start()
    for step, copy in zip((1, 3, 2), staged):
        copy.wait_recv()
        other = lax.rem(bead + 4 - step, 4)
        deliver(lambda j: stage.at[other, pl.ds(pl.multiple_of(j * 8, 8), 8)], other)
    settle(slots_ref.at[mark], own_sem)
    rest = pl.ds(0, 8 * OWN - 8)
    settle(slots_ref.at[rest], recv_sem)
    settle(slots_ref.at[rest], send_sem)
    for copy in staged:
        copy.wait_send()
    for copy in springs:
        copy.wait()


def atoms_to_slots(owner_row, tile_row, cell, frac, charge, zone):
    shape = jax.ShapeDtypeStruct((3, OWN, 128), f32)
    dma = pltpu.SemaphoreType.DMA
    return pl.pallas_call(
        atoms_kernel,
        out_shape=[jax.ShapeDtypeStruct((8 * OWN, 128), f32), shape, shape],
        in_specs=vmem(6),
        out_specs=vmem(3),
        scratch_shapes=[
            VMEM((8 * OWN, 128), f32), VMEM((4, 128, 128), f32),
            dma((3,)), dma((3,)), dma, dma, dma, dma((2,)), dma((2,)),
        ],
        compiler_params=pltpu.CompilerParams(collective_id=0, has_side_effects=True),
        name="atoms_to_slots",
    )(owner_row, tile_row, cell, frac, charge, zone)


def slot_list(slots_ref, list_ref, codes, codes_scalar, sem):
    charge = slots_ref[pl.ds(0, 2 * OWN, stride=4), :]
    along_x = slots_ref[pl.ds(1, 2 * OWN, stride=4), :]
    along_z = slots_ref[pl.ds(3, 2 * OWN, stride=4), :]
    tile_x = (jnp.max(along_x, 1, keepdims=True) * 0.125).astype(jnp.int32)
    tile_z = (jnp.max(along_z, 1, keepdims=True) * 0.125).astype(jnp.int32)
    filled = jnp.max(jnp.abs(charge), 1, keepdims=True) > 0.0
    up = lax.broadcasted_iota(jnp.int32, (128, 128), 0)
    across = lax.broadcasted_iota(jnp.int32, (128, 128), 1)
    sub = lax.broadcasted_iota(jnp.int32, (8, 128), 0)
    value = jnp.zeros((8, 128), f32)
    columns = (256 * tile_x + tile_z, 8 * tile_x, 8 * tile_z, filled.astype(jnp.int32))
    for place_in, column in enumerate(columns):
        row = jnp.sum(jnp.where(up == across, column.astype(f32), 0.0), 0, keepdims=True)
        value = jnp.where(sub == place_in, row, value)
    codes[...] = value.astype(jnp.int32)
    copy = pltpu.make_async_copy(codes, codes_scalar, sem)
    copy.start()
    copy.wait()

    def step(slot, carry):
        count, empty = carry
        held = codes_scalar[3, slot] > 0
        list_ref[count] = slot
        return count + held.astype(jnp.int32), jnp.where(held, empty, slot)

    count, empty = lax.fori_loop(0, 2 * OWN, step, (jnp.int32(0), jnp.int32(0)))
    for k in range(3):
        list_ref[count + k] = empty
    list_ref[255] = (count + 3) // 4


def spread_kernel(slots_ref, out_ref, codes_scalar, list_ref, density, codes, sem):
    slot_list(slots_ref, list_ref, codes, codes_scalar, sem)
    density[...] = jnp.zeros_like(density)
    rows16 = lax.broadcasted_iota(jnp.int32, (16, 128), 0).astype(f32) - 1.0
    rows40 = lax.broadcasted_iota(jnp.int32, (40, 128), 0).astype(f32) - 1.0
    nothing = jnp.zeros((24, 128), f32)

    def one(slot):
        plane_x, row_z = codes_scalar[1, slot], codes_scalar[2, slot]
        charge = slots_ref[pl.ds(4 * slot, 1), :]
        at_x = slots_ref[pl.ds(4 * slot + 1, 1), :] - plane_x.astype(f32)
        at_y = slots_ref[pl.ds(4 * slot + 2, 1), :]
        at_z = slots_ref[pl.ds(4 * slot + 3, 1), :] - row_z.astype(f32)
        weight_x = bspline(rows16 - at_x, False) * charge
        weight_z = bspline(rows16 - at_z, False)
        weight_y = bspline(rows40 - at_y, False)
        plane = jnp.concatenate([weight_x[i : i + 1] * weight_z for i in range(11)], 0)
        plane = jnp.concatenate(split(plane), 1)
        y_high = weight_y.astype(bf16).astype(f32)
        y_low = weight_y - y_high
        left = jnp.concatenate([y_high, nothing, y_low, nothing], 0)
        right = jnp.concatenate([y_high, nothing, jnp.zeros((64, 128), f32)], 0)
        both = jnp.concatenate([left, right], 1).astype(bf16)
        out = lax.dot_general(plane, both, (((1,), (1,)), ((), ())), preferred_element_type=f32)
        return plane_x, row_z, out

    def put(plane_x, row_z, out):
        base = pl.multiple_of(row_z, 8)
        for i in range(11):
            density[plane_x + i, pl.ds(base, 16), :] += out[16 * i : 16 * i + 16]

    def step(index, carry):
        for found in [one(list_ref[4 * index + k]) for k in range(4)]:
            put(*found)
        return carry

    lax.fori_loop(0, list_ref[255], step, 0)

    lane = lane_of(2)
    low = lane < 64
    even = (lane // 32) % 2 == 0

    def fold(plane, carry):
        density[plane, 0:8, :] += density[plane, 256:264, :]
        return carry

    lax.fori_loop(0, 36, fold, 0)

    def regroup(chunk, carry):
        here = pl.ds(pl.multiple_of(chunk * 32, 32), 32)
        rim = jnp.zeros((32, 128), f32)

        def keep(group, value):
            out_ref[group, here, :] = value

        for group in range(9):
            four = [density[4 * group + i, here, :] for i in range(4)]
            pair_even = jnp.where(low, four[0], four[2]) + turn(jnp.where(low, four[2], four[0]), 64)
            pair_odd = jnp.where(low, four[1], four[3]) + turn(jnp.where(low, four[3], four[1]), 64)
            pair_odd = turn(pair_odd, 32)
            main = jnp.where(even, pair_even, pair_odd)
            side = jnp.where(even, pair_odd, pair_even)
            if group < 8:
                keep(group, main)
                rim = rim + turn(side, 4 * group)
            else:
                last = lane >= 96
                corner = jnp.where((lane >= 96) & (lane < 100), turn(side, 64), 0.0)
                corner = jnp.where((lane >= 100) & (lane < 104), turn(side, 36), corner)
                corner = jnp.where((lane >= 104) & (lane < 108), turn(side, 8), corner)
                keep(8, jnp.where(last, corner, main))
        keep(9, rim)
        return carry

    lax.fori_loop(0, 8, regroup, 0)


def spread(slots):
    return pl.pallas_call(
        spread_kernel,
        out_shape=[
            jax.ShapeDtypeStruct((10, 256, 128), f32),
            jax.ShapeDtypeStruct((8, 128), jnp.int32),
        ],
        in_specs=vmem(1),
        out_specs=[pl.BlockSpec(memory_space=VMEM), pl.BlockSpec(memory_space=SMEM)],
        scratch_shapes=[
            SMEM((256,), jnp.int32),
            VMEM((36, 264, 128), f32),
            VMEM((8, 128), jnp.int32),
            pltpu.SemaphoreType.DMA,
        ],
        compiler_params=pltpu.CompilerParams(vmem_limit_bytes=24 << 20),
        name="spread",
    )(slots)


TABLES = ("forward_z", "forward_y", "forward_x", "back_x", "back_y", "back_z")
ROWS_OF = (0, 8, 24, 32)


def here():
    return lax.axis_index("bead"), lax.axis_index("px"), lax.axis_index("py")


def place(number, bead):
    return (number // 16, (number // 2) % 8, 2 * bead + number % 2)


def hop(step):
    return lax.rem(step * 37, OWN)


def shifted(value, steps):
    if steps == 1:
        return jnp.concatenate([value[7:8], value[0:7]], 0)
    return jnp.concatenate([value[1:8], value[0:1]], 0)


def wave_kernel(
    codes, in_z, packed, slots_ref, owner_ref, frac_ref, before_ref, after_ref, column_ref, row_ref,
    *rest,
):
    table_refs, rest = rest[:12], rest[12:]
    out_ref, rest = rest[0], rest[1:]
    table_vmem, rest = rest[:12], rest[12:]
    (
        lines, waves_in, waves_out, lines_in, plane_high, plane_low, rims, rims_out,
        lines_z, field, force, force_in, table_sem, out_send, out_recv, back_send, back_recv,
        own_sem, force_send, force_recv,
    ) = rest
    (fz, fy, fx, bx, by, bz) = [(table_vmem[2 * i], table_vmem[2 * i + 1]) for i in range(6)]
    bead, px, py = here()
    mine, grid_bead, chunk = bead * 16 + px * 2 + py % 2, py // 2, px * 8 + py
    same = bead == grid_bead
    barrier = pltpu.get_barrier_semaphore()

    def greet(step, carry):
        other = lax.rem(mine + hop(step), OWN)
        pl.semaphore_signal(barrier, inc=1, device_id=place(other, grid_bead), device_id_type=MESH)
        return carry

    def greet_atoms(step, carry):
        other = lax.rem(mine + hop(step), OWN)
        pl.semaphore_signal(barrier, inc=1, device_id=place(other, bead), device_id_type=MESH)
        return carry

    lax.fori_loop(1, OWN, greet, 0)

    @pl.when(same)
    def _():
        lax.fori_loop(1, OWN, greet_atoms, 0)

    @pl.when(jnp.logical_not(same))
    def _():
        lax.fori_loop(0, OWN, greet_atoms, 0)

    table_copies = [
        pltpu.make_async_copy(table_refs[i], table_vmem[i], table_sem.at[i]) for i in range(12)
    ]
    for copy in table_copies:
        copy.start()
    table_copies[0].wait()
    table_copies[1].wait()

    for pair in range(5):
        high, low = split(jnp.concatenate([packed[2 * pair], packed[2 * pair + 1]], 1))
        result = dots(fz[0][...], fz[1][...], high, low)
        for part in range(2):
            group = 2 * pair + part
            for c in range(4):
                start = ROWS_OF[c] + group if group < 8 else 16 + c + 4 * (group - 8)
                lines[:, start, :] = result[64 * c : 64 * c + 64, 128 * part : 128 * part + 128]

    pl.semaphore_wait(barrier, 2 * OWN - 1 - same.astype(jnp.int32))

    def own(src, dst, rows, sem):
        return pltpu.make_async_copy(src.at[mine, rows], dst.at[mine, rows], sem)

    def send_all(src, dst, rows, send_sem, recv_sem):
        def send(step, carry):
            other = lax.rem(mine + hop(step), OWN)
            remote(
                src.at[other, rows], dst.at[mine, rows], send_sem, recv_sem, place(other, grid_bead)
            ).start()
            return carry

        lax.fori_loop(1, OWN, send, 0)

    rest = pl.ds(0, OWN - 1)
    out_rows = (pl.ds(0, 24), pl.ds(24, 16))
    back_rows = (pl.ds(0, 16), pl.ds(16, 24))
    for n in range(2):
        own(lines, waves_in, out_rows[n], own_sem.at[n]).start()
        send_all(lines, waves_in, out_rows[n], out_send.at[n], out_recv.at[n])

    for copy in table_copies[2:]:
        copy.wait()

    lane = lane_of(3)
    sub = lax.broadcasted_iota(jnp.int32, (1, 8, 128), 1)
    lane_group = (lane // 4) % 8
    column = column_ref[...]
    row = row_ref[...]

    for n in range(2):
        own(lines, waves_in, out_rows[n], own_sem.at[n]).wait()
        settle(waves_in.at[rest, out_rows[n]], out_recv.at[n])
        for q in range(2):
            if n == 0:
                extra = blocks_exchanged(
                    [waves_in[pl.ds(4 * q + j, 8, stride=8), 16:24, :] for j in range(4)]
                )
                for i in range(4):
                    rims[q, i] = extra[i]
            else:
                extra = [rims[q, i] for i in range(4)]
            for half in range(2):
                c = 2 * n + half
                main = blocks_exchanged(
                    [
                        waves_in[pl.ds(4 * q + j, 8, stride=8), ROWS_OF[c] : ROWS_OF[c] + 8, :]
                        for j in range(4)
                    ]
                )
                for i in range(4):
                    value = main[i]
                    rim = jnp.where(lane_group == sub, extra[(i + 1) % 4][:, 4 + c : 5 + c, :], 0.0)
                    if i < 3:
                        value = value + jnp.where(sub == 0, shifted(extra[i][:, c : c + 1, :], 1), 0.0)
                        corner = shifted(extra[3][:, c : c + 1, :], 1)
                        rim = rim + jnp.where((sub == 0) & (lane_group == i), corner, 0.0)
                    for part, array in enumerate((value, rim)):
                        high, low = split(array.reshape(64, 128))
                        start = 256 * part + 128 * q
                        plane_high[half, 64 * i : 64 * i + 64, start : start + 128] = high
                        plane_low[half, 64 * i : 64 * i + 64, start : start + 128] = low

        real = dots(plane_high[0], plane_low[0], fy[0][...], fy[1][...])
        imag = dots(plane_high[1], plane_low[1], fy[0][...], fy[1][...])
        spec = jnp.concatenate(
            [real[:, :256] + imag[:, 256:], imag[:, :256] - real[:, 256:]], 1
        )
        both = dots(fx[0][...], fx[1][...], *split(spec))
        square = column[:, 0:1] + row[0:1, :] + in_z[4 * mine + n]
        green = column[:, 1:2] * row[1:2, :] * (in_z[4 * mine + 2 + n] * (4.0 * math.pi))
        green = jnp.where(square > 0.0, green / jnp.where(square > 0.0, square, 1.0), 0.0)
        spec = jnp.concatenate(
            [
                (both[:256, :256] + both[256:, 256:]) * green,
                (both[:256, 256:] - both[256:, :256]) * green,
            ],
            1,
        )
        both = dots(bx[0][...], bx[1][...], *split(spec))
        spec = jnp.concatenate(
            [both[:256, :256] - both[256:, 256:], both[:256, 256:] + both[256:, :256]], 0
        )
        both = dots(*split(spec), by[0][...], by[1][...])
        back = [both[:256, :512] - both[256:, 512:], both[256:, :512] + both[:256, 512:]]

        for q in range(2):
            if n == 0:
                extra = [jnp.zeros((8, 8, 128), f32) for _ in range(4)]
            else:
                extra = [rims_out[q, i] for i in range(4)]
            for half in range(2):
                c = 2 * n + half
                main, corner = [], jnp.zeros((8, 1, 128), f32)
                for i in range(4):
                    lines_of = slice(64 * i, 64 * i + 64)
                    value = back[half][lines_of, 128 * q : 128 * q + 128].reshape(8, 8, 128)
                    rim = back[half][lines_of, 256 + 128 * q : 384 + 128 * q].reshape(8, 8, 128)
                    main.append(value)
                    if i < 3:
                        extra[i] = jnp.where(sub == c, shifted(value[:, 0:1, :], -1), extra[i])
                        corner = jnp.where(lane_group == i, shifted(rim[:, 0:1, :], -1), corner)
                    side = jnp.sum(jnp.where(lane_group == sub, rim, 0.0), 1, keepdims=True)
                    extra[(i + 1) % 4] = jnp.where(sub == 4 + c, side, extra[(i + 1) % 4])
                extra[3] = jnp.where(sub == c, corner, extra[3])
                main = blocks_exchanged(main)
                for j in range(4):
                    waves_out[pl.ds(4 * q + j, 8, stride=8), ROWS_OF[c] : ROWS_OF[c] + 8, :] = main[j]
            if n == 0:
                for i in range(4):
                    rims_out[q, i] = extra[i]
            else:
                extra = blocks_exchanged(extra)
                for j in range(4):
                    waves_out[pl.ds(4 * q + j, 8, stride=8), 16:24, :] = extra[j]
        own(waves_out, lines_in, back_rows[n], own_sem.at[2 + n]).start()
        send_all(waves_out, lines_in, back_rows[n], back_send.at[n], back_recv.at[n])

    for n in range(2):
        own(waves_out, lines_in, back_rows[n], own_sem.at[2 + n]).wait()
        settle(lines_in.at[rest, back_rows[n]], back_recv.at[n])

    for pair in range(5):
        columns = []
        for group in (2 * pair, 2 * pair + 1):
            starts = [
                ROWS_OF[c] + group if group < 8 else 16 + c + 4 * (group - 8) for c in range(4)
            ]
            columns.append(jnp.concatenate([lines_in[:, start, :] for start in starts], 0))
        result = dots(bz[0][...], bz[1][...], *split(jnp.concatenate(columns, 1)))
        for part in range(2):
            lines_z[2 * pair + part, 0:256, :] = result[:, 128 * part : 128 * part + 128]
            lines_z[2 * pair + part, 256:264, :] = result[0:8, 128 * part : 128 * part + 128]

    lane = lane_of(2)
    low_half = lane < 64
    even = (lane // 32) % 2 == 0

    def regroup(part, carry):
        at = pl.ds(pl.multiple_of(part * 32, 32), 40)
        rim = lines_z[9, at, :]
        for group in range(9):
            main = lines_z[group, at, :]
            if group < 8:
                side = turn(rim, -4 * group)
            else:
                side = jnp.where(
                    lane < 64, turn(main, -64), jnp.where(lane < 96, turn(main, -36), turn(main, -8))
                )
            pair_even = jnp.where(even, main, side)
            pair_odd = turn(jnp.where(even, side, main), -32)
            for odd, value in enumerate((pair_even, pair_odd)):
                high = value.astype(bf16).astype(f32)
                low = value - high
                planes = (jnp.where(low_half, high, turn(low, 64)), jnp.where(low_half, turn(high, 64), low))
                for second in range(2):
                    for k in range(4):
                        window = planes[second][8 * k : 8 * k + 16].astype(bf16)
                        field[(4 * group + 2 * second + odd) * 32 + 4 * part + k] = window
        return carry

    lax.fori_loop(0, 8, regroup, 0)

    rows16 = lax.broadcasted_iota(jnp.int32, (16, 128), 0).astype(f32) - 1.0
    rows40 = lax.broadcasted_iota(jnp.int32, (40, 128), 0).astype(f32) - 1.0
    nothing = jnp.zeros((24, 256), f32)

    def one(number, slot):
        charge, at_x, at_y, at_z = [slot[i : i + 1] for i in range(4)]
        at_x = at_x - codes[1, number].astype(f32)
        at_z = at_z - codes[2, number].astype(f32)
        weight_x, slope_x = bspline(rows16 - at_x, True)
        weight_z, slope_z = bspline(rows16 - at_z, True)
        along_y = jnp.concatenate(bspline(rows40 - at_y, True), 1)
        y_high = along_y.astype(bf16).astype(f32)
        y_low = along_y - y_high
        both = jnp.concatenate(
            [y_high, nothing, y_high, nothing, y_low, nothing, y_low, nothing], 0
        ).astype(bf16)
        base = codes[0, number]
        window = jnp.concatenate([field[base + 32 * i] for i in range(11)], 0)
        out = jnp.dot(jnp.concatenate([window, window], 1), both, preferred_element_type=f32)
        plain = jnp.zeros((16, 128), f32)
        along_x = jnp.zeros((16, 128), f32)
        sloped = jnp.zeros((16, 128), f32)
        for i in range(11):
            value = out[16 * i : 16 * i + 16, :128]
            slope = out[16 * i : 16 * i + 16, 128:]
            plain = plain + weight_x[i : i + 1] * value
            along_x = along_x + slope_x[i : i + 1] * value
            sloped = sloped + weight_x[i : i + 1] * slope
        minus = -charge
        return jnp.concatenate(
            [
                minus * jnp.sum(along_x * weight_z, 0, keepdims=True),
                minus * jnp.sum(sloped * weight_z, 0, keepdims=True),
                minus * jnp.sum(plain * slope_z, 0, keepdims=True),
                charge,
            ],
            0,
        )

    def interpolate(step, carry):
        source = lax.rem(chunk + step, OWN)
        first = pl.ds(pl.multiple_of(8 * source, 8), 8)
        pair = slots_ref[first, :]
        force[source] = jnp.concatenate(
            [one(2 * source, pair[0:4]), one(2 * source + 1, pair[4:8])], 0
        )
        back_to_me = jnp.logical_and(same, source == chunk)

        @pl.when(jnp.logical_not(back_to_me))
        def _():
            remote(
                force.at[source], force_in.at[mine], force_send, force_recv,
                (grid_bead, source // 8, source % 8),
            ).start()

        @pl.when(back_to_me)
        def _():
            pltpu.make_async_copy(force.at[source], force_in.at[mine], own_sem.at[4]).start()

        return carry

    lax.fori_loop(0, OWN, interpolate, 0)

    chosen = jnp.where(targets(owner_ref[...], True), 1.0, 0.0).astype(bf16)

    @pl.when(same)
    def _():
        settle(force_in.at[mine], own_sem.at[4])
        settle(force_in.at[rest], force_recv)
        settle(force_in.at[rest], force_send)

    @pl.when(jnp.logical_not(same))
    def _():
        settle(force_in, force_recv)
        settle(force_in, force_send)

    for axis in range(3):
        both = jnp.concatenate([force_in[:, axis, :], force_in[:, 4 + axis, :]], 0)
        moved = sum(
            lax.dot_general(chosen, part, (((0,), (0,)), ((), ())), preferred_element_type=f32)
            for part in reversed(three(both))
        )
        spring = 2.0 * frac_ref[axis] - before_ref[axis] - after_ref[axis]
        out_ref[axis] = moved - spring_scale * spring

    for n in range(2):
        settle(lines.at[rest, out_rows[n]], out_send.at[n])
        settle(waves_out.at[rest, back_rows[n]], back_send.at[n])


def grid_to_forces(codes, packed, slots, owner_row, frac, before, after):
    table = tables()
    consts = [jnp.asarray(half) for name in TABLES for half in table[name]]
    dma = pltpu.SemaphoreType.DMA
    chunks = VMEM((OWN, 40, 128), f32)
    return pl.pallas_call(
        wave_kernel,
        out_shape=jax.ShapeDtypeStruct((3, OWN, 128), f32),
        in_specs=[pl.BlockSpec(memory_space=SMEM)] * 2
        + vmem(8)
        + [pl.BlockSpec(memory_space=pl.ANY)] * 12,
        out_specs=pl.BlockSpec(memory_space=VMEM),
        scratch_shapes=[VMEM(const.shape, bf16) for const in consts]
        + [
            chunks, chunks, chunks, chunks,
            VMEM((2, 256, 512), bf16), VMEM((2, 256, 512), bf16),
            VMEM((2, 4, 8, 8, 128), f32), VMEM((2, 4, 8, 8, 128), f32),
            VMEM((10, 264, 128), f32), VMEM((36 * 32, 16, 128), bf16),
            VMEM((OWN, 8, 128), f32), VMEM((OWN, 8, 128), f32),
            dma((12,)), dma((2,)), dma((2,)), dma((2,)), dma((2,)), dma((5,)), dma, dma,
        ],
        compiler_params=pltpu.CompilerParams(
            collective_id=1, has_side_effects=True, vmem_limit_bytes=56 << 20
        ),
        name="grid_to_forces",
    )(
        codes, jnp.asarray(table["in_z"]), packed, slots, owner_row, frac, before, after,
        jnp.asarray(table["column"]), jnp.asarray(table["row"]), *consts,
    )


def local(block_owner, block_tile, atom_cell, atom_frac, charge, zone):
    owner_row = block_owner.reshape(1, OWN)
    frac = jnp.transpose(atom_frac[0], (1, 0, 2))
    slots, before, after = atoms_to_slots(
        owner_row, block_tile.reshape(1, OWN), atom_cell, frac, charge, zone
    )
    packed, codes = spread(slots)
    total = grid_to_forces(codes, packed, slots, owner_row, frac, before, after)
    return jnp.transpose(total, (1, 0, 2))[None]


def solution(mesh):
    return jax.shard_map(
        local,
        mesh=mesh,
        in_specs=(
            P(("px", "py"), None),
            P(("px", "py")),
            P(("px", "py"), None),
            P("bead", ("px", "py"), None, None),
            P(("px", "py"), None),
            P(("px", "py"), None),
        ),
        out_specs=P("bead", ("px", "py"), None, None),
        check_vma=False,
    )
```

```python
import functools
import math

import jax
import jax.numpy as jnp
import ml_dtypes
import numpy as np
from jax import lax
from jax.experimental import pallas as pl
from jax.experimental.pallas import tpu as pltpu
from jax.sharding import PartitionSpec as P

NG = 256
OWN = 64
f32 = jnp.float32
bf16 = jnp.bfloat16
MESH = pl.DeviceIdType.MESH
VMEM = pltpu.VMEM
SMEM = pltpu.SMEM
HBM = pltpu.HBM
ewald_beta = 0.75
spring_scale = 0.25


def halves(table):
    table = table.astype(np.float32)
    high = table.astype(ml_dtypes.bfloat16)
    low = (table - high.astype(np.float32)).astype(ml_dtypes.bfloat16)
    return high, low


def waves(rows, columns):
    angle = (np.outer(rows, columns) % NG) * (2.0 * math.pi / NG)
    return np.cos(angle), np.sin(angle)


@functools.lru_cache(None)
def tables():
    whole = np.arange(NG)
    owner = np.arange(OWN)
    kz = np.stack([2 * owner, 2 * owner + 1])
    cos_z, sin_z = waves(kz.reshape(-1), whole)
    forward_z = np.concatenate([cos_z[:OWN], -sin_z[:OWN], cos_z[OWN:], -sin_z[OWN:]])
    scale = np.where(kz == 0, 1.0, 2.0) / float(NG**3)
    scale = np.repeat(scale, 2, 0).reshape(-1)
    back_z = (forward_z * scale[:, None]).T
    forward_y = np.concatenate(waves(whole, whole), 1)
    rim = (32 * (whole // 32 + 1) + whole % 4) % NG
    fold_y = np.concatenate([rim[:, None] == whole[None, :]] * 2).astype(ml_dtypes.bfloat16)
    unfold_y = np.concatenate([whole[:, None] == rim[None, :]] * 2).astype(ml_dtypes.bfloat16)
    step, block, group = np.meshgrid(np.arange(4), np.arange(8), np.arange(8), indexing="ij")
    place = (32 * block + 4 * group + step).reshape(-1)
    cos_x, sin_x = waves(whole, place)
    forward_x = np.concatenate([cos_x, sin_x])
    back_x = np.concatenate([cos_x.T, sin_x.T])
    wave = (whole + NG // 2) % NG - NG // 2
    theta = wave * (2.0 * math.pi / NG)
    factor = (6.0 / (4.0 + 2.0 * np.cos(theta))) ** 2
    factor = factor * np.exp(-theta * theta / (4.0 * ewald_beta * ewald_beta))
    row = np.zeros((8, 256), np.float32)
    row[0], row[1] = theta * theta, factor
    return dict(
        forward_z=halves(forward_z),
        back_z=halves(back_z),
        forward_y=halves(forward_y),
        fold_y=(fold_y, unfold_y),
        forward_x=halves(forward_x),
        back_x=halves(back_x),
        row=row,
    )


def split(value):
    high = value.astype(bf16)
    return high, (value - high.astype(f32)).astype(bf16)


product = functools.partial(jnp.dot, preferred_element_type=f32)


def dots(a_high, a_low, b_high, b_low):
    return product(a_high, b_high) + (product(a_high, b_low) + product(a_low, b_high))


def lane_of(rank):
    return lax.broadcasted_iota(jnp.int32, (1,) * (rank - 1) + (128,), rank - 1)


def turn(value, steps):
    steps = steps % 128
    if steps == 0:
        return value
    flat = value.reshape(-1, 128)
    return pltpu.roll(flat, steps, 1).reshape(value.shape)


def blocks_exchanged(parts):
    lane = lane_of(parts[0].ndim)
    low = lane < 64
    even = (lane // 32) % 2 == 0
    first = [
        jnp.where(low, parts[0], turn(parts[2], 64)),
        jnp.where(low, parts[1], turn(parts[3], 64)),
        jnp.where(low, turn(parts[0], 64), parts[2]),
        jnp.where(low, turn(parts[1], 64), parts[3]),
    ]
    return [
        jnp.where(even, first[0], turn(first[1], 32)),
        jnp.where(even, turn(first[0], 96), first[1]),
        jnp.where(even, first[2], turn(first[3], 32)),
        jnp.where(even, turn(first[2], 96), first[3]),
    ]


def bspline(offsets, slopes):
    v = jnp.abs(offsets)
    a = jnp.maximum(2.0 - v, 0.0)
    b = jnp.maximum(1.0 - v, 0.0)
    aa = a * a
    bb = b * b
    weight = aa * a * (1.0 / 6.0) - bb * b * (4.0 / 6.0)
    if not slopes:
        return weight
    half = 0.5 * aa - 2.0 * bb
    return weight, jnp.where(offsets < 0.0, -half, half)


def vmem(count):
    return [pl.BlockSpec(memory_space=VMEM)] * count


def targets(owner_row, apart):
    blocks = owner_row.shape[1]
    up = lax.broadcasted_iota(jnp.int32, (blocks, blocks), 0)
    across = lax.broadcasted_iota(jnp.int32, (blocks, blocks), 1)
    owner_column = jnp.sum(jnp.where(up == across, owner_row, 0).astype(f32), 1, keepdims=True)
    owner_float = owner_row.astype(f32)
    before = jnp.where((owner_column == owner_float) & (up < across), 1.0, 0.0)
    rank = jnp.sum(before, 0, keepdims=True)
    target = owner_float + OWN * rank if apart else 2.0 * owner_float + rank
    slot = lax.broadcasted_iota(jnp.int32, (2 * OWN, blocks), 0).astype(f32)
    return slot == target


def three(value):
    high = value.astype(bf16)
    rest = value - high.astype(f32)
    middle = rest.astype(bf16)
    return high, middle, (rest - middle.astype(f32)).astype(bf16)


def remote(src, dst, send_sem, recv_sem, device):
    return pltpu.make_async_remote_copy(
        src_ref=src, dst_ref=dst, send_sem=send_sem, recv_sem=recv_sem,
        device_id=device, device_id_type=MESH,
    )


def settle(ref, sem):
    pltpu.make_async_copy(ref, ref, sem).wait()


def atoms_kernel(
    owner_hbm, tile_hbm, cell_hbm, frac_hbm, charge_hbm, zone_hbm, slots_ref, spring_ref, chosen_ref,
    owner_ref, tile_ref, cell_ref, frac_ref, charge_ref, zone_ref,
    payload, stage, before_ref, after_ref,
    stage_send, stage_recv, send_sem, recv_sem, own_sem, bead_send, bead_recv, in_sem,
):
    loads = [
        pltpu.make_async_copy(src, dst, in_sem.at[i])
        for i, (src, dst) in enumerate(
            (
                (owner_hbm, owner_ref), (tile_hbm, tile_ref), (cell_hbm, cell_ref),
                (frac_hbm, frac_ref), (charge_hbm, charge_ref), (zone_hbm, zone_ref),
            )
        )
    ]
    for copy in loads:
        copy.start()
    bead, px, py = here()
    chunk = px * 8 + py
    barrier = pltpu.get_barrier_semaphore()

    def greet(step, carry):
        other = lax.rem(chunk + step, OWN)
        pl.semaphore_signal(barrier, inc=1, device_id=(bead, other // 8, other % 8), device_id_type=MESH)
        return carry

    lax.fori_loop(1, OWN, greet, 0)
    for step in range(1, 4):
        pl.semaphore_signal(barrier, inc=1, device_id=(lax.rem(bead + step, 4), px, py), device_id_type=MESH)

    for copy in loads:
        copy.wait()
    chosen = jnp.where(targets(owner_ref[...], False), 1.0, 0.0).astype(bf16)
    blocks = cell_ref.shape[0]
    up = lax.broadcasted_iota(jnp.int32, (blocks, blocks), 0)
    across = lax.broadcasted_iota(jnp.int32, (blocks, blocks), 1)
    tile = jnp.sum(jnp.where(up == across, tile_ref[...], 0).astype(f32), 1, keepdims=True)
    tile = tile.astype(jnp.int32)
    cell = cell_ref[...]
    corners = [tile >> 7, (tile >> 5) & 3, tile & 31]
    cells = [cell >> 6, (cell >> 3) & 7, cell & 7]
    fields = [charge_ref[...] * zone_ref[...].astype(f32)]
    for axis in range(3):
        base = (corners[axis] * 8).astype(f32)
        inside = cells[axis].astype(f32) + frac_ref[axis]
        fields.append(base + jnp.minimum(inside, 8.0 - 2.0**-16))
    for place_in, field in enumerate(fields):
        parts = three(field)
        moved = sum(
            jnp.dot(chosen, part, preferred_element_type=f32) for part in reversed(parts)
        )
        payload[pl.ds(place_in, 2 * OWN, stride=4), :] = moved

    pl.semaphore_wait(barrier, OWN - 1 + 3)
    staged = [
        remote(
            payload.at[pl.ds(pl.multiple_of(lax.rem(bead + step, 4) * 128, 128), 128)], stage.at[bead],
            stage_send.at[step - 1], stage_recv.at[step - 1], (lax.rem(bead + step, 4), px, py),
        )
        for step in (1, 3, 2)
    ]
    for copy in staged:
        copy.start()
    springs = [
        remote(frac_ref, target, bead_send.at[i], bead_recv.at[i], (lax.rem(bead + step, 4), px, py))
        for i, (target, step) in enumerate(((before_ref, 1), (after_ref, 3)))
    ]

    mark = pl.ds(pl.multiple_of(chunk * 8, 8), 8)

    def deliver(source, from_bead):
        def send(step, carry):
            j = lax.rem(step + 2 * px + 1, 16)
            device = (bead, j // 2, 2 * from_bead + j % 2)
            mine = jnp.logical_and(j == 2 * px + py % 2, py // 2 == from_bead)
            piece = source(j)

            @pl.when(jnp.logical_not(mine))
            def _():
                remote(piece, slots_ref.at[mark], send_sem, recv_sem, device).start()

            @pl.when(mine)
            def _():
                pltpu.make_async_copy(piece, slots_ref.at[mark], own_sem).start()

            return carry

        lax.fori_loop(0, 16, send, 0)

    deliver(lambda j: payload.at[pl.ds(pl.multiple_of(bead * 128 + j * 8, 8), 8)], bead)
    for copy in springs:
        copy.start()
    for step, copy in zip((1, 3, 2), staged):
        copy.wait_recv()
        other = lax.rem(bead + 4 - step, 4)
        deliver(lambda j: stage.at[other, pl.ds(pl.multiple_of(j * 8, 8), 8)], other)
    chosen_ref[...] = jnp.where(targets(owner_ref[...], True), 1.0, 0.0).astype(bf16)
    for copy in springs:
        copy.wait()
    for axis in range(3):
        bend = 2.0 * frac_ref[axis] - before_ref[axis] - after_ref[axis]
        spring_ref[axis] = -spring_scale * bend
    settle(slots_ref.at[mark], own_sem)
    rest = pl.ds(0, 8 * OWN - 8)
    settle(slots_ref.at[rest], recv_sem)
    settle(slots_ref.at[rest], send_sem)
    for copy in staged:
        copy.wait_send()


def atoms_to_slots(owner_row, tile_row, cell, frac, charge, zone):
    dma = pltpu.SemaphoreType.DMA
    return pl.pallas_call(
        atoms_kernel,
        out_shape=[
            jax.ShapeDtypeStruct((8 * OWN, 128), f32),
            jax.ShapeDtypeStruct((3, OWN, 128), f32),
            jax.ShapeDtypeStruct((2 * OWN, OWN), bf16),
        ],
        in_specs=[pl.BlockSpec(memory_space=HBM)] * 6,
        out_specs=vmem(3),
        scratch_shapes=[
            VMEM((1, OWN), jnp.int32), VMEM((1, OWN), jnp.int32), VMEM((OWN, 128), jnp.int32),
            VMEM((3, OWN, 128), f32), VMEM((OWN, 128), f32), VMEM((OWN, 128), jnp.int32),
            VMEM((8 * OWN, 128), f32), VMEM((4, 128, 128), f32),
            VMEM((3, OWN, 128), f32), VMEM((3, OWN, 128), f32),
            dma((3,)), dma((3,)), dma, dma, dma, dma((2,)), dma((2,)), dma((6,)),
        ],
        compiler_params=pltpu.CompilerParams(
            collective_id=0, has_side_effects=True, vmem_limit_bytes=60 << 20
        ),
        name="atoms_to_slots",
    )(owner_row, tile_row, cell, frac, charge, zone)


def slot_list(slots_ref, list_ref, codes, codes_scalar, sem):
    charge = slots_ref[pl.ds(0, 2 * OWN, stride=4), :]
    along_x = slots_ref[pl.ds(1, 2 * OWN, stride=4), :]
    along_z = slots_ref[pl.ds(3, 2 * OWN, stride=4), :]
    tile_x = (jnp.max(along_x, 1, keepdims=True) * 0.125).astype(jnp.int32)
    tile_z = (jnp.max(along_z, 1, keepdims=True) * 0.125).astype(jnp.int32)
    filled = jnp.max(jnp.abs(charge), 1, keepdims=True) > 0.0
    up = lax.broadcasted_iota(jnp.int32, (128, 128), 0)
    across = lax.broadcasted_iota(jnp.int32, (128, 128), 1)
    sub = lax.broadcasted_iota(jnp.int32, (8, 128), 0)
    value = jnp.zeros((8, 128), f32)
    columns = (256 * tile_x + tile_z, 8 * tile_x, 8 * tile_z, filled.astype(jnp.int32))
    for place_in, column in enumerate(columns):
        row = jnp.sum(jnp.where(up == across, column.astype(f32), 0.0), 0, keepdims=True)
        value = jnp.where(sub == place_in, row, value)
    codes[...] = value.astype(jnp.int32)
    copy = pltpu.make_async_copy(codes, codes_scalar, sem)
    copy.start()
    copy.wait()

    def step(slot, carry):
        count, empty = carry
        held = codes_scalar[3, slot] > 0
        list_ref[count] = slot
        return count + held.astype(jnp.int32), jnp.where(held, empty, slot)

    count, empty = lax.fori_loop(0, 2 * OWN, step, (jnp.int32(0), jnp.int32(0)))
    for k in range(15):
        list_ref[count + k] = empty
    list_ref[255] = (count + 15) // 16


def spread_kernel(slots_ref, out_hbm, codes_scalar, list_ref, density, codes, out_ref, sem, out_sem):
    slot_list(slots_ref, list_ref, codes, codes_scalar, sem)
    density[...] = jnp.zeros_like(density)
    rows16 = lax.broadcasted_iota(jnp.int32, (16, 128), 0).astype(f32) - 1.0
    rows40 = lax.broadcasted_iota(jnp.int32, (40, 128), 0).astype(f32) - 1.0

    def one(slot):
        plane_x, row_z = codes_scalar[1, slot], codes_scalar[2, slot]
        charge = slots_ref[pl.ds(4 * slot, 1), :]
        at_x = slots_ref[pl.ds(4 * slot + 1, 1), :] - plane_x.astype(f32)
        at_y = slots_ref[pl.ds(4 * slot + 2, 1), :]
        at_z = slots_ref[pl.ds(4 * slot + 3, 1), :] - row_z.astype(f32)
        weight_x = bspline(rows16 - at_x, False) * charge
        weight_z = bspline(rows16 - at_z, False)
        weight_y = jnp.concatenate([bspline(rows40 - at_y, False), jnp.zeros((24, 128), f32)], 0)
        plane = jnp.concatenate([weight_x[i : i + 1] * weight_z for i in range(11)], 0)
        plane = jnp.concatenate(split(plane), 1)
        y_high, y_low = split(weight_y)
        left = jnp.concatenate([y_high, y_low], 0)
        right = jnp.concatenate([y_high, jnp.zeros((64, 128), bf16)], 0)
        both = jnp.concatenate([left, right], 1)
        out = lax.dot_general(plane, both, (((1,), (1,)), ((), ())), preferred_element_type=f32)
        return plane_x, row_z, out

    def put(plane_x, row_z, out):
        base = pl.multiple_of(row_z, 8)
        for i in range(11):
            density[plane_x + i, pl.ds(base, 16), :] += out[16 * i : 16 * i + 16]

    def step(index, carry):
        for found in [one(list_ref[16 * index + k]) for k in range(16)]:
            put(*found)
        return carry

    lax.fori_loop(0, list_ref[255], step, 0)

    lane = lane_of(2)
    low = lane < 64
    even = (lane // 32) % 2 == 0

    def fold(plane, carry):
        density[plane, 0:8, :] += density[plane, 256:264, :]
        return carry

    lax.fori_loop(0, 36, fold, 0)

    def regroup(chunk, carry):
        here = pl.ds(pl.multiple_of(chunk * 32, 32), 32)
        rim = jnp.zeros((32, 128), f32)

        def keep(group, value):
            out_ref[group, here, :] = value

        for group in range(9):
            four = [density[4 * group + i, here, :] for i in range(4)]
            pair_even = jnp.where(low, four[0], four[2]) + turn(jnp.where(low, four[2], four[0]), 64)
            pair_odd = jnp.where(low, four[1], four[3]) + turn(jnp.where(low, four[3], four[1]), 64)
            pair_odd = turn(pair_odd, 32)
            main = jnp.where(even, pair_even, pair_odd)
            side = jnp.where(even, pair_odd, pair_even)
            if group < 8:
                keep(group, main)
                rim = rim + turn(side, 4 * group)
            else:
                last = lane >= 96
                corner = jnp.where((lane >= 96) & (lane < 100), turn(side, 64), 0.0)
                corner = jnp.where((lane >= 100) & (lane < 104), turn(side, 36), corner)
                corner = jnp.where((lane >= 104) & (lane < 108), turn(side, 8), corner)
                keep(8, jnp.where(last, corner, main))
        keep(9, rim)
        pltpu.make_async_copy(out_ref.at[:, here, :], out_hbm.at[:, here, :], out_sem.at[chunk]).start()
        return carry

    lax.fori_loop(0, 8, regroup, 0)
    for chunk in range(8):
        here = pl.ds(32 * chunk, 32)
        pltpu.make_async_copy(out_ref.at[:, here, :], out_hbm.at[:, here, :], out_sem.at[chunk]).wait()


def spread(slots):
    return pl.pallas_call(
        spread_kernel,
        out_shape=[
            jax.ShapeDtypeStruct((10, 256, 128), f32),
            jax.ShapeDtypeStruct((8, 128), jnp.int32),
        ],
        in_specs=vmem(1),
        out_specs=[pl.BlockSpec(memory_space=pl.ANY), pl.BlockSpec(memory_space=SMEM)],
        scratch_shapes=[
            SMEM((256,), jnp.int32),
            VMEM((36, 264, 128), f32),
            VMEM((8, 128), jnp.int32),
            VMEM((10, 256, 128), f32),
            pltpu.SemaphoreType.DMA,
            pltpu.SemaphoreType.DMA((8,)),
        ],
        compiler_params=pltpu.CompilerParams(vmem_limit_bytes=60 << 20),
        name="spread",
    )(slots)


TABLES = ("forward_z", "forward_y", "forward_x", "back_x", "fold_y", "back_z")
ROWS_OF = (0, 8, 24, 32)


def here():
    return lax.axis_index("bead"), lax.axis_index("px"), lax.axis_index("py")


def place(number, bead):
    return (number // 16, (number // 2) % 8, 2 * bead + number % 2)


def hop(step):
    return lax.rem(step * 37, OWN)


def shifted(value, steps):
    if steps == 1:
        return jnp.concatenate([value[7:8], value[0:7]], 0)
    return jnp.concatenate([value[1:8], value[0:1]], 0)


def wave_kernel(
    codes, *rest,
):
    table_refs, rest = rest[:17], rest[17:]
    out_ref, rest = rest[0], rest[1:]
    table_vmem, rest = rest[:17], rest[17:]
    packed, fz_high, fz_low = table_vmem[:3]
    row_ref, slots_ref, spring_ref, chosen_ref = table_vmem[13:]
    (
        lines, waves_in, waves_out, lines_in, plane, plane_rim, rims, rims_out,
        lines_z, field, force, force_in, table_sem, out_send, out_recv, back_send, back_recv,
        own_sem, force_send, force_recv,
    ) = rest
    (fz, fy, fx, bx, fold, bz) = [(table_vmem[2 * i + 1], table_vmem[2 * i + 2]) for i in range(6)]
    bead, px, py = here()
    mine, grid_bead, chunk = bead * 16 + px * 2 + py % 2, py // 2, px * 8 + py
    same = bead == grid_bead
    barrier = pltpu.get_barrier_semaphore()

    table_copies = [
        pltpu.make_async_copy(table_refs[i], table_vmem[i], table_sem.at[i]) for i in range(17)
    ]
    for copy in table_copies[:3]:
        copy.start()

    def greet(step, carry):
        other = lax.rem(mine + hop(step), OWN)
        pl.semaphore_signal(barrier, inc=1, device_id=place(other, grid_bead), device_id_type=MESH)
        return carry

    def greet_atoms(step, carry):
        other = lax.rem(mine + hop(step), OWN)
        pl.semaphore_signal(barrier, inc=1, device_id=place(other, bead), device_id_type=MESH)
        return carry

    lax.fori_loop(1, OWN, greet, 0)

    @pl.when(same)
    def _():
        lax.fori_loop(1, OWN, greet_atoms, 0)

    @pl.when(jnp.logical_not(same))
    def _():
        lax.fori_loop(0, OWN, greet_atoms, 0)

    for copy in table_copies[3:]:
        copy.start()
    for copy in table_copies[:3]:
        copy.wait()

    for pair in range(5):
        high, low = split(jnp.concatenate([packed[2 * pair], packed[2 * pair + 1]], 1))
        result = dots(fz[0][...], fz[1][...], high, low)
        for part in range(2):
            group = 2 * pair + part
            for c in range(4):
                start = ROWS_OF[c] + group if group < 8 else 16 + c + 4 * (group - 8)
                lines[:, start, :] = result[64 * c : 64 * c + 64, 128 * part : 128 * part + 128]

    pl.semaphore_wait(barrier, 2 * OWN - 1 - same.astype(jnp.int32))

    def own(src, dst, rows, sem):
        return pltpu.make_async_copy(src.at[mine, rows], dst.at[mine, rows], sem)

    def send_all(src, dst, rows, send_sem, recv_sem):
        def send(step, carry):
            other = lax.rem(mine + hop(step), OWN)
            remote(
                src.at[other, rows], dst.at[mine, rows], send_sem, recv_sem, place(other, grid_bead)
            ).start()
            return carry

        lax.fori_loop(1, OWN, send, 0)

    rest = pl.ds(0, OWN - 1)
    out_rows = (pl.ds(0, 24), pl.ds(24, 16))
    back_rows = (pl.ds(0, 16), pl.ds(16, 24))
    for n in range(2):
        own(lines, waves_in, out_rows[n], own_sem.at[n]).start()
        send_all(lines, waves_in, out_rows[n], out_send.at[n], out_recv.at[n])

    for copy in table_copies[3:]:
        copy.wait()

    lane = lane_of(3)
    sub = lax.broadcasted_iota(jnp.int32, (1, 8, 128), 1)
    lane_group = (lane // 4) % 8
    square_y, factor_y = row_ref[0:1, :], row_ref[1:2, :]
    up = lax.broadcasted_iota(jnp.int32, (256, 256), 0)
    across = lax.broadcasted_iota(jnp.int32, (256, 256), 1)
    square_x = jnp.sum(jnp.where(up == across, square_y, 0.0), 1, keepdims=True)
    factor_x = jnp.sum(jnp.where(up == across, factor_y, 0.0), 1, keepdims=True)
    mine_z = lax.broadcasted_iota(jnp.int32, (1, 256), 1) - 2 * mine

    for n in range(2):
        own(lines, waves_in, out_rows[n], own_sem.at[n]).wait()
        settle(waves_in.at[rest, out_rows[n]], out_recv.at[n])
        for q in range(2):
            if n == 0:
                extra = blocks_exchanged(
                    [waves_in[pl.ds(4 * q + j, 8, stride=8), 16:24, :] for j in range(4)]
                )
                for i in range(4):
                    rims[q, i] = extra[i]
            else:
                extra = [rims[q, i] for i in range(4)]
            for half in range(2):
                c = 2 * n + half
                main = blocks_exchanged(
                    [
                        waves_in[pl.ds(4 * q + j, 8, stride=8), ROWS_OF[c] : ROWS_OF[c] + 8, :]
                        for j in range(4)
                    ]
                )
                for i in range(4):
                    value = main[i]
                    rim = jnp.where(lane_group == sub, extra[(i + 1) % 4][:, 4 + c : 5 + c, :], 0.0)
                    if i < 3:
                        value = value + jnp.where(sub == 0, shifted(extra[i][:, c : c + 1, :], 1), 0.0)
                        corner = shifted(extra[3][:, c : c + 1, :], 1)
                        rim = rim + jnp.where((sub == 0) & (lane_group == i), corner, 0.0)
                    lines_of = slice(64 * i, 64 * i + 64)
                    plane[half, lines_of, 128 * q : 128 * q + 128] = value.reshape(64, 128)
                    high, low = split(rim.reshape(64, 128))
                    plane_rim[half, lines_of, 128 * q : 128 * q + 128] = high
                    plane_rim[half, lines_of, 256 + 128 * q : 384 + 128 * q] = low

        real, imag = [
            dots(*split(plane[half] + product(plane_rim[half], fold[0][...])), fy[0][...], fy[1][...])
            for half in range(2)
        ]
        spec = jnp.concatenate(
            [real[:, :256] + imag[:, 256:], imag[:, :256] - real[:, 256:]], 1
        )
        both = dots(fx[0][...], fx[1][...], *split(spec))
        square_z = jnp.sum(jnp.where(mine_z == n, square_y, 0.0), 1, keepdims=True)
        factor_z = jnp.sum(jnp.where(mine_z == n, factor_y, 0.0), 1, keepdims=True)
        square = square_x + square_y + square_z
        green = factor_x * factor_y * (factor_z * (4.0 * math.pi))
        green = jnp.where(square > 0.0, green / jnp.where(square > 0.0, square, 1.0), 0.0)
        spec = jnp.concatenate(
            [
                (both[:256, :256] + both[256:, 256:]) * green,
                (both[:256, 256:] - both[256:, :256]) * green,
            ],
            1,
        )
        both = dots(bx[0][...], bx[1][...], *split(spec))
        spec = jnp.concatenate(
            [both[:256, :256] - both[256:, 256:], both[:256, 256:] + both[256:, :256]], 0
        )
        both = dots(*split(spec), fy[0][...], fy[1][...])
        back = [both[:256, :256] - both[256:, 256:], both[256:, :256] + both[:256, 256:]]
        back_rim = [product(jnp.concatenate(split(value), 1), fold[1][...]) for value in back]

        for q in range(2):
            if n == 0:
                extra = [jnp.zeros((8, 8, 128), f32) for _ in range(4)]
            else:
                extra = [rims_out[q, i] for i in range(4)]
            for half in range(2):
                c = 2 * n + half
                main, corner = [], jnp.zeros((8, 1, 128), f32)
                for i in range(4):
                    lines_of = slice(64 * i, 64 * i + 64)
                    value = back[half][lines_of, 128 * q : 128 * q + 128].reshape(8, 8, 128)
                    rim = back_rim[half][lines_of, 128 * q : 128 * q + 128].reshape(8, 8, 128)
                    main.append(value)
                    if i < 3:
                        extra[i] = jnp.where(sub == c, shifted(value[:, 0:1, :], -1), extra[i])
                        corner = jnp.where(lane_group == i, shifted(rim[:, 0:1, :], -1), corner)
                    side = jnp.sum(jnp.where(lane_group == sub, rim, 0.0), 1, keepdims=True)
                    extra[(i + 1) % 4] = jnp.where(sub == 4 + c, side, extra[(i + 1) % 4])
                extra[3] = jnp.where(sub == c, corner, extra[3])
                main = blocks_exchanged(main)
                for j in range(4):
                    waves_out[pl.ds(4 * q + j, 8, stride=8), ROWS_OF[c] : ROWS_OF[c] + 8, :] = main[j]
            if n == 0:
                for i in range(4):
                    rims_out[q, i] = extra[i]
            else:
                extra = blocks_exchanged(extra)
                for j in range(4):
                    waves_out[pl.ds(4 * q + j, 8, stride=8), 16:24, :] = extra[j]
        own(waves_out, lines_in, back_rows[n], own_sem.at[2 + n]).start()
        send_all(waves_out, lines_in, back_rows[n], back_send.at[n], back_recv.at[n])

    for n in range(2):
        own(waves_out, lines_in, back_rows[n], own_sem.at[2 + n]).wait()
        settle(lines_in.at[rest, back_rows[n]], back_recv.at[n])

    for pair in range(5):
        columns = []
        for group in (2 * pair, 2 * pair + 1):
            starts = [
                ROWS_OF[c] + group if group < 8 else 16 + c + 4 * (group - 8) for c in range(4)
            ]
            columns.append(jnp.concatenate([lines_in[:, start, :] for start in starts], 0))
        result = dots(bz[0][...], bz[1][...], *split(jnp.concatenate(columns, 1)))
        for part in range(2):
            lines_z[2 * pair + part, 0:256, :] = result[:, 128 * part : 128 * part + 128]
            lines_z[2 * pair + part, 256:264, :] = result[0:8, 128 * part : 128 * part + 128]

    lane = lane_of(2)
    low_half = lane < 64
    even = (lane // 32) % 2 == 0

    def regroup(part, carry):
        at = pl.ds(pl.multiple_of(part * 32, 32), 40)
        rim = lines_z[9, at, :]
        for group in range(9):
            main = lines_z[group, at, :]
            if group < 8:
                side = turn(rim, -4 * group)
            else:
                side = jnp.where(
                    lane < 64, turn(main, -64), jnp.where(lane < 96, turn(main, -36), turn(main, -8))
                )
            pair_even = jnp.where(even, main, side)
            pair_odd = turn(jnp.where(even, side, main), -32)
            for odd, value in enumerate((pair_even, pair_odd)):
                high = value.astype(bf16).astype(f32)
                low = value - high
                planes = (jnp.where(low_half, high, turn(low, 64)), jnp.where(low_half, turn(high, 64), low))
                for second in range(2):
                    for k in range(4):
                        window = planes[second][8 * k : 8 * k + 16].astype(bf16)
                        field[(4 * group + 2 * second + odd) * 32 + 4 * part + k] = window
        return carry

    lax.fori_loop(0, 8, regroup, 0)

    rows16 = lax.broadcasted_iota(jnp.int32, (16, 128), 0).astype(f32) - 1.0
    rows40 = lax.broadcasted_iota(jnp.int32, (40, 128), 0).astype(f32) - 1.0
    nothing = jnp.zeros((24, 256), f32)

    def one(number, slot):
        charge, at_x, at_y, at_z = [slot[i : i + 1] for i in range(4)]
        at_x = at_x - codes[1, number].astype(f32)
        at_z = at_z - codes[2, number].astype(f32)
        weight_x, slope_x = bspline(rows16 - at_x, True)
        weight_z, slope_z = bspline(rows16 - at_z, True)
        along_y = jnp.concatenate(bspline(rows40 - at_y, True), 1)
        y_high, y_low = split(jnp.concatenate([along_y, nothing], 0))
        both = jnp.concatenate([y_high, y_high, y_low, y_low], 0)
        base = codes[0, number]
        window = jnp.concatenate([field[base + 32 * i] for i in range(11)], 0)
        out = jnp.dot(jnp.concatenate([window, window], 1), both, preferred_element_type=f32)
        plain = jnp.zeros((16, 128), f32)
        along_x = jnp.zeros((16, 128), f32)
        sloped = jnp.zeros((16, 128), f32)
        for i in range(11):
            value = out[16 * i : 16 * i + 16, :128]
            slope = out[16 * i : 16 * i + 16, 128:]
            plain = plain + weight_x[i : i + 1] * value
            along_x = along_x + slope_x[i : i + 1] * value
            sloped = sloped + weight_x[i : i + 1] * slope
        minus = -charge
        return jnp.concatenate(
            [
                minus * jnp.sum(along_x * weight_z, 0, keepdims=True),
                minus * jnp.sum(sloped * weight_z, 0, keepdims=True),
                minus * jnp.sum(plain * slope_z, 0, keepdims=True),
                charge,
            ],
            0,
        )

    def interpolate(step, carry):
        sources = [lax.rem(chunk + hop(4 * step + k), OWN) for k in range(4)]
        found = []
        for source in sources:
            pair = slots_ref[pl.ds(pl.multiple_of(8 * source, 8), 8), :]
            found.append(
                jnp.concatenate([one(2 * source, pair[0:4]), one(2 * source + 1, pair[4:8])], 0)
            )
        for source, value in zip(sources, found):
            force[source] = value
        for source in sources:
            back_to_me = jnp.logical_and(same, source == chunk)

            @pl.when(jnp.logical_not(back_to_me))
            def _():
                remote(
                    force.at[source], force_in.at[mine], force_send, force_recv,
                    (grid_bead, source // 8, source % 8),
                ).start()

            @pl.when(back_to_me)
            def _():
                pltpu.make_async_copy(force.at[source], force_in.at[mine], own_sem.at[4]).start()

        return carry

    lax.fori_loop(0, OWN // 4, interpolate, 0)

    chosen = chosen_ref[...]

    @pl.when(same)
    def _():
        settle(force_in.at[mine], own_sem.at[4])
        settle(force_in.at[rest], force_recv)
        settle(force_in.at[rest], force_send)

    @pl.when(jnp.logical_not(same))
    def _():
        settle(force_in, force_recv)
        settle(force_in, force_send)

    for axis in range(3):
        both = jnp.concatenate([force_in[:, axis, :], force_in[:, 4 + axis, :]], 0)
        moved = sum(
            lax.dot_general(chosen, part, (((0,), (0,)), ((), ())), preferred_element_type=f32)
            for part in reversed(three(both))
        )
        out_ref[axis] = moved + spring_ref[axis]

    for n in range(2):
        settle(lines.at[rest, out_rows[n]], out_send.at[n])
        settle(waves_out.at[rest, back_rows[n]], back_send.at[n])


def grid_to_forces(codes, packed, slots, spring, chosen):
    table = tables()
    consts = [packed] + [jnp.asarray(half) for name in TABLES for half in table[name]]
    consts += [jnp.asarray(table["row"]), slots, spring, chosen]
    dma = pltpu.SemaphoreType.DMA
    chunks = VMEM((OWN, 40, 128), f32)
    return pl.pallas_call(
        wave_kernel,
        out_shape=jax.ShapeDtypeStruct((3, OWN, 128), f32),
        in_specs=[pl.BlockSpec(memory_space=SMEM)] + [pl.BlockSpec(memory_space=HBM)] * 17,
        out_specs=pl.BlockSpec(memory_space=VMEM),
        scratch_shapes=[VMEM(const.shape, const.dtype) for const in consts]
        + [
            chunks, chunks, chunks, chunks,
            VMEM((2, 256, 256), f32), VMEM((2, 256, 512), bf16),
            VMEM((2, 4, 8, 8, 128), f32), VMEM((2, 4, 8, 8, 128), f32),
            VMEM((10, 264, 128), f32), VMEM((36 * 32, 16, 128), bf16),
            VMEM((OWN, 8, 128), f32), VMEM((OWN, 8, 128), f32),
            dma((17,)), dma((2,)), dma((2,)), dma((2,)), dma((2,)), dma((5,)), dma, dma,
        ],
        compiler_params=pltpu.CompilerParams(
            collective_id=1, has_side_effects=True, vmem_limit_bytes=60 << 20
        ),
        name="grid_to_forces",
    )(
        codes, *consts,
    )


def local(block_owner, block_tile, atom_cell, atom_frac, charge, zone):
    owner_row = block_owner.reshape(1, OWN)
    frac = jnp.transpose(atom_frac[0], (1, 0, 2))
    slots, spring, chosen = atoms_to_slots(
        owner_row, block_tile.reshape(1, OWN), atom_cell, frac, charge, zone
    )
    packed, codes = spread(slots)
    total = grid_to_forces(codes, packed, slots, spring, chosen)
    return jnp.transpose(total, (1, 0, 2))[None]


def solution(mesh):
    return jax.shard_map(
        local,
        mesh=mesh,
        in_specs=(
            P(("px", "py"), None),
            P(("px", "py")),
            P(("px", "py"), None),
            P("bead", ("px", "py"), None, None),
            P(("px", "py"), None),
            P(("px", "py"), None),
        ),
        out_specs=P("bead", ("px", "py"), None, None),
        check_vma=False,
    )
```

```python
import functools
import math

import jax
import jax.numpy as jnp
import ml_dtypes
import numpy as np
from jax import lax
from jax.experimental import pallas as pl
from jax.experimental.pallas import tpu as pltpu
from jax.sharding import PartitionSpec as P

NG = 256
OWN = 64
f32 = jnp.float32
bf16 = jnp.bfloat16
MESH = pl.DeviceIdType.MESH
VMEM = pltpu.VMEM
SMEM = pltpu.SMEM
HBM = pltpu.HBM
ewald_beta = 0.75
spring_scale = 0.25


def halves(table):
    table = table.astype(np.float32)
    high = table.astype(ml_dtypes.bfloat16)
    low = (table - high.astype(np.float32)).astype(ml_dtypes.bfloat16)
    return high, low


def waves(rows, columns):
    angle = (np.outer(rows, columns) % NG) * (2.0 * math.pi / NG)
    return np.cos(angle), np.sin(angle)


@functools.lru_cache(None)
def tables():
    whole = np.arange(NG)
    owner = np.arange(OWN)
    kz = np.stack([2 * owner, 2 * owner + 1])
    cos_z, sin_z = waves(kz.reshape(-1), whole)
    forward_z = np.concatenate([cos_z[:OWN], -sin_z[:OWN], cos_z[OWN:], -sin_z[OWN:]])
    scale = np.where(kz == 0, 1.0, 2.0) / float(NG**3)
    scale = np.repeat(scale, 2, 0).reshape(-1)
    back_z = (forward_z * scale[:, None]).T
    forward_y = np.concatenate(waves(whole, whole), 1)
    rim = (32 * (whole // 32 + 1) + whole % 4) % NG
    fold_y = np.concatenate([rim[:, None] == whole[None, :]] * 2).astype(ml_dtypes.bfloat16)
    unfold_y = np.concatenate([whole[:, None] == rim[None, :]] * 2).astype(ml_dtypes.bfloat16)
    step, block, group = np.meshgrid(np.arange(4), np.arange(8), np.arange(8), indexing="ij")
    place = (32 * block + 4 * group + step).reshape(-1)
    cos_x, sin_x = waves(whole, place)
    forward_x = np.concatenate([cos_x, sin_x])
    back_x = np.concatenate([cos_x.T, sin_x.T])
    wave = (whole + NG // 2) % NG - NG // 2
    theta = wave * (2.0 * math.pi / NG)
    factor = (6.0 / (4.0 + 2.0 * np.cos(theta))) ** 2
    factor = factor * np.exp(-theta * theta / (4.0 * ewald_beta * ewald_beta))
    row = np.zeros((8, 256), np.float32)
    row[0], row[1] = theta * theta, factor
    return dict(
        forward_z=halves(forward_z),
        back_z=halves(back_z),
        forward_y=halves(forward_y),
        fold_y=(fold_y, unfold_y),
        forward_x=halves(forward_x),
        back_x=halves(back_x),
        row=row,
    )


def split(value):
    high = value.astype(bf16)
    return high, (value - high.astype(f32)).astype(bf16)


product = functools.partial(jnp.dot, preferred_element_type=f32)


def dots(a_high, a_low, b_high, b_low):
    return product(a_high, b_high) + (product(a_high, b_low) + product(a_low, b_high))


def lane_of(rank):
    return lax.broadcasted_iota(jnp.int32, (1,) * (rank - 1) + (128,), rank - 1)


def turn(value, steps):
    steps = steps % 128
    if steps == 0:
        return value
    flat = value.reshape(-1, 128)
    return pltpu.roll(flat, steps, 1).reshape(value.shape)


def blocks_exchanged(parts):
    lane = lane_of(parts[0].ndim)
    low = lane < 64
    even = (lane // 32) % 2 == 0
    first = [
        jnp.where(low, parts[0], turn(parts[2], 64)),
        jnp.where(low, parts[1], turn(parts[3], 64)),
        jnp.where(low, turn(parts[0], 64), parts[2]),
        jnp.where(low, turn(parts[1], 64), parts[3]),
    ]
    return [
        jnp.where(even, first[0], turn(first[1], 32)),
        jnp.where(even, turn(first[0], 96), first[1]),
        jnp.where(even, first[2], turn(first[3], 32)),
        jnp.where(even, turn(first[2], 96), first[3]),
    ]


def bspline(offsets, slopes):
    v = jnp.abs(offsets)
    a = jnp.maximum(2.0 - v, 0.0)
    b = jnp.maximum(1.0 - v, 0.0)
    aa = a * a
    bb = b * b
    weight = aa * a * (1.0 / 6.0) - bb * b * (4.0 / 6.0)
    if not slopes:
        return weight
    half = 0.5 * aa - 2.0 * bb
    return weight, jnp.where(offsets < 0.0, -half, half)


def vmem(count):
    return [pl.BlockSpec(memory_space=VMEM)] * count


def targets(owner_row, apart):
    blocks = owner_row.shape[1]
    up = lax.broadcasted_iota(jnp.int32, (blocks, blocks), 0)
    across = lax.broadcasted_iota(jnp.int32, (blocks, blocks), 1)
    owner_column = jnp.sum(jnp.where(up == across, owner_row, 0).astype(f32), 1, keepdims=True)
    owner_float = owner_row.astype(f32)
    before = jnp.where((owner_column == owner_float) & (up < across), 1.0, 0.0)
    rank = jnp.sum(before, 0, keepdims=True)
    target = owner_float + OWN * rank if apart else 2.0 * owner_float + rank
    slot = lax.broadcasted_iota(jnp.int32, (2 * OWN, blocks), 0).astype(f32)
    return slot == target


def three(value):
    high = value.astype(bf16)
    rest = value - high.astype(f32)
    middle = rest.astype(bf16)
    return high, middle, (rest - middle.astype(f32)).astype(bf16)


def remote(src, dst, send_sem, recv_sem, device):
    return pltpu.make_async_remote_copy(
        src_ref=src, dst_ref=dst, send_sem=send_sem, recv_sem=recv_sem,
        device_id=device, device_id_type=MESH,
    )


def settle(ref, sem):
    pltpu.make_async_copy(ref, ref, sem).wait()


def atoms_kernel(
    owner_hbm, tile_hbm, cell_hbm, frac_hbm, charge_hbm, zone_hbm, slots_ref, spring_ref, chosen_ref,
    owner_ref, tile_ref, cell_ref, frac_ref, charge_ref, zone_ref,
    payload, stage, before_ref, after_ref,
    stage_send, stage_recv, send_sem, recv_sem, own_sem, bead_send, bead_recv, in_sem,
):
    loads = [
        pltpu.make_async_copy(src, dst, in_sem.at[i])
        for i, (src, dst) in enumerate(
            (
                (owner_hbm, owner_ref), (tile_hbm, tile_ref), (cell_hbm, cell_ref),
                (frac_hbm, frac_ref), (charge_hbm, charge_ref), (zone_hbm, zone_ref),
            )
        )
    ]
    for copy in loads:
        copy.start()
    bead, px, py = here()
    chunk = px * 8 + py
    barrier = pltpu.get_barrier_semaphore()

    def greet(step, carry):
        other = lax.rem(chunk + step, OWN)
        pl.semaphore_signal(barrier, inc=1, device_id=(bead, other // 8, other % 8), device_id_type=MESH)
        return carry

    lax.fori_loop(1, OWN, greet, 0)
    for step in range(1, 4):
        pl.semaphore_signal(barrier, inc=1, device_id=(lax.rem(bead + step, 4), px, py), device_id_type=MESH)

    for copy in loads:
        copy.wait()
    chosen = jnp.where(targets(owner_ref[...], False), 1.0, 0.0).astype(bf16)
    blocks = cell_ref.shape[0]
    up = lax.broadcasted_iota(jnp.int32, (blocks, blocks), 0)
    across = lax.broadcasted_iota(jnp.int32, (blocks, blocks), 1)
    tile = jnp.sum(jnp.where(up == across, tile_ref[...], 0).astype(f32), 1, keepdims=True)
    tile = tile.astype(jnp.int32)
    cell = cell_ref[...]
    corners = [tile >> 7, (tile >> 5) & 3, tile & 31]
    cells = [cell >> 6, (cell >> 3) & 7, cell & 7]
    fields = [charge_ref[...] * zone_ref[...].astype(f32)]
    for axis in range(3):
        base = (corners[axis] * 8).astype(f32)
        inside = cells[axis].astype(f32) + frac_ref[axis]
        fields.append(base + jnp.minimum(inside, 8.0 - 2.0**-16))
    for place_in, field in enumerate(fields):
        parts = three(field)
        moved = sum(
            jnp.dot(chosen, part, preferred_element_type=f32) for part in reversed(parts)
        )
        payload[pl.ds(place_in, 2 * OWN, stride=4), :] = moved

    pl.semaphore_wait(barrier, OWN - 1 + 3)
    staged = [
        remote(
            payload.at[pl.ds(pl.multiple_of(lax.rem(bead + step, 4) * 128, 128), 128)], stage.at[bead],
            stage_send.at[step - 1], stage_recv.at[step - 1], (lax.rem(bead + step, 4), px, py),
        )
        for step in (1, 3, 2)
    ]
    for copy in staged:
        copy.start()
    springs = [
        remote(frac_ref, target, bead_send.at[i], bead_recv.at[i], (lax.rem(bead + step, 4), px, py))
        for i, (target, step) in enumerate(((before_ref, 1), (after_ref, 3)))
    ]

    mark = pl.ds(pl.multiple_of(chunk * 8, 8), 8)

    def deliver(source, from_bead):
        def send(step, carry):
            j = lax.rem(step + 2 * px + py % 2, 16)
            remote(
                source(j), slots_ref.at[mark], send_sem, recv_sem, (bead, j // 2, 2 * from_bead + j % 2)
            ).start()
            return carry

        @pl.when(from_bead == py // 2)
        def _():
            pltpu.make_async_copy(source(2 * px + py % 2), slots_ref.at[mark], own_sem).start()

        @pl.when(jnp.logical_not(from_bead == py // 2))
        def _():
            send(0, 0)

        lax.fori_loop(1, 16, send, 0)

    deliver(lambda j: payload.at[pl.ds(pl.multiple_of(bead * 128 + j * 8, 8), 8)], bead)
    for copy in springs:
        copy.start()
    for step, copy in zip((1, 3, 2), staged):
        copy.wait_recv()
        other = lax.rem(bead + 4 - step, 4)
        deliver(lambda j: stage.at[other, pl.ds(pl.multiple_of(j * 8, 8), 8)], other)
    chosen_ref[...] = jnp.where(targets(owner_ref[...], True), 1.0, 0.0).astype(bf16)
    for copy in springs:
        copy.wait()
    for axis in range(3):
        bend = 2.0 * frac_ref[axis] - before_ref[axis] - after_ref[axis]
        spring_ref[axis] = -spring_scale * bend
    settle(slots_ref.at[mark], own_sem)
    rest = pl.ds(0, 8 * OWN - 8)
    settle(slots_ref.at[rest], recv_sem)
    settle(slots_ref.at[rest], send_sem)
    for copy in staged:
        copy.wait_send()


def atoms_to_slots(owner_row, tile_row, cell, frac, charge, zone):
    dma = pltpu.SemaphoreType.DMA
    return pl.pallas_call(
        atoms_kernel,
        out_shape=[
            jax.ShapeDtypeStruct((8 * OWN, 128), f32),
            jax.ShapeDtypeStruct((3, OWN, 128), f32),
            jax.ShapeDtypeStruct((2 * OWN, OWN), bf16),
        ],
        in_specs=[pl.BlockSpec(memory_space=HBM)] * 6,
        out_specs=vmem(3),
        scratch_shapes=[
            VMEM((1, OWN), jnp.int32), VMEM((1, OWN), jnp.int32), VMEM((OWN, 128), jnp.int32),
            VMEM((3, OWN, 128), f32), VMEM((OWN, 128), f32), VMEM((OWN, 128), jnp.int32),
            VMEM((8 * OWN, 128), f32), VMEM((4, 128, 128), f32),
            VMEM((3, OWN, 128), f32), VMEM((3, OWN, 128), f32),
            dma((3,)), dma((3,)), dma, dma, dma, dma((2,)), dma((2,)), dma((6,)),
        ],
        compiler_params=pltpu.CompilerParams(
            collective_id=0, has_side_effects=True, vmem_limit_bytes=60 << 20
        ),
        name="atoms_to_slots",
    )(owner_row, tile_row, cell, frac, charge, zone)


def tile_codes(slots_ref):
    along_x = slots_ref[pl.ds(1, 2 * OWN, stride=4), :]
    along_z = slots_ref[pl.ds(3, 2 * OWN, stride=4), :]
    tile_x = (jnp.max(along_x, 1, keepdims=True) * 0.125).astype(jnp.int32)
    tile_z = (jnp.max(along_z, 1, keepdims=True) * 0.125).astype(jnp.int32)
    up = lax.broadcasted_iota(jnp.int32, (128, 128), 0)
    across = lax.broadcasted_iota(jnp.int32, (128, 128), 1)
    sub = lax.broadcasted_iota(jnp.int32, (8, 128), 0)
    value = jnp.zeros((8, 128), f32)
    columns = (256 * tile_x + tile_z, 8 * tile_x, 8 * tile_z)
    for place_in, column in enumerate(columns):
        row = jnp.sum(jnp.where(up == across, column.astype(f32), 0.0), 0, keepdims=True)
        value = jnp.where(sub == place_in, row, value)
    return value.astype(jnp.int32)


def spread_kernel(slots_ref, out_hbm, codes_scalar, density, codes, out_ref, sem, out_sem):
    codes[...] = tile_codes(slots_ref)
    copy = pltpu.make_async_copy(codes, codes_scalar, sem)
    copy.start()
    density[...] = jnp.zeros_like(density)
    copy.wait()
    rows16 = lax.broadcasted_iota(jnp.int32, (16, 128), 0).astype(f32) - 1.0
    rows40 = lax.broadcasted_iota(jnp.int32, (40, 128), 0).astype(f32) - 1.0

    def one(number, slot):
        plane_x, row_z = codes_scalar[1, number], codes_scalar[2, number]
        charge, at_x, at_y, at_z = [slot[i : i + 1] for i in range(4)]
        at_x = at_x - plane_x.astype(f32)
        at_z = at_z - row_z.astype(f32)
        weight_x = bspline(rows16 - at_x, False) * charge
        weight_z = bspline(rows16 - at_z, False)
        weight_y = jnp.concatenate([bspline(rows40 - at_y, False), jnp.zeros((24, 128), f32)], 0)
        plane = jnp.concatenate([weight_x[i : i + 1] * weight_z for i in range(11)], 0)
        plane = jnp.concatenate(split(plane), 1)
        y_high, y_low = split(weight_y)
        left = jnp.concatenate([y_high, y_low], 0)
        right = jnp.concatenate([y_high, jnp.zeros((64, 128), bf16)], 0)
        both = jnp.concatenate([left, right], 1)
        out = lax.dot_general(plane, both, (((1,), (1,)), ((), ())), preferred_element_type=f32)
        return plane_x, row_z, out

    def put(plane_x, row_z, out):
        base = pl.multiple_of(row_z, 8)
        for i in range(11):
            density[plane_x + i, pl.ds(base, 16), :] += out[16 * i : 16 * i + 16]

    def step(index, carry):
        found = []
        for k in range(8):
            pair = slots_ref[pl.ds(pl.multiple_of(64 * index + 8 * k, 8), 8), :]
            for rank in range(2):
                found.append(one(16 * index + 2 * k + rank, pair[4 * rank : 4 * rank + 4]))
        for item in found:
            put(*item)
        return carry

    lax.fori_loop(0, 8, step, 0)

    lane = lane_of(2)
    low = lane < 64
    even = (lane // 32) % 2 == 0

    def fold(plane, carry):
        density[plane, 0:8, :] += density[plane, 256:264, :]
        return carry

    lax.fori_loop(0, 36, fold, 0)

    def regroup(chunk, carry):
        here = pl.ds(pl.multiple_of(chunk * 32, 32), 32)
        rim = jnp.zeros((32, 128), f32)

        def keep(group, value):
            out_ref[group, here, :] = value

        for group in range(9):
            four = [density[4 * group + i, here, :] for i in range(4)]
            pair_even = jnp.where(low, four[0], four[2]) + turn(jnp.where(low, four[2], four[0]), 64)
            pair_odd = jnp.where(low, four[1], four[3]) + turn(jnp.where(low, four[3], four[1]), 64)
            pair_odd = turn(pair_odd, 32)
            main = jnp.where(even, pair_even, pair_odd)
            side = jnp.where(even, pair_odd, pair_even)
            if group < 8:
                keep(group, main)
                rim = rim + turn(side, 4 * group)
            else:
                last = lane >= 96
                corner = jnp.where((lane >= 96) & (lane < 100), turn(side, 64), 0.0)
                corner = jnp.where((lane >= 100) & (lane < 104), turn(side, 36), corner)
                corner = jnp.where((lane >= 104) & (lane < 108), turn(side, 8), corner)
                keep(8, jnp.where(last, corner, main))
        keep(9, rim)
        pltpu.make_async_copy(out_ref.at[:, here, :], out_hbm.at[:, here, :], out_sem.at[chunk]).start()
        return carry

    lax.fori_loop(0, 8, regroup, 0)
    for chunk in range(8):
        here = pl.ds(32 * chunk, 32)
        pltpu.make_async_copy(out_ref.at[:, here, :], out_hbm.at[:, here, :], out_sem.at[chunk]).wait()


def spread(slots):
    return pl.pallas_call(
        spread_kernel,
        out_shape=[
            jax.ShapeDtypeStruct((10, 256, 128), f32),
            jax.ShapeDtypeStruct((8, 128), jnp.int32),
        ],
        in_specs=vmem(1),
        out_specs=[pl.BlockSpec(memory_space=pl.ANY), pl.BlockSpec(memory_space=SMEM)],
        scratch_shapes=[
            VMEM((36, 264, 128), f32),
            VMEM((8, 128), jnp.int32),
            VMEM((10, 256, 128), f32),
            pltpu.SemaphoreType.DMA,
            pltpu.SemaphoreType.DMA((8,)),
        ],
        compiler_params=pltpu.CompilerParams(vmem_limit_bytes=60 << 20),
        name="spread",
    )(slots)


TABLES = ("forward_z", "forward_y", "forward_x", "back_x", "fold_y", "back_z")
ROWS_OF = (0, 8, 24, 32)
RIMS_OF = (16, 17, 20, 21)


def here():
    return lax.axis_index("bead"), lax.axis_index("px"), lax.axis_index("py")


def place(number, bead):
    return (number // 16, (number // 2) % 8, 2 * bead + number % 2)


def hop(step):
    return lax.rem(step * 37, OWN)


def shifted(value, steps):
    if steps == 1:
        return jnp.concatenate([value[7:8], value[0:7]], 0)
    return jnp.concatenate([value[1:8], value[0:1]], 0)


def wave_kernel(
    codes, *rest,
):
    table_refs, rest = rest[:17], rest[17:]
    out_ref, rest = rest[0], rest[1:]
    table_vmem, rest = rest[:17], rest[17:]
    packed, fz_high, fz_low = table_vmem[:3]
    row_ref, slots_ref, spring_ref, chosen_ref = table_vmem[13:]
    (
        lines, waves_in, waves_out, lines_in, plane, plane_rim,
        lines_z, last, field, force, force_in, table_sem, out_send, out_recv, back_send, back_recv,
        own_sem, force_send, force_recv, blocks_sem,
    ) = rest
    (fz, fy, fx, bx, fold, bz) = [(table_vmem[2 * i + 1], table_vmem[2 * i + 2]) for i in range(6)]
    bead, px, py = here()
    mine, grid_bead, chunk = bead * 16 + px * 2 + py % 2, py // 2, px * 8 + py
    same = bead == grid_bead
    barrier = pltpu.get_barrier_semaphore()

    table_copies = [
        pltpu.make_async_copy(table_refs[i], table_vmem[i], table_sem.at[i]) for i in range(17)
    ]
    for copy in table_copies[:3]:
        copy.start()

    def greet(step, carry):
        other = lax.rem(mine + hop(step), OWN)
        pl.semaphore_signal(barrier, inc=1, device_id=place(other, grid_bead), device_id_type=MESH)
        return carry

    lax.fori_loop(1, OWN, greet, 0)
    likes = [(bead, px, lax.rem(py + 2 * k, 8)) for k in range(1, 4)]
    for like in likes:
        pl.semaphore_signal(barrier, inc=1, device_id=like, device_id_type=MESH)

    for copy in table_copies[3:]:
        copy.start()
    for copy in table_copies[:3]:
        copy.wait()

    for pair in range(5):
        high, low = split(jnp.concatenate([packed[2 * pair], packed[2 * pair + 1]], 1))
        result = dots(fz[0][...], fz[1][...], high, low)
        for part in range(2):
            group = 2 * pair + part
            for c in range(4):
                start = ROWS_OF[c] + group if group < 8 else RIMS_OF[c] + 2 * (group - 8)
                lines[:, start, :] = result[64 * c : 64 * c + 64, 128 * part : 128 * part + 128]

    pl.semaphore_wait(barrier, OWN - 1 + 3)

    def own(src, dst, rows, sem):
        return pltpu.make_async_copy(src.at[mine, rows], dst.at[mine, rows], sem)

    def send_all(src, dst, rows, send_sem, recv_sem):
        def send(step, carry):
            other = lax.rem(mine + hop(step), OWN)
            remote(
                src.at[other, rows], dst.at[mine, rows], send_sem, recv_sem, place(other, grid_bead)
            ).start()
            return carry

        lax.fori_loop(1, OWN, send, 0)

    rest = pl.ds(0, OWN - 1)
    half_rows = (pl.ds(0, 20), pl.ds(20, 20))
    for n in range(2):
        own(lines, waves_in, half_rows[n], own_sem.at[n]).start()
        send_all(lines, waves_in, half_rows[n], out_send.at[n], out_recv.at[n])

    for like in likes:
        pl.semaphore_signal(blocks_sem, inc=1, device_id=like, device_id_type=MESH)
    for copy in table_copies[3:]:
        copy.wait()

    lane = lane_of(3)
    sub = lax.broadcasted_iota(jnp.int32, (1, 8, 128), 1)
    lane_group = (lane // 4) % 8
    square_y, factor_y = row_ref[0:1, :], row_ref[1:2, :]
    up = lax.broadcasted_iota(jnp.int32, (256, 256), 0)
    across = lax.broadcasted_iota(jnp.int32, (256, 256), 1)
    square_x = jnp.sum(jnp.where(up == across, square_y, 0.0), 1, keepdims=True)
    factor_x = jnp.sum(jnp.where(up == across, factor_y, 0.0), 1, keepdims=True)
    mine_z = lax.broadcasted_iota(jnp.int32, (1, 256), 1) - 2 * mine

    for n in range(2):
        own(lines, waves_in, half_rows[n], own_sem.at[n]).wait()
        settle(waves_in.at[rest, half_rows[n]], out_recv.at[n])
        for q in range(2):
            padding = jnp.zeros((8, 4, 128), f32)
            extra = blocks_exchanged(
                [
                    jnp.concatenate(
                        [waves_in[pl.ds(4 * q + j, 8, stride=8), 16 + 4 * n : 20 + 4 * n, :], padding], 1
                    )
                    for j in range(4)
                ]
            )
            for half in range(2):
                c = 2 * n + half
                main = blocks_exchanged(
                    [
                        waves_in[pl.ds(4 * q + j, 8, stride=8), ROWS_OF[c] : ROWS_OF[c] + 8, :]
                        for j in range(4)
                    ]
                )
                for i in range(4):
                    value = main[i]
                    rim = jnp.where(lane_group == sub, extra[(i + 1) % 4][:, 2 + half : 3 + half, :], 0.0)
                    if i < 3:
                        value = value + jnp.where(sub == 0, shifted(extra[i][:, half : half + 1, :], 1), 0.0)
                        corner = shifted(extra[3][:, half : half + 1, :], 1)
                        rim = rim + jnp.where((sub == 0) & (lane_group == i), corner, 0.0)
                    lines_of = slice(64 * i, 64 * i + 64)
                    plane[half, lines_of, 128 * q : 128 * q + 128] = value.reshape(64, 128)
                    high, low = split(rim.reshape(64, 128))
                    plane_rim[half, lines_of, 128 * q : 128 * q + 128] = high
                    plane_rim[half, lines_of, 256 + 128 * q : 384 + 128 * q] = low

        real, imag = [
            dots(*split(plane[half] + product(plane_rim[half], fold[0][...])), fy[0][...], fy[1][...])
            for half in range(2)
        ]
        spec = jnp.concatenate(
            [real[:, :256] + imag[:, 256:], imag[:, :256] - real[:, 256:]], 1
        )
        both = dots(fx[0][...], fx[1][...], *split(spec))
        square_z = jnp.sum(jnp.where(mine_z == n, square_y, 0.0), 1, keepdims=True)
        factor_z = jnp.sum(jnp.where(mine_z == n, factor_y, 0.0), 1, keepdims=True)
        square = square_x + square_y + square_z
        green = factor_x * factor_y * (factor_z * (4.0 * math.pi))
        green = jnp.where(square > 0.0, green / jnp.where(square > 0.0, square, 1.0), 0.0)
        spec = jnp.concatenate(
            [
                (both[:256, :256] + both[256:, 256:]) * green,
                (both[:256, 256:] - both[256:, :256]) * green,
            ],
            1,
        )
        both = dots(bx[0][...], bx[1][...], *split(spec))
        spec = jnp.concatenate(
            [both[:256, :256] - both[256:, 256:], both[:256, 256:] + both[256:, :256]], 0
        )
        both = dots(*split(spec), fy[0][...], fy[1][...])
        back = [both[:256, :256] - both[256:, 256:], both[256:, :256] + both[:256, 256:]]
        back_rim = [product(jnp.concatenate(split(value), 1), fold[1][...]) for value in back]

        for q in range(2):
            extra = [jnp.zeros((8, 8, 128), f32) for _ in range(4)]
            for half in range(2):
                c = 2 * n + half
                main, corner = [], jnp.zeros((8, 1, 128), f32)
                for i in range(4):
                    lines_of = slice(64 * i, 64 * i + 64)
                    value = back[half][lines_of, 128 * q : 128 * q + 128].reshape(8, 8, 128)
                    rim = back_rim[half][lines_of, 128 * q : 128 * q + 128].reshape(8, 8, 128)
                    main.append(value)
                    if i < 3:
                        extra[i] = jnp.where(sub == half, shifted(value[:, 0:1, :], -1), extra[i])
                        corner = jnp.where(lane_group == i, shifted(rim[:, 0:1, :], -1), corner)
                    side = jnp.sum(jnp.where(lane_group == sub, rim, 0.0), 1, keepdims=True)
                    extra[(i + 1) % 4] = jnp.where(sub == 2 + half, side, extra[(i + 1) % 4])
                extra[3] = jnp.where(sub == half, corner, extra[3])
                main = blocks_exchanged(main)
                for j in range(4):
                    waves_out[pl.ds(4 * q + j, 8, stride=8), ROWS_OF[c] : ROWS_OF[c] + 8, :] = main[j]
            extra = blocks_exchanged(extra)
            for j in range(4):
                waves_out[pl.ds(4 * q + j, 8, stride=8), 16 + 4 * n : 20 + 4 * n, :] = extra[j][:, 0:4, :]
        own(waves_out, lines_in, half_rows[n], own_sem.at[2 + n]).start()
        send_all(waves_out, lines_in, half_rows[n], back_send.at[n], back_recv.at[n])

    for n in range(2):
        own(waves_out, lines_in, half_rows[n], own_sem.at[2 + n]).wait()
        settle(lines_in.at[rest, half_rows[n]], back_recv.at[n])

    for pair in range(5):
        columns = []
        for group in (2 * pair, 2 * pair + 1):
            starts = [
                ROWS_OF[c] + group if group < 8 else RIMS_OF[c] + 2 * (group - 8) for c in range(4)
            ]
            columns.append(jnp.concatenate([lines_in[:, start, :] for start in starts], 0))
        result = dots(bz[0][...], bz[1][...], *split(jnp.concatenate(columns, 1)))
        for part in range(2):
            lines_z[2 * pair + part, 0:256, :] = result[:, 128 * part : 128 * part + 128]
            lines_z[2 * pair + part, 256:264, :] = result[0:8, 128 * part : 128 * part + 128]

    lane = lane_of(2)
    low_half = lane < 64
    even = (lane // 32) % 2 == 0

    def regroup(part, rows):
        at = pl.ds(pl.multiple_of(part * 32, 32), rows)
        rim = lines_z[9, at, :]
        for group in range(9):
            main = lines_z[group, at, :]
            if group < 8:
                side = turn(rim, -4 * group)
            else:
                side = jnp.where(
                    lane < 64, turn(main, -64), jnp.where(lane < 96, turn(main, -36), turn(main, -8))
                )
            pair_even = jnp.where(even, main, side)
            pair_odd = turn(jnp.where(even, side, main), -32)
            for odd, value in enumerate((pair_even, pair_odd)):
                other = turn(value, 64)
                high = value.astype(bf16).astype(f32)
                high_other = other.astype(bf16).astype(f32)
                planes = (
                    jnp.where(low_half, high, other - high_other),
                    jnp.where(low_half, high_other, value - high),
                )
                for second in range(2):
                    plane_x = 4 * group + 2 * second + odd
                    whole = jnp.concatenate([last[plane_x], planes[second]], 0)
                    for k in range(rows // 8):
                        window = whole[8 * k : 8 * k + 16].astype(bf16)
                        field[plane_x * 32 + 4 * part + k] = window
                    last[plane_x] = planes[second][rows - 8 : rows]

    def regroup_step(part, carry):
        regroup(part, 32)
        return carry

    last[...] = jnp.zeros_like(last)
    lax.fori_loop(0, 8, regroup_step, 0)
    regroup(8, 8)

    rows16 = lax.broadcasted_iota(jnp.int32, (16, 128), 0).astype(f32) - 1.0
    rows40 = lax.broadcasted_iota(jnp.int32, (40, 128), 0).astype(f32) - 1.0
    nothing = jnp.zeros((24, 256), f32)

    def one(number, slot):
        charge, at_x, at_y, at_z = [slot[i : i + 1] for i in range(4)]
        at_x = at_x - codes[1, number].astype(f32)
        at_z = at_z - codes[2, number].astype(f32)
        weight_x, slope_x = bspline(rows16 - at_x, True)
        weight_z, slope_z = bspline(rows16 - at_z, True)
        along_y = jnp.concatenate(bspline(rows40 - at_y, True), 1)
        y_high, y_low = split(jnp.concatenate([along_y, nothing], 0))
        both = jnp.concatenate([y_high, y_high, y_low, y_low], 0)
        base = codes[0, number]
        window = jnp.concatenate([field[base + 32 * i + 1] for i in range(11)], 0)
        out = jnp.dot(jnp.concatenate([window, window], 1), both, preferred_element_type=f32)
        plain = jnp.zeros((16, 128), f32)
        along_x = jnp.zeros((16, 128), f32)
        sloped = jnp.zeros((16, 128), f32)
        for i in range(11):
            value = out[16 * i : 16 * i + 16, :128]
            slope = out[16 * i : 16 * i + 16, 128:]
            plain = plain + weight_x[i : i + 1] * value
            along_x = along_x + slope_x[i : i + 1] * value
            sloped = sloped + weight_x[i : i + 1] * slope
        minus = -charge
        return jnp.concatenate(
            [
                minus * jnp.sum(along_x * weight_z, 0, keepdims=True),
                minus * jnp.sum(sloped * weight_z, 0, keepdims=True),
                minus * jnp.sum(plain * slope_z, 0, keepdims=True),
                charge,
            ],
            0,
        )

    def interpolate(step):
        sources = [lax.rem(chunk + hop(4 * step + k), OWN) for k in range(4)]
        found = []
        for source in sources:
            pair = slots_ref[pl.ds(pl.multiple_of(8 * source, 8), 8), :]
            found.append(
                jnp.concatenate([one(2 * source, pair[0:4]), one(2 * source + 1, pair[4:8])], 0)
            )
        for source, value in zip(sources, found):
            force[source] = value
        return sources

    def send_force(source):
        remote(
            force.at[source], force_in.at[mine], force_send, force_recv,
            (grid_bead, source // 8, source % 8),
        ).start()

    pl.semaphore_wait(blocks_sem, 3)
    sources = interpolate(0)

    @pl.when(same)
    def _():
        pltpu.make_async_copy(force.at[chunk], force_in.at[mine], own_sem.at[4]).start()

    @pl.when(jnp.logical_not(same))
    def _():
        send_force(chunk)

    for source in sources[1:]:
        send_force(source)

    def interpolate_step(step, carry):
        for source in interpolate(step):
            send_force(source)
        return carry

    lax.fori_loop(1, OWN // 4, interpolate_step, 0)

    chosen = chosen_ref[...]

    @pl.when(same)
    def _():
        settle(force_in.at[mine], own_sem.at[4])
        settle(force_in.at[rest], force_recv)
        settle(force_in.at[rest], force_send)

    @pl.when(jnp.logical_not(same))
    def _():
        settle(force_in, force_recv)
        settle(force_in, force_send)

    for axis in range(3):
        both = jnp.concatenate([force_in[:, axis, :], force_in[:, 4 + axis, :]], 0)
        moved = sum(
            lax.dot_general(chosen, part, (((0,), (0,)), ((), ())), preferred_element_type=f32)
            for part in reversed(three(both))
        )
        out_ref[axis] = moved + spring_ref[axis]

    for n in range(2):
        settle(lines.at[rest, half_rows[n]], out_send.at[n])
        settle(waves_out.at[rest, half_rows[n]], back_send.at[n])


def grid_to_forces(codes, packed, slots, spring, chosen):
    table = tables()
    consts = [packed] + [jnp.asarray(half) for name in TABLES for half in table[name]]
    consts += [jnp.asarray(table["row"]), slots, spring, chosen]
    dma = pltpu.SemaphoreType.DMA
    chunks = VMEM((OWN, 40, 128), f32)
    return pl.pallas_call(
        wave_kernel,
        out_shape=jax.ShapeDtypeStruct((3, OWN, 128), f32),
        in_specs=[pl.BlockSpec(memory_space=SMEM)] + [pl.BlockSpec(memory_space=HBM)] * 17,
        out_specs=pl.BlockSpec(memory_space=VMEM),
        scratch_shapes=[VMEM(const.shape, const.dtype) for const in consts]
        + [
            chunks, chunks, chunks, chunks,
            VMEM((2, 256, 256), f32), VMEM((2, 256, 512), bf16),
            VMEM((10, 264, 128), f32), VMEM((36, 8, 128), f32), VMEM((36 * 32 + 1, 16, 128), bf16),
            VMEM((OWN, 8, 128), f32), VMEM((OWN, 8, 128), f32),
            dma((17,)), dma((2,)), dma((2,)), dma((2,)), dma((2,)), dma((5,)), dma, dma,
            pltpu.SemaphoreType.REGULAR,
        ],
        compiler_params=pltpu.CompilerParams(
            collective_id=1, has_side_effects=True, vmem_limit_bytes=60 << 20
        ),
        name="grid_to_forces",
    )(
        codes, *consts,
    )


def local(block_owner, block_tile, atom_cell, atom_frac, charge, zone):
    owner_row = block_owner.reshape(1, OWN)
    frac = jnp.transpose(atom_frac[0], (1, 0, 2))
    slots, spring, chosen = atoms_to_slots(
        owner_row, block_tile.reshape(1, OWN), atom_cell, frac, charge, zone
    )
    packed, codes = spread(slots)
    total = grid_to_forces(codes, packed, slots, spring, chosen)
    return jnp.transpose(total, (1, 0, 2))[None]


def solution(mesh):
    return jax.shard_map(
        local,
        mesh=mesh,
        in_specs=(
            P(("px", "py"), None),
            P(("px", "py")),
            P(("px", "py"), None),
            P("bead", ("px", "py"), None, None),
            P(("px", "py"), None),
            P(("px", "py"), None),
        ),
        out_specs=P("bead", ("px", "py"), None, None),
        check_vma=False,
    )
```

```python
import functools
import math

import jax
import jax.numpy as jnp
import ml_dtypes
import numpy as np
from jax import lax
from jax.experimental import pallas as pl
from jax.experimental.pallas import tpu as pltpu
from jax.sharding import PartitionSpec as P

NG = 256
OWN = 64
f32 = jnp.float32
bf16 = jnp.bfloat16
MESH = pl.DeviceIdType.MESH
VMEM = pltpu.VMEM
SMEM = pltpu.SMEM
HBM = pltpu.HBM
ewald_beta = 0.75
spring_scale = 0.25


def halves(table):
    table = table.astype(np.float32)
    high = table.astype(ml_dtypes.bfloat16)
    low = (table - high.astype(np.float32)).astype(ml_dtypes.bfloat16)
    return high, low


def waves(rows, columns):
    angle = (np.outer(rows, columns) % NG) * (2.0 * math.pi / NG)
    return np.cos(angle), np.sin(angle)


@functools.lru_cache(None)
def tables():
    whole = np.arange(NG)
    owner = np.arange(OWN)
    kz = np.stack([2 * owner, 2 * owner + 1])
    cos_z, sin_z = waves(kz.reshape(-1), whole)
    forward_z = np.concatenate([cos_z[:OWN], -sin_z[:OWN], cos_z[OWN:], -sin_z[OWN:]])
    scale = np.where(kz == 0, 1.0, 2.0) / float(NG**3)
    scale = np.repeat(scale, 2, 0).reshape(-1)
    back_z = (forward_z * scale[:, None]).T
    forward_y = np.concatenate(waves(whole, whole), 1)
    rim = (32 * (whole // 32 + 1) + whole % 4) % NG
    fold_y = np.concatenate([rim[:, None] == whole[None, :]] * 2).astype(ml_dtypes.bfloat16)
    unfold_y = np.concatenate([whole[:, None] == rim[None, :]] * 2).astype(ml_dtypes.bfloat16)
    step, block, group = np.meshgrid(np.arange(4), np.arange(8), np.arange(8), indexing="ij")
    place = (32 * block + 4 * group + step).reshape(-1)
    cos_x, sin_x = waves(whole, place)
    forward_x = np.concatenate([cos_x, sin_x])
    back_x = np.concatenate([cos_x.T, sin_x.T])
    wave = (whole + NG // 2) % NG - NG // 2
    theta = wave * (2.0 * math.pi / NG)
    factor = (6.0 / (4.0 + 2.0 * np.cos(theta))) ** 2
    factor = factor * np.exp(-theta * theta / (4.0 * ewald_beta * ewald_beta))
    row = np.zeros((8, 256), np.float32)
    row[0], row[1] = theta * theta, factor
    return dict(
        forward_z=halves(forward_z),
        back_z=halves(back_z),
        forward_y=halves(forward_y),
        fold_y=(fold_y, unfold_y),
        forward_x=halves(forward_x),
        back_x=halves(back_x),
        row=row,
    )


def split(value):
    high = value.astype(bf16)
    return high, (value - high.astype(f32)).astype(bf16)


product = functools.partial(jnp.dot, preferred_element_type=f32)


def dots(a_high, a_low, b_high, b_low):
    return product(a_high, b_high) + (product(a_high, b_low) + product(a_low, b_high))


def lane_of(rank):
    return lax.broadcasted_iota(jnp.int32, (1,) * (rank - 1) + (128,), rank - 1)


def turn(value, steps):
    steps = steps % 128
    if steps == 0:
        return value
    flat = value.reshape(-1, 128)
    return pltpu.roll(flat, steps, 1).reshape(value.shape)


def blocks_exchanged(parts):
    lane = lane_of(parts[0].ndim)
    low = lane < 64
    even = (lane // 32) % 2 == 0
    first = [
        jnp.where(low, parts[0], turn(parts[2], 64)),
        jnp.where(low, parts[1], turn(parts[3], 64)),
        jnp.where(low, turn(parts[0], 64), parts[2]),
        jnp.where(low, turn(parts[1], 64), parts[3]),
    ]
    return [
        jnp.where(even, first[0], turn(first[1], 32)),
        jnp.where(even, turn(first[0], 96), first[1]),
        jnp.where(even, first[2], turn(first[3], 32)),
        jnp.where(even, turn(first[2], 96), first[3]),
    ]


def bspline(offsets, slopes):
    v = jnp.abs(offsets)
    a = jnp.maximum(2.0 - v, 0.0)
    b = jnp.maximum(1.0 - v, 0.0)
    aa = a * a
    bb = b * b
    weight = aa * a * (1.0 / 6.0) - bb * b * (4.0 / 6.0)
    if not slopes:
        return weight
    half = 0.5 * aa - 2.0 * bb
    return weight, jnp.where(offsets < 0.0, -half, half)


def vmem(count):
    return [pl.BlockSpec(memory_space=VMEM)] * count


def targets(owner_row, apart):
    blocks = owner_row.shape[1]
    up = lax.broadcasted_iota(jnp.int32, (blocks, blocks), 0)
    across = lax.broadcasted_iota(jnp.int32, (blocks, blocks), 1)
    owner_column = jnp.sum(jnp.where(up == across, owner_row, 0).astype(f32), 1, keepdims=True)
    owner_float = owner_row.astype(f32)
    before = jnp.where((owner_column == owner_float) & (up < across), 1.0, 0.0)
    rank = jnp.sum(before, 0, keepdims=True)
    target = owner_float + OWN * rank if apart else 2.0 * owner_float + rank
    slot = lax.broadcasted_iota(jnp.int32, (2 * OWN, blocks), 0).astype(f32)
    return slot == target


def three(value):
    high = value.astype(bf16)
    rest = value - high.astype(f32)
    middle = rest.astype(bf16)
    return high, middle, (rest - middle.astype(f32)).astype(bf16)


def remote(src, dst, send_sem, recv_sem, device):
    return pltpu.make_async_remote_copy(
        src_ref=src, dst_ref=dst, send_sem=send_sem, recv_sem=recv_sem,
        device_id=device, device_id_type=MESH,
    )


def settle(ref, sem):
    pltpu.make_async_copy(ref, ref, sem).wait()


def atoms_kernel(
    owner_hbm, tile_hbm, cell_hbm, frac_hbm, charge_hbm, zone_hbm, slots_ref,
    owner_ref, tile_ref, cell_ref, frac_ref, charge_ref, zone_ref,
    payload, stage, stage_send, stage_recv, send_sem, recv_sem, own_sem, in_sem, lines_sem,
):
    loads = [
        pltpu.make_async_copy(src, dst, in_sem.at[i])
        for i, (src, dst) in enumerate(
            (
                (owner_hbm, owner_ref), (tile_hbm, tile_ref), (cell_hbm, cell_ref),
                (frac_hbm, frac_ref), (charge_hbm, charge_ref), (zone_hbm, zone_ref),
            )
        )
    ]
    for copy in loads:
        copy.start()
    bead, px, py = here()
    chunk = px * 8 + py
    barrier = pltpu.get_barrier_semaphore()

    crossing = [(bead, lax.rem(px + step, 8), py) for step in range(1, 8)]
    greeted = crossing + [(bead, px, lax.rem(py + step, 8)) for step in range(1, 8)]
    greeted += [(lax.rem(bead + step, 4), px, py) for step in range(1, 4)]
    for device in greeted:
        pl.semaphore_signal(barrier, inc=1, device_id=device, device_id_type=MESH)

    for copy in loads:
        copy.wait()
    chosen = jnp.where(targets(owner_ref[...], False), 1.0, 0.0).astype(bf16)
    blocks = cell_ref.shape[0]
    up = lax.broadcasted_iota(jnp.int32, (blocks, blocks), 0)
    across = lax.broadcasted_iota(jnp.int32, (blocks, blocks), 1)
    tile = jnp.sum(jnp.where(up == across, tile_ref[...], 0).astype(f32), 1, keepdims=True)
    tile = tile.astype(jnp.int32)
    cell = cell_ref[...]
    corners = [tile >> 7, (tile >> 5) & 3, tile & 31]
    cells = [cell >> 6, (cell >> 3) & 7, cell & 7]
    fields = [charge_ref[...] * zone_ref[...].astype(f32)]
    for axis in range(3):
        base = (corners[axis] * 8).astype(f32)
        inside = cells[axis].astype(f32) + frac_ref[axis]
        fields.append(base + jnp.minimum(inside, 8.0 - 2.0**-16))
    pl.semaphore_wait(barrier, 17)
    for device in crossing:
        pl.semaphore_signal(lines_sem, inc=1, device_id=device, device_id_type=MESH)
    for place_in, field in enumerate(fields):
        parts = three(field)
        moved = sum(
            jnp.dot(chosen, part, preferred_element_type=f32) for part in reversed(parts)
        )
        payload[pl.ds(place_in, 2 * OWN, stride=4), :] = moved

    staged = [
        remote(
            payload.at[pl.ds(pl.multiple_of(lax.rem(bead + step, 4) * 128, 128), 128)], stage.at[bead],
            stage_send.at[step - 1], stage_recv.at[step - 1], (lax.rem(bead + step, 4), px, py),
        )
        for step in (1, 3, 2)
    ]
    for copy in staged:
        copy.start()
    mark = pl.ds(pl.multiple_of(chunk * 8, 8), 8)
    pl.semaphore_wait(lines_sem, 7)

    def deliver(source, from_bead):
        def send(step, carry):
            j = lax.rem(step + 2 * px + py % 2, 16)
            remote(
                source(j), slots_ref.at[mark], send_sem, recv_sem, (bead, j // 2, 2 * from_bead + j % 2)
            ).start()
            return carry

        @pl.when(from_bead == py // 2)
        def _():
            pltpu.make_async_copy(source(2 * px + py % 2), slots_ref.at[mark], own_sem).start()

        @pl.when(jnp.logical_not(from_bead == py // 2))
        def _():
            send(0, 0)

        lax.fori_loop(1, 16, send, 0)

    deliver(lambda j: payload.at[pl.ds(pl.multiple_of(bead * 128 + j * 8, 8), 8)], bead)
    for step, copy in zip((1, 3, 2), staged):
        copy.wait_recv()
        other = lax.rem(bead + 4 - step, 4)
        deliver(lambda j: stage.at[other, pl.ds(pl.multiple_of(j * 8, 8), 8)], other)
    settle(slots_ref.at[mark], own_sem)
    rest = pl.ds(0, 8 * OWN - 8)
    settle(slots_ref.at[rest], recv_sem)
    settle(slots_ref.at[rest], send_sem)
    for copy in staged:
        copy.wait_send()


def atoms_to_slots(owner_row, tile_row, cell, frac, charge, zone):
    dma = pltpu.SemaphoreType.DMA
    return pl.pallas_call(
        atoms_kernel,
        out_shape=jax.ShapeDtypeStruct((8 * OWN, 128), f32),
        in_specs=[pl.BlockSpec(memory_space=HBM)] * 6,
        out_specs=pl.BlockSpec(memory_space=pl.ANY),
        scratch_shapes=[
            VMEM((1, OWN), jnp.int32), VMEM((1, OWN), jnp.int32), VMEM((OWN, 128), jnp.int32),
            VMEM((3, OWN, 128), f32), VMEM((OWN, 128), f32), VMEM((OWN, 128), jnp.int32),
            VMEM((8 * OWN, 128), f32), VMEM((4, 128, 128), f32),
            dma((3,)), dma((3,)), dma, dma, dma, dma((6,)), pltpu.SemaphoreType.REGULAR,
        ],
        compiler_params=pltpu.CompilerParams(
            collective_id=0, has_side_effects=True, vmem_limit_bytes=60 << 20
        ),
        name="atoms_to_slots",
    )(owner_row, tile_row, cell, frac, charge, zone)


def tile_codes(slots_ref):
    along_x = slots_ref[pl.ds(1, 2 * OWN, stride=4), :]
    along_z = slots_ref[pl.ds(3, 2 * OWN, stride=4), :]
    tile_x = (jnp.max(along_x, 1, keepdims=True) * 0.125).astype(jnp.int32)
    tile_z = (jnp.max(along_z, 1, keepdims=True) * 0.125).astype(jnp.int32)
    up = lax.broadcasted_iota(jnp.int32, (128, 128), 0)
    across = lax.broadcasted_iota(jnp.int32, (128, 128), 1)
    sub = lax.broadcasted_iota(jnp.int32, (8, 128), 0)
    value = jnp.zeros((8, 128), f32)
    columns = (256 * tile_x + tile_z, 8 * tile_x, 8 * tile_z)
    for place_in, column in enumerate(columns):
        row = jnp.sum(jnp.where(up == across, column.astype(f32), 0.0), 0, keepdims=True)
        value = jnp.where(sub == place_in, row, value)
    return value.astype(jnp.int32)


def spread_kernel(slots_ref, out_hbm, codes_hbm, codes_scalar, density, codes, out_ref, sem, out_sem):
    codes[...] = tile_codes(slots_ref)
    copy = pltpu.make_async_copy(codes, codes_scalar, sem.at[0])
    copy.start()
    handed = pltpu.make_async_copy(codes, codes_hbm, sem.at[1])
    handed.start()
    density[...] = jnp.zeros_like(density)
    copy.wait()
    rows16 = lax.broadcasted_iota(jnp.int32, (16, 128), 0).astype(f32) - 1.0
    rows40 = lax.broadcasted_iota(jnp.int32, (40, 128), 0).astype(f32) - 1.0

    def one(number, slot):
        plane_x, row_z = codes_scalar[1, number], codes_scalar[2, number]
        charge, at_x, at_y, at_z = [slot[i : i + 1] for i in range(4)]
        at_x = at_x - plane_x.astype(f32)
        at_z = at_z - row_z.astype(f32)
        weight_x = bspline(rows16 - at_x, False) * charge
        weight_z = bspline(rows16 - at_z, False)
        weight_y = jnp.concatenate([bspline(rows40 - at_y, False), jnp.zeros((24, 128), f32)], 0)
        plane = jnp.concatenate([weight_x[i : i + 1] * weight_z for i in range(11)], 0)
        plane = jnp.concatenate(split(plane), 1)
        y_high, y_low = split(weight_y)
        left = jnp.concatenate([y_high, y_low], 0)
        right = jnp.concatenate([y_high, jnp.zeros((64, 128), bf16)], 0)
        both = jnp.concatenate([left, right], 1)
        out = lax.dot_general(plane, both, (((1,), (1,)), ((), ())), preferred_element_type=f32)
        return plane_x, row_z, out

    def put(plane_x, row_z, out):
        base = pl.multiple_of(row_z, 8)
        for i in range(11):
            density[plane_x + i, pl.ds(base, 16), :] += out[16 * i : 16 * i + 16]

    def step(index, carry):
        found = []
        for k in range(8):
            pair = slots_ref[pl.ds(pl.multiple_of(64 * index + 8 * k, 8), 8), :]
            for rank in range(2):
                found.append(one(16 * index + 2 * k + rank, pair[4 * rank : 4 * rank + 4]))
        for item in found:
            put(*item)
        return carry

    lax.fori_loop(0, 8, step, 0)

    lane = lane_of(2)
    low = lane < 64
    even = (lane // 32) % 2 == 0

    def fold(plane, carry):
        density[plane, 0:8, :] += density[plane, 256:264, :]
        return carry

    lax.fori_loop(0, 36, fold, 0)

    def regroup(chunk, carry):
        here = pl.ds(pl.multiple_of(chunk * 32, 32), 32)
        rim = jnp.zeros((32, 128), f32)

        def keep(group, value):
            out_ref[group, here, :] = value

        for group in range(9):
            four = [density[4 * group + i, here, :] for i in range(4)]
            pair_even = jnp.where(low, four[0], four[2]) + turn(jnp.where(low, four[2], four[0]), 64)
            pair_odd = jnp.where(low, four[1], four[3]) + turn(jnp.where(low, four[3], four[1]), 64)
            pair_odd = turn(pair_odd, 32)
            main = jnp.where(even, pair_even, pair_odd)
            side = jnp.where(even, pair_odd, pair_even)
            if group < 8:
                keep(group, main)
                rim = rim + turn(side, 4 * group)
            else:
                last = lane >= 96
                corner = jnp.where((lane >= 96) & (lane < 100), turn(side, 64), 0.0)
                corner = jnp.where((lane >= 100) & (lane < 104), turn(side, 36), corner)
                corner = jnp.where((lane >= 104) & (lane < 108), turn(side, 8), corner)
                keep(8, jnp.where(last, corner, main))
        keep(9, rim)
        pltpu.make_async_copy(out_ref.at[:, here, :], out_hbm.at[:, here, :], out_sem.at[chunk]).start()
        return carry

    lax.fori_loop(0, 8, regroup, 0)
    handed.wait()
    for chunk in range(8):
        here = pl.ds(32 * chunk, 32)
        pltpu.make_async_copy(out_ref.at[:, here, :], out_hbm.at[:, here, :], out_sem.at[chunk]).wait()


def spread(slots):
    return pl.pallas_call(
        spread_kernel,
        out_shape=[
            jax.ShapeDtypeStruct((10, 256, 128), f32),
            jax.ShapeDtypeStruct((8, 128), jnp.int32),
        ],
        in_specs=vmem(1),
        out_specs=[pl.BlockSpec(memory_space=pl.ANY)] * 2,
        scratch_shapes=[
            SMEM((8, 128), jnp.int32),
            VMEM((36, 264, 128), f32),
            VMEM((8, 128), jnp.int32),
            VMEM((10, 256, 128), f32),
            pltpu.SemaphoreType.DMA((2,)),
            pltpu.SemaphoreType.DMA((8,)),
        ],
        compiler_params=pltpu.CompilerParams(vmem_limit_bytes=60 << 20),
        name="spread",
    )(slots)


TABLES = ("forward_z", "forward_y", "forward_x", "back_x", "fold_y", "back_z")
ROWS_OF = (0, 8, 24, 32)
RIMS_OF = (16, 17, 20, 21)


def here():
    return lax.axis_index("bead"), lax.axis_index("px"), lax.axis_index("py")


def place(number, bead):
    return (number // 16, (number // 2) % 8, 2 * bead + number % 2)


def hop(step):
    return lax.rem(step * 37, OWN)


def shifted(value, steps):
    if steps == 1:
        return jnp.concatenate([value[7:8], value[0:7]], 0)
    return jnp.concatenate([value[1:8], value[0:1]], 0)


def wave_kernel(
    codes_hbm, *rest,
):
    table_refs, rest = rest[:17], rest[17:]
    out_ref, rest = rest[0], rest[1:]
    table_vmem, rest = rest[:17], rest[17:]
    packed, fz_high, fz_low = table_vmem[:3]
    row_ref, slots_ref, frac_ref, owner_ref = table_vmem[13:]
    (
        lines, waves_in, waves_out, lines_in, plane, plane_rim,
        lines_z, last, field, force, force_in, table_sem, out_send, out_recv, back_send, back_recv,
        own_sem, force_send, force_recv, blocks_sem, before_ref, after_ref, bead_send, bead_recv,
        codes, codes_sem, lines_sem,
    ) = rest
    (fz, fy, fx, bx, fold, bz) = [(table_vmem[2 * i + 1], table_vmem[2 * i + 2]) for i in range(6)]
    bead, px, py = here()
    mine, grid_bead, chunk = bead * 16 + px * 2 + py % 2, py // 2, px * 8 + py
    same = bead == grid_bead
    barrier = pltpu.get_barrier_semaphore()

    table_copies = [
        pltpu.make_async_copy(table_refs[i], table_vmem[i], table_sem.at[i]) for i in range(17)
    ]
    for copy in table_copies[:3]:
        copy.start()

    crossing = [(bead, lax.rem(px + step, 8), py) for step in range(1, 8)]
    across = bead * 2 + py % 2
    along = [lax.rem(across + step, 8) for step in range(1, 8)]
    greeted = crossing + [(other // 2, px, 2 * grid_bead + other % 2) for other in along]
    likes = [(bead, px, lax.rem(py + 2 * k, 8)) for k in range(1, 4)]
    for device in greeted + likes:
        pl.semaphore_signal(barrier, inc=1, device_id=device, device_id_type=MESH)
    for copy in table_copies[3:]:
        copy.start()
    fetched = pltpu.make_async_copy(codes_hbm, codes, codes_sem)
    fetched.start()
    for copy in table_copies[:3]:
        copy.wait()
    pl.semaphore_wait(barrier, 17)
    for device in crossing:
        pl.semaphore_signal(lines_sem, inc=1, device_id=device, device_id_type=MESH)

    for pair in range(5):
        high, low = split(jnp.concatenate([packed[2 * pair], packed[2 * pair + 1]], 1))
        result = dots(fz[0][...], fz[1][...], high, low)
        for part in range(2):
            group = 2 * pair + part
            for c in range(4):
                start = ROWS_OF[c] + group if group < 8 else RIMS_OF[c] + 2 * (group - 8)
                lines[:, start, :] = result[64 * c : 64 * c + 64, 128 * part : 128 * part + 128]

    pl.semaphore_wait(lines_sem, 7)

    def own(src, dst, rows, sem):
        return pltpu.make_async_copy(src.at[mine, rows], dst.at[mine, rows], sem)

    def send_all(src, dst, rows, send_sem, recv_sem):
        def send(step, carry):
            other = lax.rem(mine + hop(step), OWN)
            remote(
                src.at[other, rows], dst.at[mine, rows], send_sem, recv_sem, place(other, grid_bead)
            ).start()
            return carry

        lax.fori_loop(1, OWN, send, 0)

    rest = pl.ds(0, OWN - 1)
    half_rows = (pl.ds(0, 20), pl.ds(20, 20))
    for n in range(2):
        own(lines, waves_in, half_rows[n], own_sem.at[n]).start()
        send_all(lines, waves_in, half_rows[n], out_send.at[n], out_recv.at[n])

    for like in likes:
        pl.semaphore_signal(blocks_sem, inc=1, device_id=like, device_id_type=MESH)
    for copy in table_copies[3:]:
        copy.wait()
    fetched.wait()
    chosen = jnp.where(targets(owner_ref[...], True), 1.0, 0.0).astype(bf16)

    lane = lane_of(3)
    sub = lax.broadcasted_iota(jnp.int32, (1, 8, 128), 1)
    lane_group = (lane // 4) % 8
    square_y, factor_y = row_ref[0:1, :], row_ref[1:2, :]
    up = lax.broadcasted_iota(jnp.int32, (256, 256), 0)
    across = lax.broadcasted_iota(jnp.int32, (256, 256), 1)
    square_x = jnp.sum(jnp.where(up == across, square_y, 0.0), 1, keepdims=True)
    factor_x = jnp.sum(jnp.where(up == across, factor_y, 0.0), 1, keepdims=True)
    mine_z = lax.broadcasted_iota(jnp.int32, (1, 256), 1) - 2 * mine

    for n in range(2):
        own(lines, waves_in, half_rows[n], own_sem.at[n]).wait()
        settle(waves_in.at[rest, half_rows[n]], out_recv.at[n])
        for q in range(2):
            padding = jnp.zeros((8, 4, 128), f32)
            extra = blocks_exchanged(
                [
                    jnp.concatenate(
                        [waves_in[pl.ds(4 * q + j, 8, stride=8), 16 + 4 * n : 20 + 4 * n, :], padding], 1
                    )
                    for j in range(4)
                ]
            )
            for half in range(2):
                c = 2 * n + half
                main = blocks_exchanged(
                    [
                        waves_in[pl.ds(4 * q + j, 8, stride=8), ROWS_OF[c] : ROWS_OF[c] + 8, :]
                        for j in range(4)
                    ]
                )
                for i in range(4):
                    value = main[i]
                    rim = jnp.where(lane_group == sub, extra[(i + 1) % 4][:, 2 + half : 3 + half, :], 0.0)
                    if i < 3:
                        value = value + jnp.where(sub == 0, shifted(extra[i][:, half : half + 1, :], 1), 0.0)
                        corner = shifted(extra[3][:, half : half + 1, :], 1)
                        rim = rim + jnp.where((sub == 0) & (lane_group == i), corner, 0.0)
                    lines_of = slice(64 * i, 64 * i + 64)
                    plane[half, lines_of, 128 * q : 128 * q + 128] = value.reshape(64, 128)
                    high, low = split(rim.reshape(64, 128))
                    plane_rim[half, lines_of, 128 * q : 128 * q + 128] = high
                    plane_rim[half, lines_of, 256 + 128 * q : 384 + 128 * q] = low

        real, imag = [
            dots(*split(plane[half] + product(plane_rim[half], fold[0][...])), fy[0][...], fy[1][...])
            for half in range(2)
        ]
        spec = jnp.concatenate(
            [real[:, :256] + imag[:, 256:], imag[:, :256] - real[:, 256:]], 1
        )
        both = dots(fx[0][...], fx[1][...], *split(spec))
        square_z = jnp.sum(jnp.where(mine_z == n, square_y, 0.0), 1, keepdims=True)
        factor_z = jnp.sum(jnp.where(mine_z == n, factor_y, 0.0), 1, keepdims=True)
        square = square_x + square_y + square_z
        green = factor_x * factor_y * (factor_z * (4.0 * math.pi))
        green = jnp.where(square > 0.0, green / jnp.where(square > 0.0, square, 1.0), 0.0)
        spec = jnp.concatenate(
            [
                (both[:256, :256] + both[256:, 256:]) * green,
                (both[:256, 256:] - both[256:, :256]) * green,
            ],
            1,
        )
        both = dots(bx[0][...], bx[1][...], *split(spec))
        spec = jnp.concatenate(
            [both[:256, :256] - both[256:, 256:], both[:256, 256:] + both[256:, :256]], 0
        )
        both = dots(*split(spec), fy[0][...], fy[1][...])
        back = [both[:256, :256] - both[256:, 256:], both[256:, :256] + both[:256, 256:]]
        back_rim = [product(jnp.concatenate(split(value), 1), fold[1][...]) for value in back]

        for q in range(2):
            extra = [jnp.zeros((8, 8, 128), f32) for _ in range(4)]
            for half in range(2):
                c = 2 * n + half
                main, corner = [], jnp.zeros((8, 1, 128), f32)
                for i in range(4):
                    lines_of = slice(64 * i, 64 * i + 64)
                    value = back[half][lines_of, 128 * q : 128 * q + 128].reshape(8, 8, 128)
                    rim = back_rim[half][lines_of, 128 * q : 128 * q + 128].reshape(8, 8, 128)
                    main.append(value)
                    if i < 3:
                        extra[i] = jnp.where(sub == half, shifted(value[:, 0:1, :], -1), extra[i])
                        corner = jnp.where(lane_group == i, shifted(rim[:, 0:1, :], -1), corner)
                    side = jnp.sum(jnp.where(lane_group == sub, rim, 0.0), 1, keepdims=True)
                    extra[(i + 1) % 4] = jnp.where(sub == 2 + half, side, extra[(i + 1) % 4])
                extra[3] = jnp.where(sub == half, corner, extra[3])
                main = blocks_exchanged(main)
                for j in range(4):
                    waves_out[pl.ds(4 * q + j, 8, stride=8), ROWS_OF[c] : ROWS_OF[c] + 8, :] = main[j]
            extra = blocks_exchanged(extra)
            for j in range(4):
                waves_out[pl.ds(4 * q + j, 8, stride=8), 16 + 4 * n : 20 + 4 * n, :] = extra[j][:, 0:4, :]
        own(waves_out, lines_in, half_rows[n], own_sem.at[2 + n]).start()
        send_all(waves_out, lines_in, half_rows[n], back_send.at[n], back_recv.at[n])

    for n in range(2):
        own(waves_out, lines_in, half_rows[n], own_sem.at[2 + n]).wait()
        settle(lines_in.at[rest, half_rows[n]], back_recv.at[n])

    for pair in range(5):
        columns = []
        for group in (2 * pair, 2 * pair + 1):
            starts = [
                ROWS_OF[c] + group if group < 8 else RIMS_OF[c] + 2 * (group - 8) for c in range(4)
            ]
            columns.append(jnp.concatenate([lines_in[:, start, :] for start in starts], 0))
        result = dots(bz[0][...], bz[1][...], *split(jnp.concatenate(columns, 1)))
        for part in range(2):
            lines_z[2 * pair + part, 0:256, :] = result[:, 128 * part : 128 * part + 128]
            lines_z[2 * pair + part, 256:264, :] = result[0:8, 128 * part : 128 * part + 128]

    lane = lane_of(2)
    low_half = lane < 64
    even = (lane // 32) % 2 == 0

    def regroup(part, rows):
        at = pl.ds(pl.multiple_of(part * 32, 32), rows)
        rim = lines_z[9, at, :]
        for group in range(9):
            main = lines_z[group, at, :]
            if group < 8:
                side = turn(rim, -4 * group)
            else:
                side = jnp.where(
                    lane < 64, turn(main, -64), jnp.where(lane < 96, turn(main, -36), turn(main, -8))
                )
            pair_even = jnp.where(even, main, side)
            pair_odd = turn(jnp.where(even, side, main), -32)
            for odd, value in enumerate((pair_even, pair_odd)):
                other = turn(value, 64)
                high = value.astype(bf16).astype(f32)
                high_other = other.astype(bf16).astype(f32)
                planes = (
                    jnp.where(low_half, high, other - high_other),
                    jnp.where(low_half, high_other, value - high),
                )
                for second in range(2):
                    plane_x = 4 * group + 2 * second + odd
                    whole = jnp.concatenate([last[plane_x], planes[second]], 0)
                    for k in range(rows // 8):
                        window = whole[8 * k : 8 * k + 16].astype(bf16)
                        field[plane_x * 32 + 4 * part + k] = window
                    last[plane_x] = planes[second][rows - 8 : rows]

    def regroup_step(part, carry):
        regroup(part, 32)
        return carry

    last[...] = jnp.zeros_like(last)
    lax.fori_loop(0, 8, regroup_step, 0)
    regroup(8, 8)

    rows16 = lax.broadcasted_iota(jnp.int32, (16, 128), 0).astype(f32) - 1.0
    rows40 = lax.broadcasted_iota(jnp.int32, (40, 128), 0).astype(f32) - 1.0
    nothing = jnp.zeros((24, 256), f32)

    def one(number, slot):
        charge, at_x, at_y, at_z = [slot[i : i + 1] for i in range(4)]
        at_x = at_x - codes[1, number].astype(f32)
        at_z = at_z - codes[2, number].astype(f32)
        weight_x, slope_x = bspline(rows16 - at_x, True)
        weight_z, slope_z = bspline(rows16 - at_z, True)
        along_y = jnp.concatenate(bspline(rows40 - at_y, True), 1)
        y_high, y_low = split(jnp.concatenate([along_y, nothing], 0))
        both = jnp.concatenate([y_high, y_high, y_low, y_low], 0)
        base = codes[0, number]
        window = jnp.concatenate([field[base + 32 * i + 1] for i in range(11)], 0)
        out = jnp.dot(jnp.concatenate([window, window], 1), both, preferred_element_type=f32)
        plain = jnp.zeros((16, 128), f32)
        along_x = jnp.zeros((16, 128), f32)
        sloped = jnp.zeros((16, 128), f32)
        for i in range(11):
            value = out[16 * i : 16 * i + 16, :128]
            slope = out[16 * i : 16 * i + 16, 128:]
            plain = plain + weight_x[i : i + 1] * value
            along_x = along_x + slope_x[i : i + 1] * value
            sloped = sloped + weight_x[i : i + 1] * slope
        minus = -charge
        return jnp.concatenate(
            [
                minus * jnp.sum(along_x * weight_z, 0, keepdims=True),
                minus * jnp.sum(sloped * weight_z, 0, keepdims=True),
                minus * jnp.sum(plain * slope_z, 0, keepdims=True),
                charge,
            ],
            0,
        )

    def interpolate(step):
        sources = [lax.rem(chunk + hop(4 * step + k), OWN) for k in range(4)]
        found = []
        for source in sources:
            pair = slots_ref[pl.ds(pl.multiple_of(8 * source, 8), 8), :]
            found.append(
                jnp.concatenate([one(2 * source, pair[0:4]), one(2 * source + 1, pair[4:8])], 0)
            )
        for source, value in zip(sources, found):
            force[source] = value

    def send_force(source):
        remote(
            force.at[source], force_in.at[mine], force_send, force_recv,
            (grid_bead, source // 8, source % 8),
        ).start()

    pl.semaphore_wait(blocks_sem, 3)
    springs = [
        remote(frac_ref, target, bead_send.at[i], bead_recv.at[i], (lax.rem(bead + step, 4), px, py))
        for i, (target, step) in enumerate(((before_ref, 1), (after_ref, 3)))
    ]
    for copy in springs:
        copy.start()
    interpolate(0)

    @pl.when(same)
    def _():
        pltpu.make_async_copy(force.at[chunk], force_in.at[mine], own_sem.at[4]).start()

    @pl.when(jnp.logical_not(same))
    def _():
        send_force(chunk)

    def send_forces(step, first):
        for k in range(first, 4):
            send_force(lax.rem(chunk + hop(4 * step + k), OWN))

    send_forces(0, 1)

    def interpolate_step(step, carry):
        interpolate(step)
        send_forces(step - 1, 0)
        return carry

    interpolate(1)
    lax.fori_loop(2, OWN // 4, interpolate_step, 0)
    send_forces(OWN // 4 - 1, 0)
    for copy in springs:
        copy.wait()
    bends = [2.0 * frac_ref[i] - before_ref[i] - after_ref[i] for i in range(3)]

    @pl.when(same)
    def _():
        settle(force_in.at[mine], own_sem.at[4])
        settle(force_in.at[rest], force_recv)
        settle(force_in.at[rest], force_send)

    @pl.when(jnp.logical_not(same))
    def _():
        settle(force_in, force_recv)
        settle(force_in, force_send)

    for axis in range(3):
        both = jnp.concatenate([force_in[:, axis, :], force_in[:, 4 + axis, :]], 0)
        moved = sum(
            lax.dot_general(chosen, part, (((0,), (0,)), ((), ())), preferred_element_type=f32)
            for part in reversed(three(both))
        )
        out_ref[axis] = moved - spring_scale * bends[axis]

    for n in range(2):
        settle(lines.at[rest, half_rows[n]], out_send.at[n])
        settle(waves_out.at[rest, half_rows[n]], back_send.at[n])


def grid_to_forces(codes, packed, slots, frac, owner_row):
    table = tables()
    consts = [packed] + [jnp.asarray(half) for name in TABLES for half in table[name]]
    consts += [jnp.asarray(table["row"]), slots, frac, owner_row]
    dma = pltpu.SemaphoreType.DMA
    chunks = VMEM((OWN, 40, 128), f32)
    return pl.pallas_call(
        wave_kernel,
        out_shape=jax.ShapeDtypeStruct((3, OWN, 128), f32),
        in_specs=[pl.BlockSpec(memory_space=HBM)] * 18,
        out_specs=pl.BlockSpec(memory_space=VMEM),
        scratch_shapes=[VMEM(const.shape, const.dtype) for const in consts]
        + [
            chunks, chunks, chunks, chunks,
            VMEM((2, 256, 256), f32), VMEM((2, 256, 512), bf16),
            VMEM((10, 264, 128), f32), VMEM((36, 8, 128), f32), VMEM((36 * 32 + 1, 16, 128), bf16),
            VMEM((OWN, 8, 128), f32), VMEM((OWN, 8, 128), f32),
            dma((17,)), dma((2,)), dma((2,)), dma((2,)), dma((2,)), dma((5,)), dma, dma,
            pltpu.SemaphoreType.REGULAR,
            VMEM((3, OWN, 128), f32), VMEM((3, OWN, 128), f32), dma((2,)), dma((2,)),
            SMEM((8, 128), jnp.int32), dma, pltpu.SemaphoreType.REGULAR,
        ],
        compiler_params=pltpu.CompilerParams(
            collective_id=1, has_side_effects=True, vmem_limit_bytes=60 << 20
        ),
        name="grid_to_forces",
    )(
        codes, *consts,
    )


def local(block_owner, block_tile, atom_cell, atom_frac, charge, zone):
    owner_row = block_owner.reshape(1, OWN)
    frac = jnp.transpose(atom_frac[0], (1, 0, 2))
    slots = atoms_to_slots(
        owner_row, block_tile.reshape(1, OWN), atom_cell, frac, charge, zone
    )
    packed, codes = spread(slots)
    total = grid_to_forces(codes, packed, slots, frac, owner_row)
    return jnp.transpose(total, (1, 0, 2))[None]


def solution(mesh):
    return jax.shard_map(
        local,
        mesh=mesh,
        in_specs=(
            P(("px", "py"), None),
            P(("px", "py")),
            P(("px", "py"), None),
            P("bead", ("px", "py"), None, None),
            P(("px", "py"), None),
            P(("px", "py"), None),
        ),
        out_specs=P("bead", ("px", "py"), None, None),
        check_vma=False,
    )
```

```python
import functools
import math

import jax
import jax.numpy as jnp
import ml_dtypes
import numpy as np
from jax import lax
from jax.experimental import pallas as pl
from jax.experimental.pallas import tpu as pltpu
from jax.sharding import PartitionSpec as P

NG = 256
OWN = 64
f32 = jnp.float32
bf16 = jnp.bfloat16
MESH = pl.DeviceIdType.MESH
VMEM = pltpu.VMEM
SMEM = pltpu.SMEM
HBM = pltpu.HBM
ewald_beta = 0.75
spring_scale = 0.25


def halves(table):
    table = table.astype(np.float32)
    high = table.astype(ml_dtypes.bfloat16)
    low = (table - high.astype(np.float32)).astype(ml_dtypes.bfloat16)
    return high, low


def waves(rows, columns):
    angle = (np.outer(rows, columns) % NG) * (2.0 * math.pi / NG)
    return np.cos(angle), np.sin(angle)


@functools.lru_cache(None)
def tables():
    whole = np.arange(NG)
    owner = np.arange(OWN)
    kz = np.stack([2 * owner, 2 * owner + 1])
    cos_z, sin_z = waves(kz.reshape(-1), whole)
    forward_z = np.concatenate([cos_z[:OWN], -sin_z[:OWN], cos_z[OWN:], -sin_z[OWN:]])
    scale = np.where(kz == 0, 1.0, 2.0) / float(NG**3)
    scale = np.repeat(scale, 2, 0).reshape(-1)
    back_z = (forward_z * scale[:, None]).T
    forward_y = np.concatenate(waves(whole, whole), 1)
    rim = (32 * (whole // 32 + 1) + whole % 4) % NG
    fold_y = np.concatenate([rim[:, None] == whole[None, :]] * 2).astype(ml_dtypes.bfloat16)
    unfold_y = np.concatenate([whole[:, None] == rim[None, :]] * 2).astype(ml_dtypes.bfloat16)
    step, block, group = np.meshgrid(np.arange(4), np.arange(8), np.arange(8), indexing="ij")
    place = (32 * block + 4 * group + step).reshape(-1)
    cos_x, sin_x = waves(whole, place)
    forward_x = np.concatenate([cos_x, sin_x])
    back_x = np.concatenate([cos_x.T, sin_x.T])
    wave = (whole + NG // 2) % NG - NG // 2
    theta = wave * (2.0 * math.pi / NG)
    factor = (6.0 / (4.0 + 2.0 * np.cos(theta))) ** 2
    factor = factor * np.exp(-theta * theta / (4.0 * ewald_beta * ewald_beta))
    row = np.zeros((8, 256), np.float32)
    row[0], row[1] = theta * theta, factor
    return dict(
        forward_z=halves(forward_z),
        back_z=halves(back_z),
        forward_y=halves(forward_y),
        fold_y=(fold_y, unfold_y),
        forward_x=halves(forward_x),
        back_x=halves(back_x),
        row=row,
    )


def split(value):
    high = value.astype(bf16)
    return high, (value - high.astype(f32)).astype(bf16)


product = functools.partial(jnp.dot, preferred_element_type=f32)


def dots(a_high, a_low, b_high, b_low):
    return product(a_high, b_high) + (product(a_high, b_low) + product(a_low, b_high))


def lane_of(rank):
    return lax.broadcasted_iota(jnp.int32, (1,) * (rank - 1) + (128,), rank - 1)


def turn(value, steps):
    steps = steps % 128
    if steps == 0:
        return value
    flat = value.reshape(-1, 128)
    return pltpu.roll(flat, steps, 1).reshape(value.shape)


def blocks_exchanged(parts):
    lane = lane_of(parts[0].ndim)
    low = lane < 64
    even = (lane // 32) % 2 == 0
    first = [
        jnp.where(low, parts[0], turn(parts[2], 64)),
        jnp.where(low, parts[1], turn(parts[3], 64)),
        jnp.where(low, turn(parts[0], 64), parts[2]),
        jnp.where(low, turn(parts[1], 64), parts[3]),
    ]
    return [
        jnp.where(even, first[0], turn(first[1], 32)),
        jnp.where(even, turn(first[0], 96), first[1]),
        jnp.where(even, first[2], turn(first[3], 32)),
        jnp.where(even, turn(first[2], 96), first[3]),
    ]


def bspline(offsets, slopes):
    v = jnp.abs(offsets)
    a = jnp.maximum(2.0 - v, 0.0)
    b = jnp.maximum(1.0 - v, 0.0)
    aa = a * a
    bb = 4.0 * (b * b)
    weight = aa * a - bb * b
    if not slopes:
        return weight
    return weight, jnp.where(offsets < 0.0, bb - aa, aa - bb)


def vmem(count):
    return [pl.BlockSpec(memory_space=VMEM)] * count


def targets(owner_row, apart):
    blocks = owner_row.shape[1]
    up = lax.broadcasted_iota(jnp.int32, (blocks, blocks), 0)
    across = lax.broadcasted_iota(jnp.int32, (blocks, blocks), 1)
    owner_column = jnp.sum(jnp.where(up == across, owner_row, 0).astype(f32), 1, keepdims=True)
    owner_float = owner_row.astype(f32)
    before = jnp.where((owner_column == owner_float) & (up < across), 1.0, 0.0)
    rank = jnp.sum(before, 0, keepdims=True)
    target = owner_float + OWN * rank if apart else 2.0 * owner_float + rank
    slot = lax.broadcasted_iota(jnp.int32, (2 * OWN, blocks), 0).astype(f32)
    return slot == target


def three(value):
    high = value.astype(bf16)
    rest = value - high.astype(f32)
    middle = rest.astype(bf16)
    return high, middle, (rest - middle.astype(f32)).astype(bf16)


def remote(src, dst, send_sem, recv_sem, device):
    return pltpu.make_async_remote_copy(
        src_ref=src, dst_ref=dst, send_sem=send_sem, recv_sem=recv_sem,
        device_id=device, device_id_type=MESH,
    )


def settle(ref, sem):
    pltpu.make_async_copy(ref, ref, sem).wait()


def atoms_kernel(
    owner_hbm, tile_hbm, cell_hbm, frac_hbm, charge_hbm, zone_hbm, slots_ref,
    owner_ref, tile_ref, cell_ref, frac_ref, charge_ref, zone_ref,
    payload, stage, stage_send, stage_recv, send_sem, recv_sem, own_sem, in_sem, lines_sem,
):
    loads = [
        pltpu.make_async_copy(src, dst, in_sem.at[i])
        for i, (src, dst) in enumerate(
            (
                (owner_hbm, owner_ref), (tile_hbm, tile_ref), (cell_hbm, cell_ref),
                (frac_hbm, frac_ref), (charge_hbm, charge_ref), (zone_hbm, zone_ref),
            )
        )
    ]
    for copy in loads:
        copy.start()
    bead, px, py = here()
    chunk = px * 8 + py
    barrier = pltpu.get_barrier_semaphore()

    crossing = [(bead, lax.rem(px + step, 8), py) for step in range(1, 8)]
    greeted = crossing + [(bead, px, lax.rem(py + step, 8)) for step in range(1, 8)]
    greeted += [(lax.rem(bead + step, 4), px, py) for step in range(1, 4)]
    for device in greeted:
        pl.semaphore_signal(barrier, inc=1, device_id=device, device_id_type=MESH)

    for copy in loads:
        copy.wait()
    chosen = jnp.where(targets(owner_ref[...], False), 1.0, 0.0).astype(bf16)
    blocks = cell_ref.shape[0]
    up = lax.broadcasted_iota(jnp.int32, (blocks, blocks), 0)
    across = lax.broadcasted_iota(jnp.int32, (blocks, blocks), 1)
    tile = jnp.sum(jnp.where(up == across, tile_ref[...], 0).astype(f32), 1, keepdims=True)
    tile = tile.astype(jnp.int32)
    cell = cell_ref[...]
    corners = [tile >> 7, (tile >> 5) & 3, tile & 31]
    cells = [cell >> 6, (cell >> 3) & 7, cell & 7]
    fields = [charge_ref[...] * zone_ref[...].astype(f32)]
    for axis in range(3):
        base = (corners[axis] * 8).astype(f32)
        inside = cells[axis].astype(f32) + frac_ref[axis]
        fields.append(base + jnp.minimum(inside, 8.0 - 2.0**-16))
    for place_in, field in enumerate(fields):
        parts = three(field)
        moved = sum(
            jnp.dot(chosen, part, preferred_element_type=f32) for part in reversed(parts)
        )
        payload[pl.ds(place_in, 2 * OWN, stride=4), :] = moved

    pl.semaphore_wait(barrier, 17)
    for device in crossing:
        pl.semaphore_signal(lines_sem, inc=1, device_id=device, device_id_type=MESH)
    staged = []
    for half in range(2):
        for step in (1, 3, 2):
            other = lax.rem(bead + step, 4)
            start = pl.multiple_of(other * 128 + half * 64, 64)
            sem = 2 * (step - 1) + half
            copy = remote(
                payload.at[pl.ds(start, 64)], stage.at[bead, half * 64 : half * 64 + 64],
                stage_send.at[sem], stage_recv.at[sem], (other, px, py),
            )
            staged.append((step, half, copy))
            copy.start()

    mark = pl.ds(pl.multiple_of(chunk * 8, 8), 8)
    pl.semaphore_wait(lines_sem, 7)

    def deliver_half(turn_of, half):
        from_bead = lax.rem(bead + turn_of, 4)

        def piece_of(step):
            j = 8 * half + lax.rem(step + 2 * px + py % 2 + 4 * (py // 2 - from_bead) + 16, 8)
            at = pl.multiple_of(j * 8, 8)
            if turn_of == 0:
                piece = payload.at[pl.ds(pl.multiple_of(bead * 128 + at, 8), 8)]
            else:
                piece = stage.at[from_bead, pl.ds(at, 8)]
            return piece, (bead, j // 2, 2 * from_bead + j % 2)

        def send(step, carry):
            piece, device = piece_of(step)
            remote(piece, slots_ref.at[mark], send_sem, recv_sem, device).start()
            return carry

        mine = jnp.logical_and(from_bead == py // 2, px // 4 == half)

        @pl.when(mine)
        def _():
            pltpu.make_async_copy(piece_of(0)[0], slots_ref.at[mark], own_sem).start()

        @pl.when(jnp.logical_not(mine))
        def _():
            send(0, 0)

        lax.fori_loop(1, 8, send, 0, unroll=7)

    for half in range(2):
        deliver_half(0, half)
    for step, half, copy in staged:
        copy.wait_recv()
        deliver_half(4 - step, half)
    settle(slots_ref.at[mark], own_sem)
    rest = pl.ds(0, 8 * OWN - 8)
    settle(slots_ref.at[rest], recv_sem)
    settle(slots_ref.at[rest], send_sem)
    for _, _, copy in staged:
        copy.wait_send()


def atoms_to_slots(owner_row, tile_row, cell, frac, charge, zone):
    dma = pltpu.SemaphoreType.DMA
    return pl.pallas_call(
        atoms_kernel,
        out_shape=jax.ShapeDtypeStruct((8 * OWN, 128), f32),
        in_specs=[pl.BlockSpec(memory_space=HBM)] * 6,
        out_specs=pl.BlockSpec(memory_space=pl.ANY),
        scratch_shapes=[
            VMEM((1, OWN), jnp.int32), VMEM((1, OWN), jnp.int32), VMEM((OWN, 128), jnp.int32),
            VMEM((3, OWN, 128), f32), VMEM((OWN, 128), f32), VMEM((OWN, 128), jnp.int32),
            VMEM((8 * OWN, 128), f32), VMEM((4, 128, 128), f32),
            dma((6,)), dma((6,)), dma, dma, dma, dma((6,)), pltpu.SemaphoreType.REGULAR,
        ],
        compiler_params=pltpu.CompilerParams(
            collective_id=0, has_side_effects=True, vmem_limit_bytes=60 << 20
        ),
        name="atoms_to_slots",
    )(owner_row, tile_row, cell, frac, charge, zone)


def tile_codes(slots_ref):
    along_x = slots_ref[pl.ds(1, 2 * OWN, stride=4), :]
    along_z = slots_ref[pl.ds(3, 2 * OWN, stride=4), :]
    tile_x = (jnp.max(along_x, 1, keepdims=True) * 0.125).astype(jnp.int32)
    tile_z = (jnp.max(along_z, 1, keepdims=True) * 0.125).astype(jnp.int32)
    up = lax.broadcasted_iota(jnp.int32, (128, 128), 0)
    across = lax.broadcasted_iota(jnp.int32, (128, 128), 1)
    sub = lax.broadcasted_iota(jnp.int32, (8, 128), 0)
    value = jnp.zeros((8, 128), f32)
    columns = (256 * tile_x + tile_z, 8 * tile_x, 8 * tile_z)
    for place_in, column in enumerate(columns):
        row = jnp.sum(jnp.where(up == across, column.astype(f32), 0.0), 0, keepdims=True)
        value = jnp.where(sub == place_in, row, value)
    return value.astype(jnp.int32)


def spread_kernel(slots_ref, out_hbm, codes_hbm, codes_scalar, density, codes, out_ref, sem, out_sem):
    codes[...] = tile_codes(slots_ref)
    copy = pltpu.make_async_copy(codes, codes_scalar, sem.at[0])
    copy.start()
    handed = pltpu.make_async_copy(codes, codes_hbm, sem.at[1])
    handed.start()
    density[...] = jnp.zeros_like(density)
    copy.wait()
    rows16 = lax.broadcasted_iota(jnp.int32, (16, 128), 0).astype(f32) - 1.0
    rows40 = lax.broadcasted_iota(jnp.int32, (40, 128), 0).astype(f32) - 1.0

    def one(number, slot):
        plane_x, row_z = codes_scalar[1, number], codes_scalar[2, number]
        charge, at_x, at_y, at_z = [slot[i : i + 1] for i in range(4)]
        at_x = at_x - plane_x.astype(f32)
        at_z = at_z - row_z.astype(f32)
        weight_x = bspline(rows16 - at_x, False) * (charge * (1.0 / 216.0))
        weight_z = bspline(rows16 - at_z, False)
        weight_y = jnp.concatenate([bspline(rows40 - at_y, False), jnp.zeros((24, 128), f32)], 0)
        plane = jnp.concatenate([weight_x[i : i + 1] * weight_z for i in range(11)], 0)
        plane = jnp.concatenate(split(plane), 1)
        y_high, y_low = split(weight_y)
        left = jnp.concatenate([y_high, y_low], 0)
        right = jnp.concatenate([y_high, jnp.zeros((64, 128), bf16)], 0)
        both = jnp.concatenate([left, right], 1)
        out = lax.dot_general(plane, both, (((1,), (1,)), ((), ())), preferred_element_type=f32)
        return plane_x, row_z, out

    def put(plane_x, row_z, out):
        base = pl.multiple_of(row_z, 8)
        for i in range(11):
            density[plane_x + i, pl.ds(base, 16), :] += out[16 * i : 16 * i + 16]

    def step(index, carry):
        found = []
        for k in range(8):
            pair = slots_ref[pl.ds(pl.multiple_of(64 * index + 8 * k, 8), 8), :]
            for rank in range(2):
                found.append(one(16 * index + 2 * k + rank, pair[4 * rank : 4 * rank + 4]))
        for item in found:
            put(*item)
        return carry

    lax.fori_loop(0, 8, step, 0)

    lane = lane_of(2)
    low = lane < 64
    even = (lane // 32) % 2 == 0

    def fold(plane, carry):
        density[plane, 0:8, :] += density[plane, 256:264, :]
        return carry

    lax.fori_loop(0, 36, fold, 0)

    def regroup(chunk, carry):
        here = pl.ds(pl.multiple_of(chunk * 32, 32), 32)
        rim = jnp.zeros((32, 128), f32)

        def keep(group, value):
            out_ref[group, here, :] = value

        for group in range(9):
            four = [density[4 * group + i, here, :] for i in range(4)]
            pair_even = jnp.where(low, four[0], four[2]) + turn(jnp.where(low, four[2], four[0]), 64)
            pair_odd = jnp.where(low, four[1], four[3]) + turn(jnp.where(low, four[3], four[1]), 64)
            pair_odd = turn(pair_odd, 32)
            main = jnp.where(even, pair_even, pair_odd)
            side = jnp.where(even, pair_odd, pair_even)
            if group < 8:
                keep(group, main)
                rim = rim + turn(side, 4 * group)
            else:
                last = lane >= 96
                corner = jnp.where((lane >= 96) & (lane < 100), turn(side, 64), 0.0)
                corner = jnp.where((lane >= 100) & (lane < 104), turn(side, 36), corner)
                corner = jnp.where((lane >= 104) & (lane < 108), turn(side, 8), corner)
                keep(8, jnp.where(last, corner, main))
        keep(9, rim)
        pltpu.make_async_copy(out_ref.at[:, here, :], out_hbm.at[:, here, :], out_sem.at[chunk]).start()
        return carry

    lax.fori_loop(0, 8, regroup, 0)
    handed.wait()
    for chunk in range(8):
        here = pl.ds(32 * chunk, 32)
        pltpu.make_async_copy(out_ref.at[:, here, :], out_hbm.at[:, here, :], out_sem.at[chunk]).wait()


def spread(slots):
    return pl.pallas_call(
        spread_kernel,
        out_shape=[
            jax.ShapeDtypeStruct((10, 256, 128), f32),
            jax.ShapeDtypeStruct((8, 128), jnp.int32),
        ],
        in_specs=vmem(1),
        out_specs=[pl.BlockSpec(memory_space=pl.ANY)] * 2,
        scratch_shapes=[
            SMEM((8, 128), jnp.int32),
            VMEM((36, 264, 128), f32),
            VMEM((8, 128), jnp.int32),
            VMEM((10, 256, 128), f32),
            pltpu.SemaphoreType.DMA((2,)),
            pltpu.SemaphoreType.DMA((8,)),
        ],
        compiler_params=pltpu.CompilerParams(vmem_limit_bytes=60 << 20),
        name="spread",
    )(slots)


TABLES = ("forward_z", "forward_y", "forward_x", "back_x", "fold_y", "back_z")
ROWS_OF = (0, 8, 24, 32)
RIMS_OF = (16, 17, 20, 21)


def here():
    return lax.axis_index("bead"), lax.axis_index("px"), lax.axis_index("py")


def place(number, bead):
    return (number // 16, (number // 2) % 8, 2 * bead + number % 2)


def hop(step):
    return lax.rem(step * 37, OWN)


def shifted(value, steps):
    if steps == 1:
        return jnp.concatenate([value[7:8], value[0:7]], 0)
    return jnp.concatenate([value[1:8], value[0:1]], 0)


def wave_kernel(
    codes_hbm, *rest,
):
    table_refs, rest = rest[:17], rest[17:]
    out_ref, rest = rest[0], rest[1:]
    table_vmem, rest = rest[:17], rest[17:]
    packed, fz_high, fz_low = table_vmem[:3]
    row_ref, slots_ref, frac_ref, owner_ref = table_vmem[13:]
    (
        lines, waves_in, waves_out, lines_in, plane, plane_rim,
        lines_z, last, field, force, force_in, table_sem, out_send, out_recv, back_send, back_recv,
        own_sem, force_send, force_recv, blocks_sem, before_ref, after_ref, bead_send, bead_recv,
        codes, codes_sem, lines_sem,
    ) = rest
    (fz, fy, fx, bx, fold, bz) = [(table_vmem[2 * i + 1], table_vmem[2 * i + 2]) for i in range(6)]
    bead, px, py = here()
    mine, grid_bead, chunk = bead * 16 + px * 2 + py % 2, py // 2, px * 8 + py
    same = bead == grid_bead
    barrier = pltpu.get_barrier_semaphore()

    table_copies = [
        pltpu.make_async_copy(table_refs[i], table_vmem[i], table_sem.at[i]) for i in range(17)
    ]
    for copy in table_copies[:3]:
        copy.start()

    crossing = [(bead, lax.rem(px + step, 8), py) for step in range(1, 8)]
    across = bead * 2 + py % 2
    along = [lax.rem(across + step, 8) for step in range(1, 8)]
    greeted = crossing + [(other // 2, px, 2 * grid_bead + other % 2) for other in along]
    likes = [(bead, px, lax.rem(py + 2 * k, 8)) for k in range(1, 4)]
    for device in greeted + likes:
        pl.semaphore_signal(barrier, inc=1, device_id=device, device_id_type=MESH)
    for copy in table_copies[3:]:
        copy.start()
    fetched = pltpu.make_async_copy(codes_hbm, codes, codes_sem)
    fetched.start()
    for copy in table_copies[:3]:
        copy.wait()
    pl.semaphore_wait(barrier, 17)
    for device in crossing:
        pl.semaphore_signal(lines_sem, inc=1, device_id=device, device_id_type=MESH)

    for pair in range(5):
        high, low = split(jnp.concatenate([packed[2 * pair], packed[2 * pair + 1]], 1))
        result = dots(fz[0][...], fz[1][...], high, low)
        for part in range(2):
            group = 2 * pair + part
            for c in range(4):
                start = ROWS_OF[c] + group if group < 8 else RIMS_OF[c] + 2 * (group - 8)
                lines[:, start, :] = result[64 * c : 64 * c + 64, 128 * part : 128 * part + 128]

    pl.semaphore_wait(lines_sem, 7)

    def own(src, dst, rows, sem):
        return pltpu.make_async_copy(src.at[mine, rows], dst.at[mine, rows], sem)

    def send_all(src, dst, rows, send_sem, recv_sem):
        def send(step, carry):
            other = lax.rem(mine + hop(step), OWN)
            remote(
                src.at[other, rows], dst.at[mine, rows], send_sem, recv_sem, place(other, grid_bead)
            ).start()
            return carry

        lax.fori_loop(1, OWN, send, 0, unroll=9)

    rest = pl.ds(0, OWN - 1)
    half_rows = (pl.ds(0, 20), pl.ds(20, 20))
    for n in range(2):
        own(lines, waves_in, half_rows[n], own_sem.at[n]).start()
        send_all(lines, waves_in, half_rows[n], out_send.at[n], out_recv.at[n])

    for like in likes:
        pl.semaphore_signal(blocks_sem, inc=1, device_id=like, device_id_type=MESH)
    for copy in table_copies[3:]:
        copy.wait()
    fetched.wait()
    chosen = jnp.where(targets(owner_ref[...], True), 1.0, 0.0).astype(bf16)

    lane = lane_of(3)
    sub = lax.broadcasted_iota(jnp.int32, (1, 8, 128), 1)
    lane_group = (lane // 4) % 8
    square_y, factor_y = row_ref[0:1, :], row_ref[1:2, :]
    up = lax.broadcasted_iota(jnp.int32, (256, 256), 0)
    across = lax.broadcasted_iota(jnp.int32, (256, 256), 1)
    square_x = jnp.sum(jnp.where(up == across, square_y, 0.0), 1, keepdims=True)
    factor_x = jnp.sum(jnp.where(up == across, factor_y, 0.0), 1, keepdims=True)
    mine_z = lax.broadcasted_iota(jnp.int32, (1, 256), 1) - 2 * mine

    for n in range(2):
        own(lines, waves_in, half_rows[n], own_sem.at[n]).wait()
        settle(waves_in.at[rest, half_rows[n]], out_recv.at[n])
        for q in range(2):
            padding = jnp.zeros((8, 4, 128), f32)
            extra = blocks_exchanged(
                [
                    jnp.concatenate(
                        [waves_in[pl.ds(4 * q + j, 8, stride=8), 16 + 4 * n : 20 + 4 * n, :], padding], 1
                    )
                    for j in range(4)
                ]
            )
            for half in range(2):
                c = 2 * n + half
                main = blocks_exchanged(
                    [
                        waves_in[pl.ds(4 * q + j, 8, stride=8), ROWS_OF[c] : ROWS_OF[c] + 8, :]
                        for j in range(4)
                    ]
                )
                for i in range(4):
                    value = main[i]
                    rim = jnp.where(lane_group == sub, extra[(i + 1) % 4][:, 2 + half : 3 + half, :], 0.0)
                    if i < 3:
                        value = value + jnp.where(sub == 0, shifted(extra[i][:, half : half + 1, :], 1), 0.0)
                        corner = shifted(extra[3][:, half : half + 1, :], 1)
                        rim = rim + jnp.where((sub == 0) & (lane_group == i), corner, 0.0)
                    lines_of = slice(64 * i, 64 * i + 64)
                    plane[half, lines_of, 128 * q : 128 * q + 128] = value.reshape(64, 128)
                    high, low = split(rim.reshape(64, 128))
                    plane_rim[half, lines_of, 128 * q : 128 * q + 128] = high
                    plane_rim[half, lines_of, 256 + 128 * q : 384 + 128 * q] = low

        real, imag = [
            dots(*split(plane[half] + product(plane_rim[half], fold[0][...])), fy[0][...], fy[1][...])
            for half in range(2)
        ]
        spec = jnp.concatenate(
            [real[:, :256] + imag[:, 256:], imag[:, :256] - real[:, 256:]], 1
        )
        both = dots(fx[0][...], fx[1][...], *split(spec))
        square_z = jnp.sum(jnp.where(mine_z == n, square_y, 0.0), 1, keepdims=True)
        factor_z = jnp.sum(jnp.where(mine_z == n, factor_y, 0.0), 1, keepdims=True)
        square = square_x + square_y + square_z
        green = factor_x * factor_y * (factor_z * (4.0 * math.pi))
        green = jnp.where(square > 0.0, green / jnp.where(square > 0.0, square, 1.0), 0.0)
        spec = jnp.concatenate(
            [
                (both[:256, :256] + both[256:, 256:]) * green,
                (both[:256, 256:] - both[256:, :256]) * green,
            ],
            1,
        )
        both = dots(bx[0][...], bx[1][...], *split(spec))
        spec = jnp.concatenate(
            [both[:256, :256] - both[256:, 256:], both[:256, 256:] + both[256:, :256]], 0
        )
        both = dots(*split(spec), fy[0][...], fy[1][...])
        back = [both[:256, :256] - both[256:, 256:], both[256:, :256] + both[:256, 256:]]
        back_rim = [product(jnp.concatenate(split(value), 1), fold[1][...]) for value in back]

        for q in range(2):
            extra = [jnp.zeros((8, 8, 128), f32) for _ in range(4)]
            for half in range(2):
                c = 2 * n + half
                main, corner = [], jnp.zeros((8, 1, 128), f32)
                for i in range(4):
                    lines_of = slice(64 * i, 64 * i + 64)
                    value = back[half][lines_of, 128 * q : 128 * q + 128].reshape(8, 8, 128)
                    rim = back_rim[half][lines_of, 128 * q : 128 * q + 128].reshape(8, 8, 128)
                    main.append(value)
                    if i < 3:
                        extra[i] = jnp.where(sub == half, shifted(value[:, 0:1, :], -1), extra[i])
                        corner = jnp.where(lane_group == i, shifted(rim[:, 0:1, :], -1), corner)
                    side = jnp.sum(jnp.where(lane_group == sub, rim, 0.0), 1, keepdims=True)
                    extra[(i + 1) % 4] = jnp.where(sub == 2 + half, side, extra[(i + 1) % 4])
                extra[3] = jnp.where(sub == half, corner, extra[3])
                main = blocks_exchanged(main)
                for j in range(4):
                    waves_out[pl.ds(4 * q + j, 8, stride=8), ROWS_OF[c] : ROWS_OF[c] + 8, :] = main[j]
            extra = blocks_exchanged(extra)
            for j in range(4):
                waves_out[pl.ds(4 * q + j, 8, stride=8), 16 + 4 * n : 20 + 4 * n, :] = extra[j][:, 0:4, :]
        own(waves_out, lines_in, half_rows[n], own_sem.at[2 + n]).start()
        send_all(waves_out, lines_in, half_rows[n], back_send.at[n], back_recv.at[n])

    for n in range(2):
        own(waves_out, lines_in, half_rows[n], own_sem.at[2 + n]).wait()
        settle(lines_in.at[rest, half_rows[n]], back_recv.at[n])

    for pair in range(5):
        columns = []
        for group in (2 * pair, 2 * pair + 1):
            starts = [
                ROWS_OF[c] + group if group < 8 else RIMS_OF[c] + 2 * (group - 8) for c in range(4)
            ]
            columns.append(jnp.concatenate([lines_in[:, start, :] for start in starts], 0))
        result = dots(bz[0][...], bz[1][...], *split(jnp.concatenate(columns, 1)))
        for part in range(2):
            lines_z[2 * pair + part, 0:256, :] = result[:, 128 * part : 128 * part + 128]
            lines_z[2 * pair + part, 256:264, :] = result[0:8, 128 * part : 128 * part + 128]

    lane = lane_of(2)
    low_half = lane < 64
    even = (lane // 32) % 2 == 0

    def regroup(part, rows):
        at = pl.ds(pl.multiple_of(part * 32, 32), rows)
        rim = lines_z[9, at, :]
        for group in range(9):
            main = lines_z[group, at, :]
            if group < 8:
                side = turn(rim, -4 * group)
            else:
                side = jnp.where(
                    lane < 64, turn(main, -64), jnp.where(lane < 96, turn(main, -36), turn(main, -8))
                )
            pair_even = jnp.where(even, main, side)
            pair_odd = turn(jnp.where(even, side, main), -32)
            for odd, value in enumerate((pair_even, pair_odd)):
                other = turn(value, 64)
                high = value.astype(bf16).astype(f32)
                high_other = other.astype(bf16).astype(f32)
                planes = (
                    jnp.where(low_half, high, other - high_other),
                    jnp.where(low_half, high_other, value - high),
                )
                for second in range(2):
                    plane_x = 4 * group + 2 * second + odd
                    whole = jnp.concatenate([last[plane_x], planes[second]], 0)
                    for k in range(rows // 8):
                        window = whole[8 * k : 8 * k + 16].astype(bf16)
                        field[plane_x * 32 + 4 * part + k] = window
                    last[plane_x] = planes[second][rows - 8 : rows]

    def regroup_step(part, carry):
        regroup(part, 32)
        return carry

    last[...] = jnp.zeros_like(last)
    lax.fori_loop(0, 8, regroup_step, 0)
    regroup(8, 8)

    rows16 = lax.broadcasted_iota(jnp.int32, (16, 128), 0).astype(f32) - 1.0
    rows40 = lax.broadcasted_iota(jnp.int32, (40, 128), 0).astype(f32) - 1.0
    nothing = jnp.zeros((24, 256), f32)

    def one(number, slot):
        charge, at_x, at_y, at_z = [slot[i : i + 1] for i in range(4)]
        at_x = at_x - codes[1, number].astype(f32)
        at_z = at_z - codes[2, number].astype(f32)
        weight_x, slope_x = bspline(rows16 - at_x, True)
        weight_z, slope_z = bspline(rows16 - at_z, True)
        along_y = jnp.concatenate(bspline(rows40 - at_y, True), 1)
        y_high, y_low = split(jnp.concatenate([along_y, nothing], 0))
        both = jnp.concatenate([y_high, y_high, y_low, y_low], 0)
        base = codes[0, number]
        window = jnp.concatenate([field[base + 32 * i + 1] for i in range(11)], 0)
        out = jnp.dot(jnp.concatenate([window, window], 1), both, preferred_element_type=f32)
        plain = jnp.zeros((16, 128), f32)
        along_x = jnp.zeros((16, 128), f32)
        sloped = jnp.zeros((16, 128), f32)
        for i in range(11):
            value = out[16 * i : 16 * i + 16, :128]
            slope = out[16 * i : 16 * i + 16, 128:]
            plain = plain + weight_x[i : i + 1] * value
            along_x = along_x + slope_x[i : i + 1] * value
            sloped = sloped + weight_x[i : i + 1] * slope
        minus = charge * (-1.0 / 72.0)
        return jnp.concatenate(
            [
                minus * jnp.sum(along_x * weight_z, 0, keepdims=True),
                minus * jnp.sum(sloped * weight_z, 0, keepdims=True),
                minus * jnp.sum(plain * slope_z, 0, keepdims=True),
                charge,
            ],
            0,
        )

    def source_at(n):
        return lax.rem(chunk + hop(OWN - 1 - n), OWN)

    def interpolate(step):
        sources = [source_at(4 * step + k) for k in range(4)]
        found = []
        for source in sources:
            pair = slots_ref[pl.ds(pl.multiple_of(8 * source, 8), 8), :]
            found.append(
                jnp.concatenate([one(2 * source, pair[0:4]), one(2 * source + 1, pair[4:8])], 0)
            )
        for source, value in zip(sources, found):
            force[source] = value

    def send_force(source):
        remote(
            force.at[source], force_in.at[mine], force_send, force_recv,
            (grid_bead, source // 8, source % 8),
        ).start()

    pl.semaphore_wait(blocks_sem, 3)
    springs = [
        remote(frac_ref, target, bead_send.at[i], bead_recv.at[i], (lax.rem(bead + step, 4), px, py))
        for i, (target, step) in enumerate(((before_ref, 1), (after_ref, 3)))
    ]
    for copy in springs:
        copy.start()
    def send_forces(step, count):
        for k in range(count):
            send_force(source_at(4 * step + k))

    def interpolate_step(step, carry):
        interpolate(step)
        send_forces(step - 1, 4)
        return carry

    interpolate(0)
    lax.fori_loop(1, OWN // 4, interpolate_step, 0)
    send_forces(OWN // 4 - 1, 3)

    @pl.when(same)
    def _():
        pltpu.make_async_copy(force.at[chunk], force_in.at[mine], own_sem.at[4]).start()

    @pl.when(jnp.logical_not(same))
    def _():
        send_force(chunk)

    for copy in springs:
        copy.wait()
    bends = [2.0 * frac_ref[i] - before_ref[i] - after_ref[i] for i in range(3)]

    @pl.when(same)
    def _():
        settle(force_in.at[mine], own_sem.at[4])
        settle(force_in.at[rest], force_recv)
        settle(force_in.at[rest], force_send)

    @pl.when(jnp.logical_not(same))
    def _():
        settle(force_in, force_recv)
        settle(force_in, force_send)

    for axis in range(3):
        both = jnp.concatenate([force_in[:, axis, :], force_in[:, 4 + axis, :]], 0)
        moved = sum(
            lax.dot_general(chosen, part, (((0,), (0,)), ((), ())), preferred_element_type=f32)
            for part in reversed(three(both))
        )
        out_ref[axis] = moved - spring_scale * bends[axis]

    for n in range(2):
        settle(lines.at[rest, half_rows[n]], out_send.at[n])
        settle(waves_out.at[rest, half_rows[n]], back_send.at[n])


def grid_to_forces(codes, packed, slots, frac, owner_row):
    table = tables()
    consts = [packed] + [jnp.asarray(half) for name in TABLES for half in table[name]]
    consts += [jnp.asarray(table["row"]), slots, frac, owner_row]
    dma = pltpu.SemaphoreType.DMA
    chunks = VMEM((OWN, 40, 128), f32)
    return pl.pallas_call(
        wave_kernel,
        out_shape=jax.ShapeDtypeStruct((3, OWN, 128), f32),
        in_specs=[pl.BlockSpec(memory_space=HBM)] * 18,
        out_specs=pl.BlockSpec(memory_space=VMEM),
        scratch_shapes=[VMEM(const.shape, const.dtype) for const in consts]
        + [
            chunks, chunks, chunks, chunks,
            VMEM((2, 256, 256), f32), VMEM((2, 256, 512), bf16),
            VMEM((10, 264, 128), f32), VMEM((36, 8, 128), f32), VMEM((36 * 32 + 1, 16, 128), bf16),
            VMEM((OWN, 8, 128), f32), VMEM((OWN, 8, 128), f32),
            dma((17,)), dma((2,)), dma((2,)), dma((2,)), dma((2,)), dma((5,)), dma, dma,
            pltpu.SemaphoreType.REGULAR,
            VMEM((3, OWN, 128), f32), VMEM((3, OWN, 128), f32), dma((2,)), dma((2,)),
            SMEM((8, 128), jnp.int32), dma, pltpu.SemaphoreType.REGULAR,
        ],
        compiler_params=pltpu.CompilerParams(
            collective_id=1, has_side_effects=True, vmem_limit_bytes=60 << 20
        ),
        name="grid_to_forces",
    )(
        codes, *consts,
    )


def local(block_owner, block_tile, atom_cell, atom_frac, charge, zone):
    owner_row = block_owner.reshape(1, OWN)
    frac = jnp.transpose(atom_frac[0], (1, 0, 2))
    slots = atoms_to_slots(
        owner_row, block_tile.reshape(1, OWN), atom_cell, frac, charge, zone
    )
    packed, codes = spread(slots)
    total = grid_to_forces(codes, packed, slots, frac, owner_row)
    return jnp.transpose(total, (1, 0, 2))[None]


def solution(mesh):
    return jax.shard_map(
        local,
        mesh=mesh,
        in_specs=(
            P(("px", "py"), None),
            P(("px", "py")),
            P(("px", "py"), None),
            P("bead", ("px", "py"), None, None),
            P(("px", "py"), None),
            P(("px", "py"), None),
        ),
        out_specs=P("bead", ("px", "py"), None, None),
        check_vma=False,
    )
```

```python
import functools
import math

import jax
import jax.numpy as jnp
import ml_dtypes
import numpy as np
from jax import lax
from jax.experimental import pallas as pl
from jax.experimental.pallas import tpu as pltpu
from jax.sharding import PartitionSpec as P

NG = 256
OWN = 64
f32 = jnp.float32
bf16 = jnp.bfloat16
MESH = pl.DeviceIdType.MESH
VMEM = pltpu.VMEM
SMEM = pltpu.SMEM
HBM = pltpu.HBM
ewald_beta = 0.75
spring_scale = 0.25


def halves(table):
    table = table.astype(np.float32)
    high = table.astype(ml_dtypes.bfloat16)
    low = (table - high.astype(np.float32)).astype(ml_dtypes.bfloat16)
    return high, low


def waves(rows, columns):
    angle = (np.outer(rows, columns) % NG) * (2.0 * math.pi / NG)
    return np.cos(angle), np.sin(angle)


@functools.lru_cache(None)
def tables():
    whole = np.arange(NG)
    owner = np.arange(OWN)
    kz = np.stack([2 * owner, 2 * owner + 1])
    cos_z, sin_z = waves(kz.reshape(-1), whole)
    forward_z = np.concatenate([cos_z[:OWN], -sin_z[:OWN], cos_z[OWN:], -sin_z[OWN:]])
    scale = np.where(kz == 0, 1.0, 2.0) / float(NG**3)
    scale = np.repeat(scale, 2, 0).reshape(-1)
    back_z = (forward_z * scale[:, None]).T
    forward_y = np.concatenate(waves(whole, whole), 1)
    rim = (32 * (whole // 32 + 1) + whole % 4) % NG
    fold_y = np.concatenate([rim[:, None] == whole[None, :]] * 2).astype(ml_dtypes.bfloat16)
    unfold_y = np.concatenate([whole[:, None] == rim[None, :]] * 2).astype(ml_dtypes.bfloat16)
    step, block, group = np.meshgrid(np.arange(4), np.arange(8), np.arange(8), indexing="ij")
    place = (32 * block + 4 * group + step).reshape(-1)
    cos_x, sin_x = waves(whole, place)
    forward_x = np.concatenate([cos_x, sin_x])
    back_x = np.concatenate([cos_x.T, sin_x.T])
    wave = (whole + NG // 2) % NG - NG // 2
    theta = wave * (2.0 * math.pi / NG)
    factor = (6.0 / (4.0 + 2.0 * np.cos(theta))) ** 2
    factor = factor * np.exp(-theta * theta / (4.0 * ewald_beta * ewald_beta))
    row = np.zeros((8, 256), np.float32)
    row[0], row[1] = theta * theta, factor
    return dict(
        forward_z=halves(forward_z),
        back_z=halves(back_z),
        forward_y=halves(forward_y),
        fold_y=(fold_y, unfold_y),
        forward_x=halves(forward_x),
        back_x=halves(back_x),
        row=row,
    )


def split(value):
    high = value.astype(bf16)
    return high, (value - high.astype(f32)).astype(bf16)


product = functools.partial(jnp.dot, preferred_element_type=f32)


def dots(a_high, a_low, b_high, b_low):
    return product(a_high, b_high) + (product(a_high, b_low) + product(a_low, b_high))


def lane_of(rank):
    return lax.broadcasted_iota(jnp.int32, (1,) * (rank - 1) + (128,), rank - 1)


def turn(value, steps):
    steps = steps % 128
    if steps == 0:
        return value
    flat = value.reshape(-1, 128)
    return pltpu.roll(flat, steps, 1).reshape(value.shape)


def blocks_exchanged(parts):
    lane = lane_of(parts[0].ndim)
    low = lane < 64
    even = (lane // 32) % 2 == 0
    first = [
        jnp.where(low, parts[0], turn(parts[2], 64)),
        jnp.where(low, parts[1], turn(parts[3], 64)),
        jnp.where(low, turn(parts[0], 64), parts[2]),
        jnp.where(low, turn(parts[1], 64), parts[3]),
    ]
    return [
        jnp.where(even, first[0], turn(first[1], 32)),
        jnp.where(even, turn(first[0], 96), first[1]),
        jnp.where(even, first[2], turn(first[3], 32)),
        jnp.where(even, turn(first[2], 96), first[3]),
    ]


def bspline(offsets, slopes):
    v = jnp.abs(offsets)
    a = jnp.maximum(2.0 - v, 0.0)
    b = jnp.maximum(1.0 - v, 0.0)
    aa = a * a
    bb = 4.0 * (b * b)
    weight = aa * a - bb * b
    if not slopes:
        return weight
    return weight, jnp.where(offsets < 0.0, bb - aa, aa - bb)


def rows_of_y():
    row = lax.broadcasted_iota(jnp.int32, (40, 128), 0)
    return jnp.where(row < 36, row, row - 4).astype(f32) - 1.0


def with_rims(rows):
    return jnp.concatenate([rows] + [rows[32:40]] * 3, 0)


def vmem(count):
    return [pl.BlockSpec(memory_space=VMEM)] * count


def targets(owner_row, apart):
    blocks = owner_row.shape[1]
    up = lax.broadcasted_iota(jnp.int32, (blocks, blocks), 0)
    across = lax.broadcasted_iota(jnp.int32, (blocks, blocks), 1)
    owner_column = jnp.sum(jnp.where(up == across, owner_row, 0).astype(f32), 1, keepdims=True)
    owner_float = owner_row.astype(f32)
    before = jnp.where((owner_column == owner_float) & (up < across), 1.0, 0.0)
    rank = jnp.sum(before, 0, keepdims=True)
    target = owner_float + OWN * rank if apart else 2.0 * owner_float + rank
    slot = lax.broadcasted_iota(jnp.int32, (2 * OWN, blocks), 0).astype(f32)
    return slot == target


def three(value):
    high = value.astype(bf16)
    rest = value - high.astype(f32)
    middle = rest.astype(bf16)
    return high, middle, (rest - middle.astype(f32)).astype(bf16)


def remote(src, dst, send_sem, recv_sem, device):
    return pltpu.make_async_remote_copy(
        src_ref=src, dst_ref=dst, send_sem=send_sem, recv_sem=recv_sem,
        device_id=device, device_id_type=MESH,
    )


def settle(ref, sem):
    pltpu.make_async_copy(ref, ref, sem).wait()


def atoms_kernel(
    owner_hbm, tile_hbm, cell_hbm, frac_hbm, charge_hbm, zone_hbm, slots_ref,
    owner_ref, tile_ref, cell_ref, frac_ref, charge_ref, zone_ref,
    payload, stage, stage_send, stage_recv, send_sem, recv_sem, own_sem, in_sem, lines_sem,
):
    loads = [
        pltpu.make_async_copy(src, dst, in_sem.at[i])
        for i, (src, dst) in enumerate(
            (
                (owner_hbm, owner_ref), (tile_hbm, tile_ref), (cell_hbm, cell_ref),
                (frac_hbm, frac_ref), (charge_hbm, charge_ref), (zone_hbm, zone_ref),
            )
        )
    ]
    for copy in loads:
        copy.start()
    bead, px, py = here()
    chunk = px * 8 + py
    barrier = pltpu.get_barrier_semaphore()

    crossing = [(bead, lax.rem(px + step, 8), py) for step in range(1, 8)]
    greeted = crossing + [(bead, px, lax.rem(py + step, 8)) for step in range(1, 8)]
    greeted += [(lax.rem(bead + step, 4), px, py) for step in range(1, 4)]
    for device in greeted:
        pl.semaphore_signal(barrier, inc=1, device_id=device, device_id_type=MESH)

    for copy in loads:
        copy.wait()
    chosen = jnp.where(targets(owner_ref[...], False), 1.0, 0.0).astype(bf16)
    blocks = cell_ref.shape[0]
    up = lax.broadcasted_iota(jnp.int32, (blocks, blocks), 0)
    across = lax.broadcasted_iota(jnp.int32, (blocks, blocks), 1)
    tile = jnp.sum(jnp.where(up == across, tile_ref[...], 0).astype(f32), 1, keepdims=True)
    tile = tile.astype(jnp.int32)
    cell = cell_ref[...]
    corners = [tile >> 7, (tile >> 5) & 3, tile & 31]
    cells = [cell >> 6, (cell >> 3) & 7, cell & 7]
    fields = [charge_ref[...] * zone_ref[...].astype(f32)]
    for axis in range(3):
        base = (corners[axis] * 8).astype(f32)
        inside = cells[axis].astype(f32) + frac_ref[axis]
        fields.append(base + jnp.minimum(inside, 8.0 - 2.0**-16))
    for place_in, field in enumerate(fields):
        parts = three(field)
        moved = sum(
            jnp.dot(chosen, part, preferred_element_type=f32) for part in reversed(parts)
        )
        payload[pl.ds(place_in, 2 * OWN, stride=4), :] = moved

    pl.semaphore_wait(barrier, 17)
    for device in crossing:
        pl.semaphore_signal(lines_sem, inc=1, device_id=device, device_id_type=MESH)
    staged = []
    for half in range(2):
        for step in (1, 3, 2):
            other = lax.rem(bead + step, 4)
            start = pl.multiple_of(other * 128 + half * 64, 64)
            sem = 2 * (step - 1) + half
            copy = remote(
                payload.at[pl.ds(start, 64)], stage.at[bead, half * 64 : half * 64 + 64],
                stage_send.at[sem], stage_recv.at[sem], (other, px, py),
            )
            staged.append((step, half, copy))
            copy.start()

    mark = pl.ds(pl.multiple_of(chunk * 8, 8), 8)
    pl.semaphore_wait(lines_sem, 7)

    def deliver_half(turn_of, half):
        from_bead = lax.rem(bead + turn_of, 4)

        def piece_of(step):
            j = 8 * half + lax.rem(step + 2 * px + py % 2 + 4 * (py // 2 - from_bead) + 16, 8)
            at = pl.multiple_of(j * 8, 8)
            if turn_of == 0:
                piece = payload.at[pl.ds(pl.multiple_of(bead * 128 + at, 8), 8)]
            else:
                piece = stage.at[from_bead, pl.ds(at, 8)]
            return piece, (bead, j // 2, 2 * from_bead + j % 2)

        def send(step, carry):
            piece, device = piece_of(step)
            remote(piece, slots_ref.at[mark], send_sem, recv_sem, device).start()
            return carry

        mine = jnp.logical_and(from_bead == py // 2, px // 4 == half)

        @pl.when(mine)
        def _():
            pltpu.make_async_copy(piece_of(0)[0], slots_ref.at[mark], own_sem).start()

        @pl.when(jnp.logical_not(mine))
        def _():
            send(0, 0)

        lax.fori_loop(1, 8, send, 0, unroll=7)

    for half in range(2):
        deliver_half(0, half)
    for step, half, copy in staged:
        copy.wait_recv()
        deliver_half(4 - step, half)
    settle(slots_ref.at[mark], own_sem)
    rest = pl.ds(0, 8 * OWN - 8)
    settle(slots_ref.at[rest], recv_sem)
    settle(slots_ref.at[rest], send_sem)
    for _, _, copy in staged:
        copy.wait_send()


def atoms_to_slots(owner_row, tile_row, cell, frac, charge, zone):
    dma = pltpu.SemaphoreType.DMA
    return pl.pallas_call(
        atoms_kernel,
        out_shape=jax.ShapeDtypeStruct((8 * OWN, 128), f32),
        in_specs=[pl.BlockSpec(memory_space=HBM)] * 6,
        out_specs=pl.BlockSpec(memory_space=pl.ANY),
        scratch_shapes=[
            VMEM((1, OWN), jnp.int32), VMEM((1, OWN), jnp.int32), VMEM((OWN, 128), jnp.int32),
            VMEM((3, OWN, 128), f32), VMEM((OWN, 128), f32), VMEM((OWN, 128), jnp.int32),
            VMEM((8 * OWN, 128), f32), VMEM((4, 128, 128), f32),
            dma((6,)), dma((6,)), dma, dma, dma, dma((6,)), pltpu.SemaphoreType.REGULAR,
        ],
        compiler_params=pltpu.CompilerParams(
            collective_id=0, has_side_effects=True, vmem_limit_bytes=60 << 20
        ),
        name="atoms_to_slots",
    )(owner_row, tile_row, cell, frac, charge, zone)


def tile_codes(slots_ref):
    along_x = slots_ref[pl.ds(1, 2 * OWN, stride=4), :]
    along_z = slots_ref[pl.ds(3, 2 * OWN, stride=4), :]
    tile_x = (jnp.max(along_x, 1, keepdims=True) * 0.125).astype(jnp.int32)
    tile_z = (jnp.max(along_z, 1, keepdims=True) * 0.125).astype(jnp.int32)
    up = lax.broadcasted_iota(jnp.int32, (128, 128), 0)
    across = lax.broadcasted_iota(jnp.int32, (128, 128), 1)
    sub = lax.broadcasted_iota(jnp.int32, (8, 128), 0)
    value = jnp.zeros((8, 128), f32)
    columns = (256 * tile_x + tile_z, 8 * tile_x, 8 * tile_z)
    for place_in, column in enumerate(columns):
        row = jnp.sum(jnp.where(up == across, column.astype(f32), 0.0), 0, keepdims=True)
        value = jnp.where(sub == place_in, row, value)
    return value.astype(jnp.int32)


def spread_kernel(
    slots_hbm, out_hbm, codes_hbm, codes_scalar, slots_ref, density, codes, out_ref, sem, out_sem
):
    load = pltpu.make_async_copy(slots_hbm, slots_ref, sem.at[2])
    load.start()
    density[0:18] = jnp.zeros((18, 264, 128), f32)
    load.wait()
    codes[...] = tile_codes(slots_ref)
    copy = pltpu.make_async_copy(codes, codes_scalar, sem.at[0])
    copy.start()
    handed = pltpu.make_async_copy(codes, codes_hbm, sem.at[1])
    handed.start()
    density[18:36] = jnp.zeros((18, 264, 128), f32)
    copy.wait()
    rows16 = lax.broadcasted_iota(jnp.int32, (16, 128), 0).astype(f32) - 1.0
    rows40 = rows_of_y()

    def one(number, slot):
        plane_x, row_z = codes_scalar[1, number], codes_scalar[2, number]
        charge, at_x, at_y, at_z = [slot[i : i + 1] for i in range(4)]
        at_x = at_x - plane_x.astype(f32)
        at_z = at_z - row_z.astype(f32)
        weight_x = bspline(rows16 - at_x, False) * (charge * (1.0 / 216.0))
        weight_z = bspline(rows16 - at_z, False)
        weight_y = with_rims(bspline(rows40 - at_y, False))
        plane = jnp.concatenate([weight_x[i : i + 1] * weight_z for i in range(11)], 0)
        plane = jnp.concatenate(split(plane), 1)
        y_high, y_low = split(weight_y)
        left = jnp.concatenate([y_high, y_low], 0)
        right = jnp.concatenate([y_high, jnp.zeros((64, 128), bf16)], 0)
        both = jnp.concatenate([left, right], 1)
        out = lax.dot_general(plane, both, (((1,), (1,)), ((), ())), preferred_element_type=f32)
        return plane_x, row_z, out

    def put(plane_x, row_z, out):
        base = pl.multiple_of(row_z, 8)
        for i in range(11):
            density[plane_x + i, pl.ds(base, 16), :] += out[16 * i : 16 * i + 16]

    def step(index, carry):
        found = []
        for k in range(8):
            pair = slots_ref[pl.ds(pl.multiple_of(64 * index + 8 * k, 8), 8), :]
            for rank in range(2):
                found.append(one(16 * index + 2 * k + rank, pair[4 * rank : 4 * rank + 4]))
        for item in found:
            put(*item)
        return carry

    lax.fori_loop(0, 8, step, 0)

    lane = lane_of(2)
    lane_group = (lane // 4) % 8
    low = lane < 64
    even = (lane // 32) % 2 == 0

    def fold(plane, carry):
        density[plane, 0:8, :] += density[plane, 256:264, :]
        return carry

    lax.fori_loop(0, 36, fold, 0)

    def regroup(chunk, carry):
        here = pl.ds(pl.multiple_of(chunk * 32, 32), 32)
        rim = jnp.zeros((32, 128), f32)

        def keep(group, value):
            out_ref[group, here, :] = value

        for group in range(9):
            four = [density[4 * group + i, here, :] for i in range(4)]
            pair_even = jnp.where(low, four[0], four[2]) + turn(jnp.where(low, four[2], four[0]), 64)
            pair_odd = jnp.where(low, four[1], four[3]) + turn(jnp.where(low, four[3], four[1]), 64)
            pair_odd = turn(pair_odd, 32)
            main = jnp.where(even, pair_even, pair_odd)
            side = jnp.where(even, pair_odd, pair_even)
            if group < 8:
                keep(group, main)
                rim = jnp.where(lane_group == group, side, rim)
            else:
                last = lane >= 96
                corner = jnp.where(lane_group == 0, turn(side, 64), 0.0)
                corner = jnp.where(lane_group == 1, turn(side, 32), corner)
                corner = jnp.where(lane_group == 2, side, corner)
                keep(8, jnp.where(last, corner, main))
        keep(9, rim)
        pltpu.make_async_copy(out_ref.at[:, here, :], out_hbm.at[:, here, :], out_sem.at[chunk]).start()
        return carry

    lax.fori_loop(0, 8, regroup, 0)
    handed.wait()
    for chunk in range(8):
        here = pl.ds(32 * chunk, 32)
        pltpu.make_async_copy(out_ref.at[:, here, :], out_hbm.at[:, here, :], out_sem.at[chunk]).wait()


def spread(slots):
    return pl.pallas_call(
        spread_kernel,
        out_shape=[
            jax.ShapeDtypeStruct((10, 256, 128), f32),
            jax.ShapeDtypeStruct((8, 128), jnp.int32),
        ],
        in_specs=[pl.BlockSpec(memory_space=HBM)],
        out_specs=[pl.BlockSpec(memory_space=pl.ANY)] * 2,
        scratch_shapes=[
            SMEM((8, 128), jnp.int32),
            VMEM((8 * OWN, 128), f32),
            VMEM((36, 264, 128), f32),
            VMEM((8, 128), jnp.int32),
            VMEM((10, 256, 128), f32),
            pltpu.SemaphoreType.DMA((3,)),
            pltpu.SemaphoreType.DMA((8,)),
        ],
        compiler_params=pltpu.CompilerParams(vmem_limit_bytes=60 << 20),
        name="spread",
    )(slots)


TABLES = ("forward_z", "forward_y", "forward_x", "back_x", "fold_y", "back_z")
ROWS_OF = (0, 8, 24, 32)
RIMS_OF = (16, 17, 20, 21)


def here():
    return lax.axis_index("bead"), lax.axis_index("px"), lax.axis_index("py")


def place(number, bead):
    return (number // 16, (number // 2) % 8, 2 * bead + number % 2)


def hop(step):
    return lax.rem(step * 37, OWN)


def shifted(value, steps):
    if steps == 1:
        return jnp.concatenate([value[7:8], value[0:7]], 0)
    return jnp.concatenate([value[1:8], value[0:1]], 0)


def wave_kernel(
    codes_hbm, *rest,
):
    table_refs, rest = rest[:17], rest[17:]
    out_ref, rest = rest[0], rest[1:]
    table_vmem, rest = rest[:17], rest[17:]
    packed, fz_high, fz_low = table_vmem[:3]
    row_ref, slots_ref, frac_ref, owner_ref = table_vmem[13:]
    (
        lines, waves_in, waves_out, lines_in, plane, plane_rim,
        lines_z, last, field, force, force_in, table_sem, out_send, out_recv, back_send, back_recv,
        own_sem, force_send, force_recv, blocks_sem, before_ref, after_ref, bead_send, bead_recv,
        codes, codes_sem, lines_sem, packed_sem,
    ) = rest
    (fz, fy, fx, bx, fold, bz) = [(table_vmem[2 * i + 1], table_vmem[2 * i + 2]) for i in range(6)]
    bead, px, py = here()
    mine, grid_bead, chunk = bead * 16 + px * 2 + py % 2, py // 2, px * 8 + py
    same = bead == grid_bead
    barrier = pltpu.get_barrier_semaphore()

    table_copies = [
        pltpu.make_async_copy(table_refs[i], table_vmem[i], table_sem.at[i]) for i in range(1, 17)
    ]
    packed_copy = pltpu.make_async_copy(table_refs[0], packed, packed_sem)
    packed_copy.start()
    for copy in table_copies[:2]:
        copy.start()

    crossing = [(bead, lax.rem(px + step, 8), py) for step in range(1, 8)]
    across = bead * 2 + py % 2
    along = [lax.rem(across + step, 8) for step in range(1, 8)]
    greeted = crossing + [(other // 2, px, 2 * grid_bead + other % 2) for other in along]
    likes = [(bead, px, lax.rem(py + 2 * k, 8)) for k in range(1, 4)]
    for device in greeted + likes:
        pl.semaphore_signal(barrier, inc=1, device_id=device, device_id_type=MESH)
    for copy in table_copies[2:]:
        copy.start()
    fetched = pltpu.make_async_copy(codes_hbm, codes, codes_sem)
    fetched.start()
    pl.semaphore_wait(barrier, 17)
    for device in crossing:
        pl.semaphore_signal(lines_sem, inc=1, device_id=device, device_id_type=MESH)

    packed_copy.wait()
    for copy in table_copies[:2]:
        copy.wait()

    for pair in range(5):
        high, low = split(jnp.concatenate([packed[2 * pair], packed[2 * pair + 1]], 1))
        result = dots(fz[0][...], fz[1][...], high, low)
        for part in range(2):
            group = 2 * pair + part
            for c in range(4):
                start = ROWS_OF[c] + group if group < 8 else RIMS_OF[c] + 2 * (group - 8)
                lines[:, start, :] = result[64 * c : 64 * c + 64, 128 * part : 128 * part + 128]

    pl.semaphore_wait(lines_sem, 7)

    def own(src, dst, rows, sem):
        return pltpu.make_async_copy(src.at[mine, rows], dst.at[mine, rows], sem)

    def send_all(src, dst, rows, send_sem, recv_sem):
        def send(step, carry):
            other = lax.rem(mine + hop(step), OWN)
            remote(
                src.at[other, rows], dst.at[mine, rows], send_sem, recv_sem, place(other, grid_bead)
            ).start()
            return carry

        lax.fori_loop(1, OWN, send, 0, unroll=9)

    rest = pl.ds(0, OWN - 1)
    half_rows = (pl.ds(0, 20), pl.ds(20, 20))
    for n in range(2):
        own(lines, waves_in, half_rows[n], own_sem.at[n]).start()
        send_all(lines, waves_in, half_rows[n], out_send.at[n], out_recv.at[n])

    for like in likes:
        pl.semaphore_signal(blocks_sem, inc=1, device_id=like, device_id_type=MESH)
    for copy in table_copies[2:]:
        copy.wait()
    fetched.wait()
    chosen = jnp.where(targets(owner_ref[...], True), 1.0, 0.0).astype(bf16)

    lane = lane_of(3)
    sub = lax.broadcasted_iota(jnp.int32, (1, 8, 128), 1)
    lane_group = (lane // 4) % 8
    square_y, factor_y = row_ref[0:1, :], row_ref[1:2, :]
    up = lax.broadcasted_iota(jnp.int32, (256, 256), 0)
    across = lax.broadcasted_iota(jnp.int32, (256, 256), 1)
    square_x = jnp.sum(jnp.where(up == across, square_y, 0.0), 1, keepdims=True)
    factor_x = jnp.sum(jnp.where(up == across, factor_y, 0.0), 1, keepdims=True)
    mine_z = lax.broadcasted_iota(jnp.int32, (1, 256), 1) - 2 * mine

    for n in range(2):
        own(lines, waves_in, half_rows[n], own_sem.at[n]).wait()
        settle(waves_in.at[rest, half_rows[n]], out_recv.at[n])
        for q in range(2):
            padding = jnp.zeros((8, 4, 128), f32)
            extra = blocks_exchanged(
                [
                    jnp.concatenate(
                        [waves_in[pl.ds(4 * q + j, 8, stride=8), 16 + 4 * n : 20 + 4 * n, :], padding], 1
                    )
                    for j in range(4)
                ]
            )
            for half in range(2):
                c = 2 * n + half
                main = blocks_exchanged(
                    [
                        waves_in[pl.ds(4 * q + j, 8, stride=8), ROWS_OF[c] : ROWS_OF[c] + 8, :]
                        for j in range(4)
                    ]
                )
                for i in range(4):
                    value = main[i]
                    rim = jnp.where(lane_group == sub, extra[(i + 1) % 4][:, 2 + half : 3 + half, :], 0.0)
                    if i < 3:
                        value = value + jnp.where(sub == 0, shifted(extra[i][:, half : half + 1, :], 1), 0.0)
                        corner = shifted(extra[3][:, half : half + 1, :], 1)
                        rim = rim + jnp.where((sub == 0) & (lane_group == i), corner, 0.0)
                    lines_of = slice(64 * i, 64 * i + 64)
                    plane[half, lines_of, 128 * q : 128 * q + 128] = value.reshape(64, 128)
                    high, low = split(rim.reshape(64, 128))
                    plane_rim[half, lines_of, 128 * q : 128 * q + 128] = high
                    plane_rim[half, lines_of, 256 + 128 * q : 384 + 128 * q] = low

        real, imag = [
            dots(*split(plane[half] + product(plane_rim[half], fold[0][...])), fy[0][...], fy[1][...])
            for half in range(2)
        ]
        spec = jnp.concatenate(
            [real[:, :256] + imag[:, 256:], imag[:, :256] - real[:, 256:]], 1
        )
        both = dots(fx[0][...], fx[1][...], *split(spec))
        square_z = jnp.sum(jnp.where(mine_z == n, square_y, 0.0), 1, keepdims=True)
        factor_z = jnp.sum(jnp.where(mine_z == n, factor_y, 0.0), 1, keepdims=True)
        square = square_x + square_y + square_z
        green = factor_x * factor_y * (factor_z * (4.0 * math.pi))
        green = jnp.where(square > 0.0, green / jnp.where(square > 0.0, square, 1.0), 0.0)
        spec = jnp.concatenate(
            [
                (both[:256, :256] + both[256:, 256:]) * green,
                (both[:256, 256:] - both[256:, :256]) * green,
            ],
            1,
        )
        both = dots(bx[0][...], bx[1][...], *split(spec))
        spec = jnp.concatenate(
            [both[:256, :256] - both[256:, 256:], both[:256, 256:] + both[256:, :256]], 0
        )
        both = dots(*split(spec), fy[0][...], fy[1][...])
        back = [both[:256, :256] - both[256:, 256:], both[256:, :256] + both[:256, 256:]]
        back_rim = [product(jnp.concatenate(split(value), 1), fold[1][...]) for value in back]

        for q in range(2):
            extra = [jnp.zeros((8, 8, 128), f32) for _ in range(4)]
            for half in range(2):
                c = 2 * n + half
                main, corner = [], jnp.zeros((8, 1, 128), f32)
                for i in range(4):
                    lines_of = slice(64 * i, 64 * i + 64)
                    value = back[half][lines_of, 128 * q : 128 * q + 128].reshape(8, 8, 128)
                    rim = back_rim[half][lines_of, 128 * q : 128 * q + 128].reshape(8, 8, 128)
                    main.append(value)
                    if i < 3:
                        extra[i] = jnp.where(sub == half, shifted(value[:, 0:1, :], -1), extra[i])
                        corner = jnp.where(lane_group == i, shifted(rim[:, 0:1, :], -1), corner)
                    side = jnp.sum(jnp.where(lane_group == sub, rim, 0.0), 1, keepdims=True)
                    extra[(i + 1) % 4] = jnp.where(sub == 2 + half, side, extra[(i + 1) % 4])
                extra[3] = jnp.where(sub == half, corner, extra[3])
                main = blocks_exchanged(main)
                for j in range(4):
                    waves_out[pl.ds(4 * q + j, 8, stride=8), ROWS_OF[c] : ROWS_OF[c] + 8, :] = main[j]
            extra = blocks_exchanged(extra)
            for j in range(4):
                waves_out[pl.ds(4 * q + j, 8, stride=8), 16 + 4 * n : 20 + 4 * n, :] = extra[j][:, 0:4, :]
        own(waves_out, lines_in, half_rows[n], own_sem.at[2 + n]).start()
        send_all(waves_out, lines_in, half_rows[n], back_send.at[n], back_recv.at[n])

    for n in range(2):
        own(waves_out, lines_in, half_rows[n], own_sem.at[2 + n]).wait()
        settle(lines_in.at[rest, half_rows[n]], back_recv.at[n])

    for pair in range(5):
        columns = []
        for group in (2 * pair, 2 * pair + 1):
            starts = [
                ROWS_OF[c] + group if group < 8 else RIMS_OF[c] + 2 * (group - 8) for c in range(4)
            ]
            columns.append(jnp.concatenate([lines_in[:, start, :] for start in starts], 0))
        result = dots(bz[0][...], bz[1][...], *split(jnp.concatenate(columns, 1)))
        for part in range(2):
            lines_z[2 * pair + part, 0:256, :] = result[:, 128 * part : 128 * part + 128]
            lines_z[2 * pair + part, 256:264, :] = result[0:8, 128 * part : 128 * part + 128]

    lane = lane_of(2)
    lane_group = (lane // 4) % 8
    low_half = lane < 64
    even = (lane // 32) % 2 == 0

    def regroup(part, rows):
        at = pl.ds(pl.multiple_of(part * 32, 32), rows)
        rim = lines_z[9, at, :]
        for group in range(9):
            main = lines_z[group, at, :]
            if group < 8:
                side = jnp.where(lane_group == group, rim, 0.0)
            else:
                side = jnp.where((lane_group == 2) & (lane >= 96), main, 0.0)
                side = jnp.where((lane_group == 1) & (lane >= 64) & (lane < 96), turn(main, -32), side)
                side = jnp.where((lane_group == 0) & (lane >= 32) & (lane < 64), turn(main, -64), side)
            pair_even = jnp.where(even, main, side)
            pair_odd = turn(jnp.where(even, side, main), -32)
            for odd, value in enumerate((pair_even, pair_odd)):
                other = turn(value, 64)
                high = value.astype(bf16).astype(f32)
                high_other = other.astype(bf16).astype(f32)
                planes = (
                    jnp.where(low_half, high, other - high_other),
                    jnp.where(low_half, high_other, value - high),
                )
                for second in range(2):
                    plane_x = 4 * group + 2 * second + odd
                    whole = jnp.concatenate([last[plane_x], planes[second]], 0)
                    for k in range(rows // 8):
                        window = whole[8 * k : 8 * k + 16].astype(bf16)
                        field[plane_x * 32 + 4 * part + k] = window
                    last[plane_x] = planes[second][rows - 8 : rows]

    def regroup_step(part, carry):
        regroup(part, 32)
        return carry

    last[...] = jnp.zeros_like(last)
    lax.fori_loop(0, 8, regroup_step, 0)
    regroup(8, 8)

    rows16 = lax.broadcasted_iota(jnp.int32, (16, 128), 0).astype(f32) - 1.0
    rows40 = rows_of_y()

    def one(number, slot):
        charge, at_x, at_y, at_z = [slot[i : i + 1] for i in range(4)]
        at_x = at_x - codes[1, number].astype(f32)
        at_z = at_z - codes[2, number].astype(f32)
        weight_x, slope_x = bspline(rows16 - at_x, True)
        weight_z, slope_z = bspline(rows16 - at_z, True)
        along_y = jnp.concatenate(bspline(rows40 - at_y, True), 1)
        y_high, y_low = split(with_rims(along_y))
        both = jnp.concatenate([y_high, y_high, y_low, y_low], 0)
        base = codes[0, number]
        window = jnp.concatenate([field[base + 32 * i + 1] for i in range(11)], 0)
        out = jnp.dot(jnp.concatenate([window, window], 1), both, preferred_element_type=f32)
        plain = jnp.zeros((16, 128), f32)
        along_x = jnp.zeros((16, 128), f32)
        sloped = jnp.zeros((16, 128), f32)
        for i in range(11):
            value = out[16 * i : 16 * i + 16, :128]
            slope = out[16 * i : 16 * i + 16, 128:]
            plain = plain + weight_x[i : i + 1] * value
            along_x = along_x + slope_x[i : i + 1] * value
            sloped = sloped + weight_x[i : i + 1] * slope
        minus = charge * (-1.0 / 72.0)
        return jnp.concatenate(
            [
                minus * jnp.sum(along_x * weight_z, 0, keepdims=True),
                minus * jnp.sum(sloped * weight_z, 0, keepdims=True),
                minus * jnp.sum(plain * slope_z, 0, keepdims=True),
                charge,
            ],
            0,
        )

    def source_at(n):
        return lax.rem(chunk + hop(OWN - 1 - n), OWN)

    def interpolate(step):
        sources = [source_at(4 * step + k) for k in range(4)]
        found = []
        for source in sources:
            pair = slots_ref[pl.ds(pl.multiple_of(8 * source, 8), 8), :]
            found.append(
                jnp.concatenate([one(2 * source, pair[0:4]), one(2 * source + 1, pair[4:8])], 0)
            )
        for source, value in zip(sources, found):
            force[source] = value

    def send_force(source):
        remote(
            force.at[source], force_in.at[mine], force_send, force_recv,
            (grid_bead, source // 8, source % 8),
        ).start()

    pl.semaphore_wait(blocks_sem, 3)
    springs = [
        remote(frac_ref, target, bead_send.at[i], bead_recv.at[i], (lax.rem(bead + step, 4), px, py))
        for i, (target, step) in enumerate(((before_ref, 1), (after_ref, 3)))
    ]
    for copy in springs:
        copy.start()
    def send_forces(step, count):
        for k in range(count):
            send_force(source_at(4 * step + k))

    def interpolate_step(step, carry):
        interpolate(step)
        send_forces(step - 1, 4)
        return carry

    interpolate(0)
    lax.fori_loop(1, OWN // 4, interpolate_step, 0)
    send_forces(OWN // 4 - 1, 3)

    @pl.when(same)
    def _():
        pltpu.make_async_copy(force.at[chunk], force_in.at[mine], own_sem.at[4]).start()

    @pl.when(jnp.logical_not(same))
    def _():
        send_force(chunk)

    for copy in springs:
        copy.wait()
    bends = [2.0 * frac_ref[i] - before_ref[i] - after_ref[i] for i in range(3)]

    @pl.when(same)
    def _():
        settle(force_in.at[mine], own_sem.at[4])
        settle(force_in.at[rest], force_recv)
        settle(force_in.at[rest], force_send)

    @pl.when(jnp.logical_not(same))
    def _():
        settle(force_in, force_recv)
        settle(force_in, force_send)

    for axis in range(3):
        both = jnp.concatenate([force_in[:, axis, :], force_in[:, 4 + axis, :]], 0)
        moved = sum(
            lax.dot_general(chosen, part, (((0,), (0,)), ((), ())), preferred_element_type=f32)
            for part in reversed(three(both))
        )
        out_ref[axis] = moved - spring_scale * bends[axis]

    for n in range(2):
        settle(lines.at[rest, half_rows[n]], out_send.at[n])
        settle(waves_out.at[rest, half_rows[n]], back_send.at[n])


def grid_to_forces(codes, packed, slots, frac, owner_row):
    table = tables()
    consts = [packed] + [jnp.asarray(half) for name in TABLES for half in table[name]]
    consts += [jnp.asarray(table["row"]), slots, frac, owner_row]
    dma = pltpu.SemaphoreType.DMA
    chunks = VMEM((OWN, 40, 128), f32)
    return pl.pallas_call(
        wave_kernel,
        out_shape=jax.ShapeDtypeStruct((3, OWN, 128), f32),
        in_specs=[pl.BlockSpec(memory_space=HBM)] * 18,
        out_specs=pl.BlockSpec(memory_space=VMEM),
        scratch_shapes=[VMEM(const.shape, const.dtype) for const in consts]
        + [
            chunks, chunks, chunks, chunks,
            VMEM((2, 256, 256), f32), VMEM((2, 256, 512), bf16),
            VMEM((10, 264, 128), f32), VMEM((36, 8, 128), f32), VMEM((36 * 32 + 1, 16, 128), bf16),
            VMEM((OWN, 8, 128), f32), VMEM((OWN, 8, 128), f32),
            dma((17,)), dma((2,)), dma((2,)), dma((2,)), dma((2,)), dma((5,)), dma, dma,
            pltpu.SemaphoreType.REGULAR,
            VMEM((3, OWN, 128), f32), VMEM((3, OWN, 128), f32), dma((2,)), dma((2,)),
            SMEM((8, 128), jnp.int32), dma, pltpu.SemaphoreType.REGULAR, dma,
        ],
        compiler_params=pltpu.CompilerParams(
            collective_id=1, has_side_effects=True, vmem_limit_bytes=60 << 20
        ),
        name="grid_to_forces",
    )(
        codes, *consts,
    )


def local(block_owner, block_tile, atom_cell, atom_frac, charge, zone):
    owner_row = block_owner.reshape(1, OWN)
    frac = jnp.transpose(atom_frac[0], (1, 0, 2))
    slots = atoms_to_slots(
        owner_row, block_tile.reshape(1, OWN), atom_cell, frac, charge, zone
    )
    packed, codes = spread(slots)
    total = grid_to_forces(codes, packed, slots, frac, owner_row)
    return jnp.transpose(total, (1, 0, 2))[None]


def solution(mesh):
    return jax.shard_map(
        local,
        mesh=mesh,
        in_specs=(
            P(("px", "py"), None),
            P(("px", "py")),
            P(("px", "py"), None),
            P("bead", ("px", "py"), None, None),
            P(("px", "py"), None),
            P(("px", "py"), None),
        ),
        out_specs=P("bead", ("px", "py"), None, None),
        check_vma=False,
    )
```

```python
import functools
import math

import jax
import jax.numpy as jnp
import ml_dtypes
import numpy as np
from jax import lax
from jax.experimental import pallas as pl
from jax.experimental.pallas import tpu as pltpu
from jax.sharding import PartitionSpec as P

NG = 256
OWN = 64
f32 = jnp.float32
bf16 = jnp.bfloat16
MESH = pl.DeviceIdType.MESH
VMEM = pltpu.VMEM
SMEM = pltpu.SMEM
HBM = pltpu.HBM
ewald_beta = 0.75
spring_scale = 0.25


def halves(table):
    table = table.astype(np.float32)
    high = table.astype(ml_dtypes.bfloat16)
    low = (table - high.astype(np.float32)).astype(ml_dtypes.bfloat16)
    return high, low


def waves(rows, columns):
    angle = (np.outer(rows, columns) % NG) * (2.0 * math.pi / NG)
    return np.cos(angle), np.sin(angle)


@functools.lru_cache(None)
def tables():
    whole = np.arange(NG)
    owner = np.arange(OWN)
    kz = np.stack([2 * owner, 2 * owner + 1])
    cos_z, sin_z = waves(kz.reshape(-1), whole)
    forward_z = np.concatenate([cos_z[:OWN], -sin_z[:OWN], cos_z[OWN:], -sin_z[OWN:]])
    scale = np.where(kz == 0, 1.0, 2.0) / float(NG**3)
    scale = np.repeat(scale, 2, 0).reshape(-1)
    back_z = (forward_z * scale[:, None]).T
    forward_y = np.concatenate(waves(whole, whole), 1)
    rim = (32 * (whole // 32 + 1) + whole % 4) % NG
    fold_y = np.concatenate([rim[:, None] == whole[None, :]] * 2).astype(ml_dtypes.bfloat16)
    unfold_y = np.concatenate([whole[:, None] == rim[None, :]] * 2).astype(ml_dtypes.bfloat16)
    step, block, group = np.meshgrid(np.arange(4), np.arange(8), np.arange(8), indexing="ij")
    place = (32 * block + 4 * group + step).reshape(-1)
    cos_x, sin_x = waves(whole, place)
    forward_x = np.concatenate([cos_x, sin_x])
    back_x = np.concatenate([cos_x.T, sin_x.T])
    wave = (whole + NG // 2) % NG - NG // 2
    theta = wave * (2.0 * math.pi / NG)
    factor = (6.0 / (4.0 + 2.0 * np.cos(theta))) ** 2
    factor = factor * np.exp(-theta * theta / (4.0 * ewald_beta * ewald_beta))
    row = np.zeros((8, 256), np.float32)
    row[0], row[1] = theta * theta, factor
    return dict(
        forward_z=halves(forward_z),
        back_z=halves(back_z),
        forward_y=halves(forward_y),
        fold_y=(fold_y, unfold_y),
        forward_x=halves(forward_x),
        back_x=halves(back_x),
        row=row,
    )


def split(value):
    high = value.astype(bf16)
    return high, (value - high.astype(f32)).astype(bf16)


product = functools.partial(jnp.dot, preferred_element_type=f32)


def dots(a_high, a_low, b_high, b_low):
    return product(a_high, b_high) + (product(a_high, b_low) + product(a_low, b_high))


def lane_of(rank):
    return lax.broadcasted_iota(jnp.int32, (1,) * (rank - 1) + (128,), rank - 1)


def turn(value, steps):
    steps = steps % 128
    if steps == 0:
        return value
    flat = value.reshape(-1, 128)
    return pltpu.roll(flat, steps, 1).reshape(value.shape)


def blocks_exchanged(parts):
    lane = lane_of(parts[0].ndim)
    low = lane < 64
    even = (lane // 32) % 2 == 0
    first = [
        jnp.where(low, parts[0], turn(parts[2], 64)),
        jnp.where(low, parts[1], turn(parts[3], 64)),
        jnp.where(low, turn(parts[0], 64), parts[2]),
        jnp.where(low, turn(parts[1], 64), parts[3]),
    ]
    return [
        jnp.where(even, first[0], turn(first[1], 32)),
        jnp.where(even, turn(first[0], 96), first[1]),
        jnp.where(even, first[2], turn(first[3], 32)),
        jnp.where(even, turn(first[2], 96), first[3]),
    ]


def bspline(offsets, slopes):
    v = jnp.abs(offsets)
    a = jnp.maximum(2.0 - v, 0.0)
    b = jnp.maximum(1.0 - v, 0.0)
    aa = a * a
    bb = 4.0 * (b * b)
    weight = aa * a - bb * b
    if not slopes:
        return weight
    return weight, jnp.where(offsets < 0.0, bb - aa, aa - bb)


def rows_of_y():
    row = lax.broadcasted_iota(jnp.int32, (40, 128), 0)
    return jnp.where(row < 36, row, row - 4).astype(f32) - 1.0


def with_rims(rows):
    return jnp.concatenate([rows] + [rows[32:40]] * 3, 0)


def vmem(count):
    return [pl.BlockSpec(memory_space=VMEM)] * count


def targets(owner_row, apart):
    blocks = owner_row.shape[1]
    up = lax.broadcasted_iota(jnp.int32, (blocks, blocks), 0)
    across = lax.broadcasted_iota(jnp.int32, (blocks, blocks), 1)
    owner_column = jnp.sum(jnp.where(up == across, owner_row, 0).astype(f32), 1, keepdims=True)
    owner_float = owner_row.astype(f32)
    before = jnp.where((owner_column == owner_float) & (up < across), 1.0, 0.0)
    rank = jnp.sum(before, 0, keepdims=True)
    target = owner_float + OWN * rank if apart else 2.0 * owner_float + rank
    slot = lax.broadcasted_iota(jnp.int32, (2 * OWN, blocks), 0).astype(f32)
    return slot == target


def three(value):
    high = value.astype(bf16)
    rest = value - high.astype(f32)
    middle = rest.astype(bf16)
    return high, middle, (rest - middle.astype(f32)).astype(bf16)


def remote(src, dst, send_sem, recv_sem, device):
    return pltpu.make_async_remote_copy(
        src_ref=src, dst_ref=dst, send_sem=send_sem, recv_sem=recv_sem,
        device_id=device, device_id_type=MESH,
    )


def settle(ref, sem):
    pltpu.make_async_copy(ref, ref, sem).wait()


def atoms_kernel(
    owner_hbm, tile_hbm, cell_hbm, frac_hbm, charge_hbm, zone_hbm, slots_ref,
    owner_ref, tile_ref, cell_ref, frac_ref, charge_ref, zone_ref,
    payload, stage, stage_send, stage_recv, send_sem, recv_sem, own_sem, in_sem, lines_sem,
):
    loads = [
        pltpu.make_async_copy(src, dst, in_sem.at[i])
        for i, (src, dst) in enumerate(
            (
                (owner_hbm, owner_ref), (tile_hbm, tile_ref), (cell_hbm, cell_ref),
                (frac_hbm, frac_ref), (charge_hbm, charge_ref), (zone_hbm, zone_ref),
            )
        )
    ]
    for copy in loads:
        copy.start()
    bead, px, py = here()
    chunk = px * 8 + py
    barrier = pltpu.get_barrier_semaphore()

    crossing = [(bead, lax.rem(px + step, 8), py) for step in range(1, 8)]
    greeted = crossing + [(bead, px, lax.rem(py + step, 8)) for step in range(1, 8)]
    greeted += [(lax.rem(bead + step, 4), px, py) for step in range(1, 4)]
    for device in greeted:
        pl.semaphore_signal(barrier, inc=1, device_id=device, device_id_type=MESH)

    for copy in loads:
        copy.wait()
    chosen = jnp.where(targets(owner_ref[...], False), 1.0, 0.0).astype(bf16)
    blocks = cell_ref.shape[0]
    up = lax.broadcasted_iota(jnp.int32, (blocks, blocks), 0)
    across = lax.broadcasted_iota(jnp.int32, (blocks, blocks), 1)
    tile = jnp.sum(jnp.where(up == across, tile_ref[...], 0).astype(f32), 1, keepdims=True)
    tile = tile.astype(jnp.int32)
    cell = cell_ref[...]
    corners = [tile >> 7, (tile >> 5) & 3, tile & 31]
    cells = [cell >> 6, (cell >> 3) & 7, cell & 7]
    fields = [charge_ref[...] * zone_ref[...].astype(f32)]
    for axis in range(3):
        base = (corners[axis] * 8).astype(f32)
        inside = cells[axis].astype(f32) + frac_ref[axis]
        fields.append(base + jnp.minimum(inside, 8.0 - 2.0**-16))
    for place_in, field in enumerate(fields):
        parts = three(field)
        moved = sum(
            jnp.dot(chosen, part, preferred_element_type=f32) for part in reversed(parts)
        )
        payload[pl.ds(place_in, 2 * OWN, stride=4), :] = moved

    pl.semaphore_wait(barrier, 17)
    for device in crossing:
        pl.semaphore_signal(lines_sem, inc=1, device_id=device, device_id_type=MESH)
    staged = []
    for half in range(2):
        for step in (1, 3, 2):
            other = lax.rem(bead + step, 4)
            start = pl.multiple_of(other * 128 + half * 64, 64)
            sem = 2 * (step - 1) + half
            copy = remote(
                payload.at[pl.ds(start, 64)], stage.at[bead, half * 64 : half * 64 + 64],
                stage_send.at[sem], stage_recv.at[sem], (other, px, py),
            )
            staged.append((step, half, copy))
            copy.start()

    mark = pl.ds(pl.multiple_of(chunk * 8, 8), 8)
    pl.semaphore_wait(lines_sem, 7)

    def deliver_half(turn_of, half):
        from_bead = lax.rem(bead + turn_of, 4)

        def piece_of(step):
            j = 8 * half + lax.rem(step + 2 * px + py % 2 + 4 * (py // 2 - from_bead) + 16, 8)
            at = pl.multiple_of(j * 8, 8)
            if turn_of == 0:
                piece = payload.at[pl.ds(pl.multiple_of(bead * 128 + at, 8), 8)]
            else:
                piece = stage.at[from_bead, pl.ds(at, 8)]
            return piece, (bead, j // 2, 2 * from_bead + j % 2)

        def send(step, carry):
            piece, device = piece_of(step)
            remote(piece, slots_ref.at[mark], send_sem, recv_sem, device).start()
            return carry

        mine = jnp.logical_and(from_bead == py // 2, px // 4 == half)

        @pl.when(mine)
        def _():
            pltpu.make_async_copy(piece_of(0)[0], slots_ref.at[mark], own_sem).start()

        @pl.when(jnp.logical_not(mine))
        def _():
            send(0, 0)

        lax.fori_loop(1, 8, send, 0, unroll=7)

    for half in range(2):
        deliver_half(0, half)
    for step, half, copy in staged:
        copy.wait_recv()
        deliver_half(4 - step, half)
    settle(slots_ref.at[mark], own_sem)
    rest = pl.ds(0, 8 * OWN - 8)
    settle(slots_ref.at[rest], recv_sem)
    settle(slots_ref.at[rest], send_sem)
    for _, _, copy in staged:
        copy.wait_send()


def atoms_to_slots(owner_row, tile_row, cell, frac, charge, zone):
    dma = pltpu.SemaphoreType.DMA
    return pl.pallas_call(
        atoms_kernel,
        out_shape=jax.ShapeDtypeStruct((8 * OWN, 128), f32),
        in_specs=[pl.BlockSpec(memory_space=HBM)] * 6,
        out_specs=pl.BlockSpec(memory_space=pl.ANY),
        scratch_shapes=[
            VMEM((1, OWN), jnp.int32), VMEM((1, OWN), jnp.int32), VMEM((OWN, 128), jnp.int32),
            VMEM((3, OWN, 128), f32), VMEM((OWN, 128), f32), VMEM((OWN, 128), jnp.int32),
            VMEM((8 * OWN, 128), f32), VMEM((4, 128, 128), f32),
            dma((6,)), dma((6,)), dma, dma, dma, dma((6,)), pltpu.SemaphoreType.REGULAR,
        ],
        compiler_params=pltpu.CompilerParams(
            collective_id=0, has_side_effects=True, vmem_limit_bytes=60 << 20
        ),
        name="atoms_to_slots",
    )(owner_row, tile_row, cell, frac, charge, zone)


def tile_codes(slots_ref):
    along_x = slots_ref[pl.ds(1, 2 * OWN, stride=4), :]
    along_z = slots_ref[pl.ds(3, 2 * OWN, stride=4), :]
    tile_x = (jnp.max(along_x, 1, keepdims=True) * 0.125).astype(jnp.int32)
    tile_z = (jnp.max(along_z, 1, keepdims=True) * 0.125).astype(jnp.int32)
    up = lax.broadcasted_iota(jnp.int32, (128, 128), 0)
    across = lax.broadcasted_iota(jnp.int32, (128, 128), 1)
    sub = lax.broadcasted_iota(jnp.int32, (8, 128), 0)
    value = jnp.zeros((8, 128), f32)
    columns = (256 * tile_x + tile_z, 8 * tile_x, 8 * tile_z)
    for place_in, column in enumerate(columns):
        row = jnp.sum(jnp.where(up == across, column.astype(f32), 0.0), 0, keepdims=True)
        value = jnp.where(sub == place_in, row, value)
    return value.astype(jnp.int32)


def spread_kernel(
    slots_hbm, out_hbm, codes_hbm, codes_scalar, slots_ref, density, codes, out_ref, sem, out_sem
):
    load = pltpu.make_async_copy(slots_hbm, slots_ref, sem.at[2])
    load.start()
    density[0:18] = jnp.zeros((18, 264, 128), f32)
    load.wait()
    codes[...] = tile_codes(slots_ref)
    copy = pltpu.make_async_copy(codes, codes_scalar, sem.at[0])
    copy.start()
    handed = pltpu.make_async_copy(codes, codes_hbm, sem.at[1])
    handed.start()
    density[18:36] = jnp.zeros((18, 264, 128), f32)
    copy.wait()
    rows16 = lax.broadcasted_iota(jnp.int32, (16, 128), 0).astype(f32) - 1.0
    rows40 = rows_of_y()

    def one(number, slot):
        plane_x, row_z = codes_scalar[1, number], codes_scalar[2, number]
        charge, at_x, at_y, at_z = [slot[i : i + 1] for i in range(4)]
        at_x = at_x - plane_x.astype(f32)
        at_z = at_z - row_z.astype(f32)
        weight_x = bspline(rows16 - at_x, False) * (charge * (1.0 / 216.0))
        weight_z = bspline(rows16 - at_z, False)
        weight_y = with_rims(bspline(rows40 - at_y, False))
        plane = jnp.concatenate([weight_x[i : i + 1] * weight_z for i in range(11)], 0)
        plane = jnp.concatenate(split(plane), 1)
        y_high, y_low = split(weight_y)
        left = jnp.concatenate([y_high, y_low], 0)
        right = jnp.concatenate([y_high, jnp.zeros((64, 128), bf16)], 0)
        both = jnp.concatenate([left, right], 1)
        out = lax.dot_general(plane, both, (((1,), (1,)), ((), ())), preferred_element_type=f32)
        return plane_x, row_z, out

    def put(plane_x, row_z, out):
        base = pl.multiple_of(row_z, 8)
        for i in range(11):
            density[plane_x + i, pl.ds(base, 16), :] += out[16 * i : 16 * i + 16]

    def step(index, carry):
        found = []
        for k in range(8):
            pair = slots_ref[pl.ds(pl.multiple_of(64 * index + 8 * k, 8), 8), :]
            for rank in range(2):
                found.append(one(16 * index + 2 * k + rank, pair[4 * rank : 4 * rank + 4]))
        for item in found:
            put(*item)
        return carry

    lax.fori_loop(0, 8, step, 0)

    lane = lane_of(2)
    lane_group = (lane // 4) % 8
    low = lane < 64
    even = (lane // 32) % 2 == 0

    def fold(plane, carry):
        density[plane, 0:8, :] += density[plane, 256:264, :]
        return carry

    lax.fori_loop(0, 36, fold, 0)

    def regroup(chunk, carry):
        here = pl.ds(pl.multiple_of(chunk * 32, 32), 32)
        rim = jnp.zeros((32, 128), f32)

        def keep(group, value):
            out_ref[group, here, :] = value

        for group in range(9):
            four = [density[4 * group + i, here, :] for i in range(4)]
            pair_even = jnp.where(low, four[0], four[2]) + turn(jnp.where(low, four[2], four[0]), 64)
            pair_odd = jnp.where(low, four[1], four[3]) + turn(jnp.where(low, four[3], four[1]), 64)
            pair_odd = turn(pair_odd, 32)
            main = jnp.where(even, pair_even, pair_odd)
            side = jnp.where(even, pair_odd, pair_even)
            if group < 8:
                keep(group, main)
                rim = jnp.where(lane_group == group, side, rim)
            else:
                last = lane >= 96
                corner = jnp.where(lane_group == 0, turn(side, 64), 0.0)
                corner = jnp.where(lane_group == 1, turn(side, 32), corner)
                corner = jnp.where(lane_group == 2, side, corner)
                keep(8, jnp.where(last, corner, main))
        keep(9, rim)
        pltpu.make_async_copy(out_ref.at[:, here, :], out_hbm.at[:, here, :], out_sem.at[chunk]).start()
        return carry

    lax.fori_loop(0, 8, regroup, 0)
    handed.wait()
    for chunk in range(8):
        here = pl.ds(32 * chunk, 32)
        pltpu.make_async_copy(out_ref.at[:, here, :], out_hbm.at[:, here, :], out_sem.at[chunk]).wait()


def spread(slots):
    return pl.pallas_call(
        spread_kernel,
        out_shape=[
            jax.ShapeDtypeStruct((10, 256, 128), f32),
            jax.ShapeDtypeStruct((8, 128), jnp.int32),
        ],
        in_specs=[pl.BlockSpec(memory_space=HBM)],
        out_specs=[pl.BlockSpec(memory_space=pl.ANY)] * 2,
        scratch_shapes=[
            SMEM((8, 128), jnp.int32),
            VMEM((8 * OWN, 128), f32),
            VMEM((36, 264, 128), f32),
            VMEM((8, 128), jnp.int32),
            VMEM((10, 256, 128), f32),
            pltpu.SemaphoreType.DMA((3,)),
            pltpu.SemaphoreType.DMA((8,)),
        ],
        compiler_params=pltpu.CompilerParams(vmem_limit_bytes=60 << 20),
        name="spread",
    )(slots)


TABLES = ("forward_z", "forward_y", "forward_x", "back_x", "fold_y", "back_z")
ROWS_OF = (0, 8, 24, 32)
RIMS_OF = (16, 17, 20, 21)


def here():
    return lax.axis_index("bead"), lax.axis_index("px"), lax.axis_index("py")


def place(number, bead):
    return (number // 16, (number // 2) % 8, 2 * bead + number % 2)


def hop(step):
    return lax.rem(step * 37, OWN)


def shifted(value, steps):
    if steps == 1:
        return jnp.concatenate([value[7:8], value[0:7]], 0)
    return jnp.concatenate([value[1:8], value[0:1]], 0)


def wave_kernel(
    codes_hbm, *rest,
):
    table_refs, rest = rest[:17], rest[17:]
    out_ref, rest = rest[0], rest[1:]
    table_vmem, rest = rest[:17], rest[17:]
    packed, fz_high, fz_low = table_vmem[:3]
    row_ref, slots_ref, frac_ref, owner_ref = table_vmem[13:]
    (
        lines, waves_in, waves_out, lines_in, plane, plane_rim,
        lines_z, last, field, force, force_in, table_sem, out_send, out_recv, back_send, back_recv,
        own_sem, force_send, force_recv, blocks_sem, before_ref, after_ref, bead_send, bead_recv,
        codes, codes_sem, lines_sem, packed_sem,
    ) = rest
    (fz, fy, fx, bx, fold, bz) = [(table_vmem[2 * i + 1], table_vmem[2 * i + 2]) for i in range(6)]
    bead, px, py = here()
    mine, grid_bead, chunk = bead * 16 + px * 2 + py % 2, py // 2, px * 8 + py
    same = bead == grid_bead
    barrier = pltpu.get_barrier_semaphore()

    table_copies = [
        pltpu.make_async_copy(table_refs[i], table_vmem[i], table_sem.at[i]) for i in range(1, 17)
    ]
    packed_copy = pltpu.make_async_copy(table_refs[0], packed, packed_sem)
    packed_copy.start()
    for copy in table_copies[:2]:
        copy.start()

    crossing = [(bead, lax.rem(px + step, 8), py) for step in range(1, 8)]
    across = bead * 2 + py % 2
    along = [lax.rem(across + step, 8) for step in range(1, 8)]
    greeted = crossing + [(other // 2, px, 2 * grid_bead + other % 2) for other in along]
    likes = [(bead, px, lax.rem(py + 2 * k, 8)) for k in range(1, 4)]
    for device in greeted + likes:
        pl.semaphore_signal(barrier, inc=1, device_id=device, device_id_type=MESH)
    for copy in table_copies[2:]:
        copy.start()
    fetched = pltpu.make_async_copy(codes_hbm, codes, codes_sem)
    fetched.start()
    pl.semaphore_wait(barrier, 17)
    for device in crossing:
        pl.semaphore_signal(lines_sem, inc=1, device_id=device, device_id_type=MESH)

    packed_copy.wait()
    for copy in table_copies[:2]:
        copy.wait()

    def own(src, dst, rows, sem):
        return pltpu.make_async_copy(src.at[mine, rows], dst.at[mine, rows], sem)

    def send_all(src, dst, rows, send_sem, recv_sem):
        def send(step, carry):
            other = lax.rem(mine + hop(step), OWN)
            remote(
                src.at[other, rows], dst.at[mine, rows], send_sem, recv_sem, place(other, grid_bead)
            ).start()
            return carry

        lax.fori_loop(1, OWN, send, 0, unroll=9)

    rest = pl.ds(0, OWN - 1)
    half_rows = (pl.ds(0, 20), pl.ds(20, 20))
    for n in range(2):
        mine_of = slice(128 * n, 128 * n + 128)
        for pair in range(5):
            high, low = split(jnp.concatenate([packed[2 * pair], packed[2 * pair + 1]], 1))
            result = dots(fz[0][mine_of, :], fz[1][mine_of, :], high, low)
            for part in range(2):
                group = 2 * pair + part
                for half in range(2):
                    c = 2 * n + half
                    start = ROWS_OF[c] + group if group < 8 else RIMS_OF[c] + 2 * (group - 8)
                    lines[:, start, :] = result[
                        64 * half : 64 * half + 64, 128 * part : 128 * part + 128
                    ]
        if n == 0:
            pl.semaphore_wait(lines_sem, 7)
        own(lines, waves_in, half_rows[n], own_sem.at[n]).start()
        send_all(lines, waves_in, half_rows[n], out_send.at[n], out_recv.at[n])

    for like in likes:
        pl.semaphore_signal(blocks_sem, inc=1, device_id=like, device_id_type=MESH)
    for copy in table_copies[2:]:
        copy.wait()
    fetched.wait()
    chosen = jnp.where(targets(owner_ref[...], True), 1.0, 0.0).astype(bf16)

    lane = lane_of(3)
    sub = lax.broadcasted_iota(jnp.int32, (1, 8, 128), 1)
    lane_group = (lane // 4) % 8
    square_y, factor_y = row_ref[0:1, :], row_ref[1:2, :]
    up = lax.broadcasted_iota(jnp.int32, (256, 256), 0)
    across = lax.broadcasted_iota(jnp.int32, (256, 256), 1)
    square_x = jnp.sum(jnp.where(up == across, square_y, 0.0), 1, keepdims=True)
    factor_x = jnp.sum(jnp.where(up == across, factor_y, 0.0), 1, keepdims=True)
    mine_z = lax.broadcasted_iota(jnp.int32, (1, 256), 1) - 2 * mine

    for n in range(2):
        own(lines, waves_in, half_rows[n], own_sem.at[n]).wait()
        settle(waves_in.at[rest, half_rows[n]], out_recv.at[n])
        for q in range(2):
            padding = jnp.zeros((8, 4, 128), f32)
            extra = blocks_exchanged(
                [
                    jnp.concatenate(
                        [waves_in[pl.ds(4 * q + j, 8, stride=8), 16 + 4 * n : 20 + 4 * n, :], padding], 1
                    )
                    for j in range(4)
                ]
            )
            for half in range(2):
                c = 2 * n + half
                main = blocks_exchanged(
                    [
                        waves_in[pl.ds(4 * q + j, 8, stride=8), ROWS_OF[c] : ROWS_OF[c] + 8, :]
                        for j in range(4)
                    ]
                )
                for i in range(4):
                    value = main[i]
                    rim = jnp.where(lane_group == sub, extra[(i + 1) % 4][:, 2 + half : 3 + half, :], 0.0)
                    if i < 3:
                        value = value + jnp.where(sub == 0, shifted(extra[i][:, half : half + 1, :], 1), 0.0)
                        corner = shifted(extra[3][:, half : half + 1, :], 1)
                        rim = rim + jnp.where((sub == 0) & (lane_group == i), corner, 0.0)
                    lines_of = slice(64 * i, 64 * i + 64)
                    plane[half, lines_of, 128 * q : 128 * q + 128] = value.reshape(64, 128)
                    high, low = split(rim.reshape(64, 128))
                    plane_rim[half, lines_of, 128 * q : 128 * q + 128] = high
                    plane_rim[half, lines_of, 256 + 128 * q : 384 + 128 * q] = low

        real, imag = [
            dots(*split(plane[half] + product(plane_rim[half], fold[0][...])), fy[0][...], fy[1][...])
            for half in range(2)
        ]
        spec = jnp.concatenate(
            [real[:, :256] + imag[:, 256:], imag[:, :256] - real[:, 256:]], 1
        )
        both = dots(fx[0][...], fx[1][...], *split(spec))
        square_z = jnp.sum(jnp.where(mine_z == n, square_y, 0.0), 1, keepdims=True)
        factor_z = jnp.sum(jnp.where(mine_z == n, factor_y, 0.0), 1, keepdims=True)
        square = square_x + square_y + square_z
        green = factor_x * factor_y * (factor_z * (4.0 * math.pi))
        green = jnp.where(square > 0.0, green / jnp.where(square > 0.0, square, 1.0), 0.0)
        spec = jnp.concatenate(
            [
                (both[:256, :256] + both[256:, 256:]) * green,
                (both[:256, 256:] - both[256:, :256]) * green,
            ],
            1,
        )
        both = dots(bx[0][...], bx[1][...], *split(spec))
        spec = jnp.concatenate(
            [both[:256, :256] - both[256:, 256:], both[:256, 256:] + both[256:, :256]], 0
        )
        both = dots(*split(spec), fy[0][...], fy[1][...])
        back = [both[:256, :256] - both[256:, 256:], both[256:, :256] + both[:256, 256:]]
        back_rim = [product(jnp.concatenate(split(value), 1), fold[1][...]) for value in back]

        for q in range(2):
            extra = [jnp.zeros((8, 8, 128), f32) for _ in range(4)]
            for half in range(2):
                c = 2 * n + half
                main, corner = [], jnp.zeros((8, 1, 128), f32)
                for i in range(4):
                    lines_of = slice(64 * i, 64 * i + 64)
                    value = back[half][lines_of, 128 * q : 128 * q + 128].reshape(8, 8, 128)
                    rim = back_rim[half][lines_of, 128 * q : 128 * q + 128].reshape(8, 8, 128)
                    main.append(value)
                    if i < 3:
                        extra[i] = jnp.where(sub == half, shifted(value[:, 0:1, :], -1), extra[i])
                        corner = jnp.where(lane_group == i, shifted(rim[:, 0:1, :], -1), corner)
                    side = jnp.sum(jnp.where(lane_group == sub, rim, 0.0), 1, keepdims=True)
                    extra[(i + 1) % 4] = jnp.where(sub == 2 + half, side, extra[(i + 1) % 4])
                extra[3] = jnp.where(sub == half, corner, extra[3])
                main = blocks_exchanged(main)
                for j in range(4):
                    waves_out[pl.ds(4 * q + j, 8, stride=8), ROWS_OF[c] : ROWS_OF[c] + 8, :] = main[j]
            extra = blocks_exchanged(extra)
            for j in range(4):
                waves_out[pl.ds(4 * q + j, 8, stride=8), 16 + 4 * n : 20 + 4 * n, :] = extra[j][:, 0:4, :]
        own(waves_out, lines_in, half_rows[n], own_sem.at[2 + n]).start()
        send_all(waves_out, lines_in, half_rows[n], back_send.at[n], back_recv.at[n])

    for n in range(2):
        own(waves_out, lines_in, half_rows[n], own_sem.at[2 + n]).wait()
        settle(lines_in.at[rest, half_rows[n]], back_recv.at[n])

    for pair in range(5):
        columns = []
        for group in (2 * pair, 2 * pair + 1):
            starts = [
                ROWS_OF[c] + group if group < 8 else RIMS_OF[c] + 2 * (group - 8) for c in range(4)
            ]
            columns.append(jnp.concatenate([lines_in[:, start, :] for start in starts], 0))
        result = dots(bz[0][...], bz[1][...], *split(jnp.concatenate(columns, 1)))
        for part in range(2):
            lines_z[2 * pair + part, 0:256, :] = result[:, 128 * part : 128 * part + 128]
            lines_z[2 * pair + part, 256:264, :] = result[0:8, 128 * part : 128 * part + 128]

    lane = lane_of(2)
    lane_group = (lane // 4) % 8
    low_half = lane < 64
    even = (lane // 32) % 2 == 0

    def regroup(part, rows):
        at = pl.ds(pl.multiple_of(part * 32, 32), rows)
        rim = lines_z[9, at, :]
        for group in range(9):
            main = lines_z[group, at, :]
            if group < 8:
                side = jnp.where(lane_group == group, rim, 0.0)
            else:
                side = jnp.where((lane_group == 2) & (lane >= 96), main, 0.0)
                side = jnp.where((lane_group == 1) & (lane >= 64) & (lane < 96), turn(main, -32), side)
                side = jnp.where((lane_group == 0) & (lane >= 32) & (lane < 64), turn(main, -64), side)
            pair_even = jnp.where(even, main, side)
            pair_odd = turn(jnp.where(even, side, main), -32)
            for odd, value in enumerate((pair_even, pair_odd)):
                other = turn(value, 64)
                high = value.astype(bf16).astype(f32)
                high_other = other.astype(bf16).astype(f32)
                planes = (
                    jnp.where(low_half, high, other - high_other),
                    jnp.where(low_half, high_other, value - high),
                )
                for second in range(2):
                    plane_x = 4 * group + 2 * second + odd
                    whole = jnp.concatenate([last[plane_x], planes[second]], 0)
                    for k in range(rows // 8):
                        window = whole[8 * k : 8 * k + 16].astype(bf16)
                        field[plane_x * 32 + 4 * part + k] = window
                    last[plane_x] = planes[second][rows - 8 : rows]

    def regroup_step(part, carry):
        regroup(part, 32)
        return carry

    last[...] = jnp.zeros_like(last)
    lax.fori_loop(0, 8, regroup_step, 0)
    regroup(8, 8)

    rows16 = lax.broadcasted_iota(jnp.int32, (16, 128), 0).astype(f32) - 1.0
    rows40 = rows_of_y()

    def one(number, slot):
        charge, at_x, at_y, at_z = [slot[i : i + 1] for i in range(4)]
        at_x = at_x - codes[1, number].astype(f32)
        at_z = at_z - codes[2, number].astype(f32)
        weight_x, slope_x = bspline(rows16 - at_x, True)
        weight_z, slope_z = bspline(rows16 - at_z, True)
        along_y = jnp.concatenate(bspline(rows40 - at_y, True), 1)
        y_high, y_low = split(with_rims(along_y))
        both = jnp.concatenate([y_high, y_high, y_low, y_low], 0)
        base = codes[0, number]
        window = jnp.concatenate([field[base + 32 * i + 1] for i in range(11)], 0)
        out = jnp.dot(jnp.concatenate([window, window], 1), both, preferred_element_type=f32)
        plain = jnp.zeros((16, 128), f32)
        along_x = jnp.zeros((16, 128), f32)
        sloped = jnp.zeros((16, 128), f32)
        for i in range(11):
            value = out[16 * i : 16 * i + 16, :128]
            slope = out[16 * i : 16 * i + 16, 128:]
            plain = plain + weight_x[i : i + 1] * value
            along_x = along_x + slope_x[i : i + 1] * value
            sloped = sloped + weight_x[i : i + 1] * slope
        minus = charge * (-1.0 / 72.0)
        return jnp.concatenate(
            [
                minus * jnp.sum(along_x * weight_z, 0, keepdims=True),
                minus * jnp.sum(sloped * weight_z, 0, keepdims=True),
                minus * jnp.sum(plain * slope_z, 0, keepdims=True),
                charge,
            ],
            0,
        )

    def source_at(n):
        return lax.rem(chunk + hop(OWN - 1 - n), OWN)

    def interpolate(step):
        sources = [source_at(4 * step + k) for k in range(4)]
        found = []
        for source in sources:
            pair = slots_ref[pl.ds(pl.multiple_of(8 * source, 8), 8), :]
            found.append(
                jnp.concatenate([one(2 * source, pair[0:4]), one(2 * source + 1, pair[4:8])], 0)
            )
        for source, value in zip(sources, found):
            force[source] = value

    def send_force(source):
        remote(
            force.at[source], force_in.at[mine], force_send, force_recv,
            (grid_bead, source // 8, source % 8),
        ).start()

    pl.semaphore_wait(blocks_sem, 3)
    springs = [
        remote(frac_ref, target, bead_send.at[i], bead_recv.at[i], (lax.rem(bead + step, 4), px, py))
        for i, (target, step) in enumerate(((before_ref, 1), (after_ref, 3)))
    ]
    for copy in springs:
        copy.start()
    def send_forces(step, count):
        for k in range(count):
            send_force(source_at(4 * step + k))

    def interpolate_step(step, carry):
        interpolate(step)
        send_forces(step - 1, 4)
        return carry

    interpolate(0)
    lax.fori_loop(1, OWN // 4, interpolate_step, 0)
    send_forces(OWN // 4 - 1, 3)

    @pl.when(same)
    def _():
        pltpu.make_async_copy(force.at[chunk], force_in.at[mine], own_sem.at[4]).start()

    @pl.when(jnp.logical_not(same))
    def _():
        send_force(chunk)

    for copy in springs:
        copy.wait()
    bends = [2.0 * frac_ref[i] - before_ref[i] - after_ref[i] for i in range(3)]

    @pl.when(same)
    def _():
        settle(force_in.at[mine], own_sem.at[4])
        settle(force_in.at[rest], force_recv)
        settle(force_in.at[rest], force_send)

    @pl.when(jnp.logical_not(same))
    def _():
        settle(force_in, force_recv)
        settle(force_in, force_send)

    for axis in range(3):
        both = jnp.concatenate([force_in[:, axis, :], force_in[:, 4 + axis, :]], 0)
        moved = sum(
            lax.dot_general(chosen, part, (((0,), (0,)), ((), ())), preferred_element_type=f32)
            for part in reversed(three(both))
        )
        out_ref[axis] = moved - spring_scale * bends[axis]

    for n in range(2):
        settle(lines.at[rest, half_rows[n]], out_send.at[n])
        settle(waves_out.at[rest, half_rows[n]], back_send.at[n])


def grid_to_forces(codes, packed, slots, frac, owner_row):
    table = tables()
    consts = [packed] + [jnp.asarray(half) for name in TABLES for half in table[name]]
    consts += [jnp.asarray(table["row"]), slots, frac, owner_row]
    dma = pltpu.SemaphoreType.DMA
    chunks = VMEM((OWN, 40, 128), f32)
    return pl.pallas_call(
        wave_kernel,
        out_shape=jax.ShapeDtypeStruct((3, OWN, 128), f32),
        in_specs=[pl.BlockSpec(memory_space=HBM)] * 18,
        out_specs=pl.BlockSpec(memory_space=VMEM),
        scratch_shapes=[VMEM(const.shape, const.dtype) for const in consts]
        + [
            chunks, chunks, chunks, chunks,
            VMEM((2, 256, 256), f32), VMEM((2, 256, 512), bf16),
            VMEM((10, 264, 128), f32), VMEM((36, 8, 128), f32), VMEM((36 * 32 + 1, 16, 128), bf16),
            VMEM((OWN, 8, 128), f32), VMEM((OWN, 8, 128), f32),
            dma((17,)), dma((2,)), dma((2,)), dma((2,)), dma((2,)), dma((5,)), dma, dma,
            pltpu.SemaphoreType.REGULAR,
            VMEM((3, OWN, 128), f32), VMEM((3, OWN, 128), f32), dma((2,)), dma((2,)),
            SMEM((8, 128), jnp.int32), dma, pltpu.SemaphoreType.REGULAR, dma,
        ],
        compiler_params=pltpu.CompilerParams(
            collective_id=1, has_side_effects=True, vmem_limit_bytes=60 << 20
        ),
        name="grid_to_forces",
    )(
        codes, *consts,
    )


def local(block_owner, block_tile, atom_cell, atom_frac, charge, zone):
    owner_row = block_owner.reshape(1, OWN)
    frac = jnp.transpose(atom_frac[0], (1, 0, 2))
    slots = atoms_to_slots(
        owner_row, block_tile.reshape(1, OWN), atom_cell, frac, charge, zone
    )
    packed, codes = spread(slots)
    total = grid_to_forces(codes, packed, slots, frac, owner_row)
    return jnp.transpose(total, (1, 0, 2))[None]


def solution(mesh):
    return jax.shard_map(
        local,
        mesh=mesh,
        in_specs=(
            P(("px", "py"), None),
            P(("px", "py")),
            P(("px", "py"), None),
            P("bead", ("px", "py"), None, None),
            P(("px", "py"), None),
            P(("px", "py"), None),
        ),
        out_specs=P("bead", ("px", "py"), None, None),
        check_vma=False,
    )
```
